32 devices in a mesh: dp: 8 (over y, x, core), head: 4 (over z).
Axes of the slice: x: 2, y: 2, z: 4, core: 2. Of those that a mesh axis runs over, the one named last changes fastest.
Arguments:
- interface: float32 [8, 1024, 512], P('dp', 'head'), may hold values from -6 to 6
- latents: float32 [8, 128, 1024], P('dp'), may hold values from -6 to 6
- segment_ids: int32 [8, 1024], P('dp'), may hold values from 0 to 3, never falling along the last dimension, each value on 1 to 512 neighbouring positions
- read_gain_lat: float32 [1024], replicated, may hold values from 0.1 to 1.9
- read_gain_int: float32 [512], P('head'), may hold values from 0.1 to 1.9
- read_query: float32 [1024, 1024], P(None, 'head'), may hold values from -0.1875 to 0.1875
- read_keyval: float32 [512, 2, 1024], P(None, None, 'head'), may hold values from -0.25 to 0.25
- read_out: float32 [1024, 1024], P('head'), may hold values from -0.75 to 0.75
- read_gain_mlp: float32 [1024], replicated, may hold values from 0.1 to 1.9
- read_up: float32 [1024, 4096], P(None, 'head'), may hold values from -0.1875 to 0.1875
- read_down: float32 [4096, 1024], P('head'), may hold values from -0.09375 to 0.09375
- layer_gain_att: float32 [1, 1024], replicated, may hold values from 0.1 to 1.9
- layer_qkv: float32 [1, 1024, 3, 1024], P(None, None, None, 'head'), may hold values from -0.1875 to 0.1875
- layer_out: float32 [1, 1024, 1024], P(None, 'head'), may hold values from -0.375 to 0.375
- layer_gain_mlp: float32 [1, 1024], replicated, may hold values from 0.1 to 1.9
- layer_up: float32 [1, 1024, 4096], P(None, None, 'head'), may hold values from -0.1875 to 0.1875
- layer_down: float32 [1, 4096, 1024], P(None, 'head'), may hold values from -0.09375 to 0.09375
- write_gain_int: float32 [512], P('head'), may hold values from 0.1 to 1.9
- write_query: float32 [512, 512], P('head'), may hold values from -0.25 to 0.25
- write_gain_lat: float32 [1024], replicated, may hold values from 0.1 to 1.9
- write_keyval: float32 [1024, 2, 512], P(None, None, 'head'), may hold values from -0.1875 to 0.1875
- write_out: float32 [512, 512], P('head'), may hold values from -0.5 to 0.5
- write_gain_mlp: float32 [512], P('head'), may hold values from 0.1 to 1.9
- write_up: float32 [512, 2048], P('head'), may hold values from -0.25 to 0.25
- write_down: float32 [2048, 512], P('head'), may hold values from -0.125 to 0.125
- interface_cot: float32 [8, 1024, 512], P('dp', 'head'), may hold values from -6 to 6
- latents_cot: float32 [8, 128, 1024], P('dp'), may hold values from -6 to 6
Outputs:
- interface_new: float32 [8, 1024, 512], P('dp', 'head')
- latents_new: float32 [8, 128, 1024], P('dp')
- interface_grad: float32 [8, 1024, 512], P('dp', 'head')
- latents_grad: float32 [8, 128, 1024], P('dp')
- grad_read_gain_lat: float32 [1024], replicated
- grad_read_gain_int: float32 [512], P('head')
- grad_read_query: float32 [1024, 1024], P(None, 'head')
- grad_read_keyval: float32 [512, 2, 1024], P(None, None, 'head')
- grad_read_out: float32 [1024, 1024], P('head')
- grad_read_gain_mlp: float32 [1024], replicated
- grad_read_up: float32 [1024, 4096], P(None, 'head')
- grad_read_down: float32 [4096, 1024], P('head')
- grad_layer_gain_att: float32 [1, 1024], replicated
- grad_layer_qkv: float32 [1, 1024, 3, 1024], P(None, None, None, 'head')
- grad_layer_out: float32 [1, 1024, 1024], P(None, 'head')
- grad_layer_gain_mlp: float32 [1, 1024], replicated
- grad_layer_up: float32 [1, 1024, 4096], P(None, None, 'head')
- grad_layer_down: float32 [1, 4096, 1024], P(None, 'head')
- grad_write_gain_int: float32 [512], P('head')
- grad_write_query: float32 [512, 512], P('head')
- grad_write_gain_lat: float32 [1024], replicated
- grad_write_keyval: float32 [1024, 2, 512], P(None, None, 'head')
- grad_write_out: float32 [512, 512], P('head')
- grad_write_gain_mlp: float32 [512], P('head')
- grad_write_up: float32 [512, 2048], P('head')
- grad_write_down: float32 [2048, 512], P('head')
The draws below stay inside these ranges and needn't reach their ends.
Inputs may be any that keep to these rules, and one draw needn't show every extreme that they name: `segment_ids`: along each sequence the crop numbers never fall; every crop holds 1 to 512 patches, and some crop of each sequence holds exactly 512.
All inputs are finite; a program needn't handle non-finite values.
Results may differ from the reference program's by a relative error of at most 0.0003.
Values sent between devices are 32-bit elements; how exact they have to be, the bound alone decides.
No kernel may reach another device: no remote copies, remote signals or barrier semaphores. Data moves between devices by JAX's collectives and lax.ppermute only.
A program may use at most 256 MiB of HBM per device.

```python
import math
import jax
import jax.numpy as jnp
import numpy as np
from jax import lax

DL = 1024
DI = 512
HEADS = 16
NL = 128
NI = 1024
CROPS = 4
LAYERS = 1
FFL = 4096
FFI = 2048
SEQS = 8


def level_of(rng, shape, pieces, low, largest):
    def one(dim, blocks):
        heights = jax.random.uniform(jax.random.fold_in(jax.random.fold_in(rng, 6), dim), (blocks,), jnp.float32, low / len(pieces), largest / len(pieces))
        return jnp.repeat(jnp.exp(heights), shape[dim] // blocks).reshape((-1,) + (1,) * (len(shape) - dim - 1))

    level = one(*pieces[0])
    for cut in pieces[1:]:
        level = level * one(*cut)
    return level


def profile(amount, total, bound, skew):
    weights = [(1 << 20) // math.isqrt(standing ** skew) + 1 for standing in range(2, amount + 1)]
    spare, holding = total - bound - (amount - 1), [1] * (amount - 1)
    while spare > 0:
        free = [i for i in range(amount - 1) if holding[i] < bound]
        whole, remaining = sum([weights[i] for i in free]), spare
        for i in free:
            more = min(bound - holding[i], max(1, remaining * weights[i] // whole), spare)
            holding[i] = holding[i] + more
            spare = spare - more
    return np.array([bound] + holding)


def ragged(own_key, count, total, limit, skew):
    if count == 2:
        one = jax.random.randint(own_key, (), max(1, total - limit), min(limit, total - 1) + 1)
        return jnp.stack([one, total - one])
    sizes = jnp.asarray(profile(count, total, limit, skew), jnp.int32)
    pairs = (count - 1) // 2
    donor, taker = sizes[1:1 + 2 * pairs:2], sizes[2:2 + 2 * pairs:2]
    margin = jnp.minimum(donor - 1, limit - taker)
    passed = jax.random.randint(jax.random.fold_in(own_key, 1), (pairs,), 0, 1 << 20) % (margin + 1)
    sizes = sizes.at[1:1 + 2 * pairs:2].set(donor - passed).at[2:2 + 2 * pairs:2].set(taker + passed)
    return sizes[jax.random.permutation(jax.random.fold_in(own_key, 2), count)]


def bell_draw(rng, extent, scale, reach, cuts=(), kind=jnp.bfloat16):
    values = scale * jax.random.normal(rng, extent, jnp.float32)
    if cuts:
        values = values * level_of(rng, extent, cuts, -0.22, 0.18)
    return jnp.clip(values, -reach, reach).astype(kind)


def setup_inputs(seed: int = 0) -> dict:
    seeds = jax.random.split(jax.random.key(seed), 28)
    interface = bell_draw(seeds[0], (SEQS, NI, DI), 1.0, 6.0, ((0, 8), (1, 4)), jnp.float32)
    latents = bell_draw(seeds[1], (SEQS, NL, DL), 1.0, 6.0, ((0, 8),), jnp.float32)
    segment_ids = jax.vmap(lambda own: jnp.searchsorted(jnp.cumsum(ragged(own, CROPS, NI, NI // 2, 2)), jnp.arange(NI), side="right"))(jax.random.split(seeds[2], SEQS)).reshape((SEQS, NI)).astype(jnp.int32)
    read_gain_lat = jnp.clip(1.0 + 0.18 * jax.random.normal(seeds[3], (DL,), jnp.float32), 0.1, 1.9)
    read_gain_int = jnp.clip(1.0 + 0.18 * jax.random.normal(seeds[4], (DI,), jnp.float32), 0.1, 1.9)
    read_query = bell_draw(seeds[5], (DL, DL), DL ** -0.5, 0.1875, ((1, 4),), jnp.float32)
    read_keyval = bell_draw(seeds[6], (DI, 2, DL), DI ** -0.5, 0.25, ((2, 4),), jnp.float32)
    read_out = bell_draw(seeds[7], (DL, DL), (DL // 16) ** -0.5, 0.75, ((0, 4),), jnp.float32)
    read_gain_mlp = jnp.clip(1.0 + 0.18 * jax.random.normal(seeds[8], (DL,), jnp.float32), 0.1, 1.9)
    read_up = bell_draw(seeds[9], (DL, FFL), DL ** -0.5, 0.1875, ((1, 4),), jnp.float32)
    read_down = bell_draw(seeds[10], (FFL, DL), FFL ** -0.5, 0.09375, ((0, 4),), jnp.float32)
    layer_gain_att = jnp.clip(1.0 + 0.18 * jax.random.normal(seeds[11], (LAYERS, DL), jnp.float32), 0.1, 1.9)
    layer_qkv = bell_draw(seeds[12], (LAYERS, DL, 3, DL), DL ** -0.5, 0.1875, ((3, 4),), jnp.float32)
    layer_out = bell_draw(seeds[13], (LAYERS, DL, DL), (DL // 4) ** -0.5, 0.375, ((1, 4),), jnp.float32)
    layer_gain_mlp = jnp.clip(1.0 + 0.18 * jax.random.normal(seeds[14], (LAYERS, DL), jnp.float32), 0.1, 1.9)
    layer_up = bell_draw(seeds[15], (LAYERS, DL, FFL), DL ** -0.5, 0.1875, ((2, 4),), jnp.float32)
    layer_down = bell_draw(seeds[16], (LAYERS, FFL, DL), FFL ** -0.5, 0.09375, ((1, 4),), jnp.float32)
    write_gain_int = jnp.clip(1.0 + 0.18 * jax.random.normal(seeds[17], (DI,), jnp.float32), 0.1, 1.9)
    write_query = bell_draw(seeds[18], (DI, DI), DI ** -0.5, 0.25, ((0, 4),), jnp.float32)
    write_gain_lat = jnp.clip(1.0 + 0.18 * jax.random.normal(seeds[19], (DL,), jnp.float32), 0.1, 1.9)
    write_keyval = bell_draw(seeds[20], (DL, 2, DI), DL ** -0.5, 0.1875, ((2, 4),), jnp.float32)
    write_out = bell_draw(seeds[21], (DI, DI), (DI // 4) ** -0.5, 0.5, ((0, 4),), jnp.float32)
    write_gain_mlp = jnp.clip(1.0 + 0.18 * jax.random.normal(seeds[22], (DI,), jnp.float32), 0.1, 1.9)
    write_up = bell_draw(seeds[23], (DI, FFI), DI ** -0.5, 0.25, ((0, 4),), jnp.float32)
    write_down = bell_draw(seeds[24], (FFI, DI), FFI ** -0.5, 0.125, ((0, 4),), jnp.float32)
    interface_cot = bell_draw(seeds[25], (SEQS, NI, DI), 1.0, 6.0, ((0, 8), (1, 4)), jnp.float32)
    latents_cot = bell_draw(seeds[26], (SEQS, NL, DL), 1.0, 6.0, ((0, 8),), jnp.float32)
    return dict(interface=interface, latents=latents, segment_ids=segment_ids, read_gain_lat=read_gain_lat, read_gain_int=read_gain_int, read_query=read_query, read_keyval=read_keyval, read_out=read_out, read_gain_mlp=read_gain_mlp, read_up=read_up, read_down=read_down, layer_gain_att=layer_gain_att, layer_qkv=layer_qkv, layer_out=layer_out, layer_gain_mlp=layer_gain_mlp, layer_up=layer_up, layer_down=layer_down, write_gain_int=write_gain_int, write_query=write_query, write_gain_lat=write_gain_lat, write_keyval=write_keyval, write_out=write_out, write_gain_mlp=write_gain_mlp, write_up=write_up, write_down=write_down, interface_cot=interface_cot, latents_cot=latents_cot)


PRECISE = lax.Precision.HIGHEST
EPSILON = 1e-05

def layer_norm(values, scaling):
    average = lax.optimization_barrier(jnp.mean(values, axis=-1, keepdims=True))
    centred = values - average
    spread = lax.optimization_barrier(jnp.mean(centred * centred, axis=-1, keepdims=True))
    return centred * lax.rsqrt(spread + EPSILON) * scaling

def product(former, latter):
    return jnp.matmul(former, latter, precision=PRECISE)

def feed_forward(normed, upward, downward):
    return product(jax.nn.gelu(product(normed, upward), approximate=False), downward)

def split_heads(values, head_count):
    return values.reshape(values.shape[:-1] + (head_count, values.shape[-1] // head_count))

def attend(queries, key_rows, value_rows, allowed, head_count):
    query_heads = split_heads(queries, head_count)
    key_heads = split_heads(key_rows, head_count)
    value_heads = split_heads(value_rows, head_count)
    factor = query_heads.shape[-1] ** (-0.5)
    scores = jnp.einsum('sqhd,skhd->shqk', query_heads, key_heads, precision=PRECISE) * factor
    scores = jnp.where(allowed[:, None], scores, -1e+30)
    weights = jax.nn.softmax(scores, axis=-1)
    blended = jnp.einsum('shqk,skhd->sqhd', weights, value_heads, precision=PRECISE)
    return blended.reshape(blended.shape[:-2] + (-1,))

def build_masks(segment_ids):
    latent_crop = jnp.arange(NL, dtype=jnp.int32) // (NL // CROPS)
    read_mask = latent_crop[None, :, None] == segment_ids[:, None, :]
    self_mask = jnp.broadcast_to(latent_crop[:, None] == latent_crop[None, :], (segment_ids.shape[0], NL, NL))
    write_mask = segment_ids[:, :, None] == latent_crop[None, None, :]
    return (read_mask, self_mask, write_mask)

def forward(params, interface, latents, segment_ids):
    read_gain_lat, read_gain_int, read_query, read_keyval, read_out, read_gain_mlp, read_up, read_down, layer_gain_att, layer_qkv, layer_out, layer_gain_mlp, layer_up, layer_down, write_gain_int, write_query, write_gain_lat, write_keyval, write_out, write_gain_mlp, write_up, write_down = params
    read_mask, self_mask, write_mask = build_masks(segment_ids)
    lat_normed = layer_norm(latents, read_gain_lat)
    int_normed = layer_norm(interface, read_gain_int)
    keyval = jnp.einsum('sni,icd->sncd', int_normed, read_keyval, precision=PRECISE)
    attended = attend(product(lat_normed, read_query), keyval[:, :, 0], keyval[:, :, 1], read_mask, HEADS)
    carried = latents + product(attended, read_out)
    carried = carried + feed_forward(layer_norm(carried, read_gain_mlp), read_up, read_down)
    for layer_no in range(LAYERS):
        normed = layer_norm(carried, layer_gain_att[layer_no])
        packed = jnp.einsum('snd,dce->snce', normed, layer_qkv[layer_no], precision=PRECISE)
        attended = attend(packed[:, :, 0], packed[:, :, 1], packed[:, :, 2], self_mask, HEADS)
        carried = carried + product(attended, layer_out[layer_no])
        carried = carried + feed_forward(layer_norm(carried, layer_gain_mlp[layer_no]), layer_up[layer_no], layer_down[layer_no])
    lat_normed = layer_norm(carried, write_gain_lat)
    keyval = jnp.einsum('sni,icd->sncd', lat_normed, write_keyval, precision=PRECISE)
    queries = product(layer_norm(interface, write_gain_int), write_query)
    attended = attend(queries, keyval[:, :, 0], keyval[:, :, 1], write_mask, HEADS)
    result = interface + product(attended, write_out)
    result = result + feed_forward(layer_norm(result, write_gain_mlp), write_up, write_down)
    return (result, carried)

def reference(interface, latents, segment_ids, read_gain_lat, read_gain_int, read_query, read_keyval, read_out, read_gain_mlp, read_up, read_down, layer_gain_att, layer_qkv, layer_out, layer_gain_mlp, layer_up, layer_down, write_gain_int, write_query, write_gain_lat, write_keyval, write_out, write_gain_mlp, write_up, write_down, interface_cot, latents_cot):
    params = (read_gain_lat, read_gain_int, read_query, read_keyval, read_out, read_gain_mlp, read_up, read_down, layer_gain_att, layer_qkv, layer_out, layer_gain_mlp, layer_up, layer_down, write_gain_int, write_query, write_gain_lat, write_keyval, write_out, write_gain_mlp, write_up, write_down)
    group_size = math.gcd(SEQS, 4)
    batches = SEQS // group_size

    def regroup(tensor):
        return tensor.reshape((batches, group_size) + tensor.shape[1:])

    def flatten(tensor):
        return tensor.reshape((SEQS,) + tensor.shape[2:])

    def one_group(totals, inputs):
        inter_part, latent_part, segment_part, inter_cot, latent_cot = inputs

        def local_forward(weights_all, inter_in, latent_in):
            return forward(weights_all, inter_in, latent_in, segment_part)
        outputs, pullback = jax.vjp(local_forward, params, inter_part, latent_part)
        grads_weights, grad_inter, grad_latent = pullback((inter_cot, latent_cot))
        totals = jax.tree.map(lambda running, addend: running + addend, totals, grads_weights)
        return (totals, (outputs[0], outputs[1], grad_inter, grad_latent))
    initial = jax.tree.map(jnp.zeros_like, params)
    totals, stacked = lax.scan(one_group, initial, (regroup(interface), regroup(latents), regroup(segment_ids), regroup(interface_cot), regroup(latents_cot)))
    return (flatten(stacked[0]), flatten(stacked[1]), flatten(stacked[2]), flatten(stacked[3]), totals[0], totals[1], totals[2], totals[3], totals[4], totals[5], totals[6], totals[7], totals[8], totals[9], totals[10], totals[11], totals[12], totals[13], totals[14], totals[15], totals[16], totals[17], totals[18], totals[19], totals[20], totals[21])
```

```python
import jax
import jax.numpy as jnp
from jax import lax
from jax.sharding import PartitionSpec as P

HEADS = 16
CROPS = 4
EPSILON = 1e-05
PRECISE = lax.Precision.HIGH
ROOT_HALF = 0.7071067811865476
DENSITY = 0.3989422804014327


def mm(left, right):
    return lax.dot_general(left, right, (((1,), (0,)), ((), ())), precision=PRECISE)


def mmt(left, right):
    return lax.dot_general(left, right, (((1,), (1,)), ((), ())), precision=PRECISE)


def tmm(left, right):
    return lax.dot_general(left, right, (((0,), (0,)), ((), ())), precision=PRECISE)


def normalise(values):
    centred = values - jnp.mean(values, axis=-1, keepdims=True)
    root = lax.rsqrt(jnp.mean(centred * centred, axis=-1, keepdims=True) + EPSILON)
    return centred * root, root


def norm_back(grad, xhat, root, gain):
    scaled = grad * gain
    return root * (
        scaled
        - jnp.mean(scaled, axis=-1, keepdims=True)
        - xhat * jnp.mean(scaled * xhat, axis=-1, keepdims=True)
    )


def cdf(values):
    return 0.5 * (1.0 + lax.erf(values * ROOT_HALF))


def gelu_slope(values):
    return cdf(values) + values * DENSITY * jnp.exp(-0.5 * values * values)


def heads_of(values, count):
    return values.reshape(values.shape[0], count, values.shape[1] // count)


def attend(queries, keys, values, mask, count):
    q, k, v = heads_of(queries, count), heads_of(keys, count), heads_of(values, count)
    scores = jnp.einsum("qhd,khd->hqk", q, k, precision=PRECISE) * (q.shape[-1] ** -0.5)
    scores = jnp.where(mask[None], scores, -1e30)
    top = jnp.max(scores, axis=-1, keepdims=True)
    weights = jnp.exp(scores - top)
    weights = weights / jnp.sum(weights, axis=-1, keepdims=True)
    out = jnp.einsum("hqk,khd->qhd", weights, v, precision=PRECISE)
    return out.reshape(queries.shape), weights


def attend_back(grad, queries, keys, values, weights, count):
    q, k, v = heads_of(queries, count), heads_of(keys, count), heads_of(values, count)
    g = heads_of(grad, count)
    factor = q.shape[-1] ** -0.5
    dv = jnp.einsum("hqk,qhd->khd", weights, g, precision=PRECISE)
    dp = jnp.einsum("qhd,khd->hqk", g, v, precision=PRECISE)
    ds = weights * (dp - jnp.sum(dp * weights, axis=-1, keepdims=True)) * factor
    dq = jnp.einsum("hqk,khd->qhd", ds, k, precision=PRECISE)
    dk = jnp.einsum("hqk,qhd->khd", ds, q, precision=PRECISE)
    return dq.reshape(queries.shape), dk.reshape(keys.shape), dv.reshape(values.shape)


def local(
    interface,
    latents,
    segment_ids,
    read_gain_lat,
    read_gain_int,
    read_query,
    read_keyval,
    read_out,
    read_gain_mlp,
    read_up,
    read_down,
    layer_gain_att,
    layer_qkv,
    layer_out,
    layer_gain_mlp,
    layer_up,
    layer_down,
    write_gain_int,
    write_query,
    write_gain_lat,
    write_keyval,
    write_out,
    write_gain_mlp,
    write_up,
    write_down,
    interface_cot,
    latents_cot,
):
    zs, ds = lax.axis_size("head"), lax.axis_size("dp")
    me, dd = lax.axis_index("head"), lax.axis_index("dp")
    here = HEADS // zs

    def shift(values, step):
        return lax.ppermute(values, "head", [(i, (i + step) % zs) for i in range(zs)])

    def z_scatter(parts):
        total = lax.dynamic_index_in_dim(parts, me, 0, keepdims=False)
        for step in range(1, zs):
            sent = lax.dynamic_index_in_dim(parts, (me + step) % zs, 0, keepdims=False)
            total = total + shift(sent, step)
        return total

    def z_gather(own):
        out = jnp.zeros((zs,) + own.shape, own.dtype)
        out = lax.dynamic_update_index_in_dim(out, own, me, 0)
        for step in range(1, zs):
            out = lax.dynamic_update_index_in_dim(out, shift(own, step), (me - step) % zs, 0)
        return out

    def add_sum(base, partial):
        rows = base.shape[0] // zs
        own = z_scatter(partial.reshape(zs, rows, -1))
        own = own + lax.dynamic_slice_in_dim(base, me * rows, rows, 0)
        return z_gather(own).reshape(base.shape)

    def head_sum(partial):
        rows = partial.shape[0] // zs
        own = z_scatter(partial.reshape(zs, rows, -1))
        return z_gather(own).reshape(partial.shape)

    def d_gather(parts):
        joined = jnp.concatenate(parts, axis=1) if len(parts) > 1 else parts[0]
        full = lax.all_gather(joined, "dp", axis=0, tiled=True)
        out, at = [], 0
        for part in parts:
            out.append(full[:, at : at + part.shape[1]])
            at += part.shape[1]
        return out

    interface, latents, segments = interface[0], latents[0], segment_ids[0]
    interface_cot, latents_cot = interface_cot[0], latents_cot[0]
    layer_gain_att, layer_gain_mlp = layer_gain_att[0], layer_gain_mlp[0]
    layer_out, layer_up, layer_down = layer_out[0], layer_up[0], layer_down[0]
    patches, wide = interface.shape
    count, deep = latents.shape
    qkv = layer_qkv[0].reshape(deep, -1)
    keyval = read_keyval.reshape(wide, -1)
    part = deep // zs
    hidden = write_down.shape[0] * zs

    crop = jnp.arange(count, dtype=jnp.int32) // (count // CROPS)
    own_segments = lax.dynamic_slice_in_dim(segments, me * patches, patches, 0)
    read_mask = crop[:, None] == segments[None, :]
    self_mask = crop[:, None] == crop[None, :]
    write_mask = own_segments[:, None] == crop[None, :]

    int_hat, int_root = normalise(interface)
    int_all = z_gather(int_hat).reshape(zs * patches, wide)
    gains = jnp.stack([read_gain_int, write_gain_int, write_gain_mlp])
    gains = jnp.transpose(z_gather(gains), (1, 0, 2)).reshape(3, wide)
    gain_read, gain_write, gain_mlp = gains[0], gains[1], gains[2]

    wq_rows, up_cols, kv_rows = wide // zs // ds, hidden // ds, deep // ds
    up_share = write_up.reshape(wide // zs, zs, ds, hidden // zs // ds)
    up_share = lax.dynamic_index_in_dim(up_share, dd, 2, keepdims=False).reshape(wide // zs, up_cols)
    down_share = lax.dynamic_index_in_dim(write_down.reshape(ds, -1, wide), dd, 0, keepdims=False)
    kv_share = lax.dynamic_slice_in_dim(write_keyval, dd * kv_rows, kv_rows, 0).reshape(kv_rows, -1)
    q_share = lax.dynamic_slice_in_dim(write_query, dd * wq_rows, wq_rows, 0)
    o_share = lax.dynamic_slice_in_dim(write_out, dd * wq_rows, wq_rows, 0)

    def d_z_gather(share):
        return lax.all_gather(z_gather(share), "dp", axis=0, tiled=False)

    shares = [up_share, down_share, kv_share, q_share, o_share]
    flat = jnp.concatenate([s.reshape(-1, 128) for s in shares], axis=0)
    int_all, flat = lax.optimization_barrier((int_all, flat))
    everything = d_z_gather(flat)
    pieces, at = [], 0
    for s in shares:
        n = s.size // 128
        pieces.append(everything[:, :, at : at + n].reshape((ds, zs) + s.shape))
        at += n
    full_up = jnp.transpose(pieces[0], (1, 2, 0, 3)).reshape(wide, hidden)
    full_down = pieces[1].reshape(hidden, wide)
    full_kv = jnp.transpose(pieces[2].reshape(ds, zs, kv_rows, 2, -1), (0, 2, 3, 1, 4)).reshape(deep, 2 * wide)
    full_query = jnp.transpose(pieces[3], (1, 0, 2, 3)).reshape(wide, wide)
    full_out = jnp.transpose(pieces[4], (1, 0, 2, 3)).reshape(wide, wide)

    lat_hat, lat_root = normalise(latents)
    lat_normed = lat_hat * read_gain_lat
    query = mm(lat_normed, read_query)
    int_normed = int_all * gain_read
    read_kv = mm(int_normed, keyval)
    read_k, read_v = read_kv[:, :part], read_kv[:, part:]
    read_attended, read_weights = attend(query, read_k, read_v, read_mask, here)
    state1 = add_sum(latents, mm(read_attended, read_out))
    hat1, root1 = normalise(state1)
    normed1 = hat1 * read_gain_mlp
    pre1 = mm(normed1, read_up)
    act1 = pre1 * cdf(pre1)
    state2 = add_sum(state1, mm(act1, read_down))
    lat_all, read_att_all, normed1_all, act1_all = d_gather([lat_normed, read_attended, normed1, act1])

    hat2, root2 = normalise(state2)
    normed2 = hat2 * layer_gain_att
    packed = mm(normed2, qkv)
    q2, k2, v2 = packed[:, :part], packed[:, part : 2 * part], packed[:, 2 * part :]
    self_attended, self_weights = attend(q2, k2, v2, self_mask, here)
    state3 = add_sum(state2, mm(self_attended, layer_out))
    hat3, root3 = normalise(state3)
    normed3 = hat3 * layer_gain_mlp
    pre3 = mm(normed3, layer_up)
    act3 = pre3 * cdf(pre3)
    state4 = add_sum(state3, mm(act3, layer_down))
    hat4, root4 = normalise(state4)
    normed4 = hat4 * write_gain_lat
    normed2_all, self_att_all, normed3_all, act3_all, normed4_all = d_gather(
        [normed2, self_attended, normed3, act3, normed4]
    )

    kv4 = mm(normed4, full_kv)
    write_k, write_v = kv4[:, :wide], kv4[:, wide:]
    write_normed = int_hat * gain_write
    write_q = mm(write_normed, full_query)
    write_attended, write_weights = attend(write_q, write_k, write_v, write_mask, HEADS)
    after = interface + mm(write_attended, full_out)
    after_hat, after_root = normalise(after)
    after_normed = after_hat * gain_mlp
    pre5 = mm(after_normed, full_up)
    act5 = pre5 * cdf(pre5)
    interface_new = after + mm(act5, full_down)

    dpre5 = mmt(interface_cot, full_down) * gelu_slope(pre5)
    dafter_normed = mmt(dpre5, full_up)
    dafter = interface_cot + norm_back(dafter_normed, after_hat, after_root, gain_mlp)
    dattended = mmt(dafter, full_out)
    dwrite_q, dwrite_k, dwrite_v = attend_back(
        dattended, write_q, write_k, write_v, write_weights, HEADS
    )
    dkv4 = jnp.concatenate([dwrite_k, dwrite_v], axis=1)
    dnormed4 = mmt(dkv4, full_kv)
    dsum4 = head_sum(dnormed4)
    dstate4 = latents_cot + norm_back(dsum4, hat4, root4, write_gain_lat)

    dup = tmm(after_normed, dpre5).reshape(zs, wide // zs, ds, -1)
    dup = jnp.transpose(dup, (2, 0, 1, 3)).reshape(ds, zs, -1, 128)
    ddown = tmm(act5, interface_cot).reshape(ds, zs, -1, 128)
    dquery = jnp.transpose(tmm(write_normed, dwrite_q).reshape(zs, ds, wq_rows, wide), (1, 0, 2, 3))
    dquery = dquery.reshape(ds, zs, -1, 128)
    dout = jnp.transpose(tmm(write_attended, dafter).reshape(zs, ds, wq_rows, wide), (1, 0, 2, 3))
    dout = dout.reshape(ds, zs, -1, 128)
    packed_grads = jnp.concatenate([dup, ddown, dquery, dout], axis=2)
    grads_mine = lax.psum_scatter(packed_grads, "dp", scatter_dimension=0, tiled=False)
    grads_mine = z_scatter(grads_mine)
    grads_all = lax.all_gather(grads_mine, "dp", axis=0, tiled=False)
    sizes = [dup.shape[2], ddown.shape[2], dquery.shape[2], dout.shape[2]]
    cut, at = [], 0
    for n in sizes:
        cut.append(grads_all[:, at : at + n])
        at += n
    grad_write_up = jnp.transpose(cut[0].reshape(ds, wide // zs, zs, -1), (1, 2, 0, 3)).reshape(write_up.shape)
    down_mine = cut[1].reshape(write_down.shape)
    grad_write_query = cut[2].reshape(write_query.shape)
    grad_write_out = cut[3].reshape(write_out.shape)

    dwrite_normed = mmt(dwrite_q, full_query)
    dint = dafter + norm_back(dwrite_normed, int_hat, int_root, gain_write)

    dkv_parts = jnp.transpose(dkv4.reshape(count, 2, zs, -1), (2, 0, 1, 3)).reshape(zs, count, -1)
    dkv_mine = z_scatter(dkv_parts)
    dpre3 = mmt(dstate4, layer_down) * gelu_slope(pre3)
    dnormed3 = head_sum(mmt(dpre3, layer_up))
    dkv_all, dstate4_all, dpre3_all = d_gather([dkv_mine, dstate4, dpre3])
    dstate3 = dstate4 + norm_back(dnormed3, hat3, root3, layer_gain_mlp)
    dself = mmt(dstate3, layer_out)
    dq2, dk2, dv2 = attend_back(dself, q2, k2, v2, self_weights, here)
    dpacked = jnp.concatenate([dq2, dk2, dv2], axis=1)
    dnormed2 = head_sum(mmt(dpacked, qkv))
    dstate3_all, dpacked_all = d_gather([dstate3, dpacked])
    dstate2 = dstate3 + norm_back(dnormed2, hat2, root2, layer_gain_att)

    dpre1 = mmt(dstate2, read_down) * gelu_slope(pre1)
    dnormed1 = head_sum(mmt(dpre1, read_up))
    dstate2_all, dpre1_all = d_gather([dstate2, dpre1])
    dstate1 = dstate2 + norm_back(dnormed1, hat1, root1, read_gain_mlp)
    dread = mmt(dstate1, read_out)
    dquery0, dread_k, dread_v = attend_back(dread, query, read_k, read_v, read_weights, here)
    dread_kv = jnp.concatenate([dread_k, dread_v], axis=1)
    dstate1_all, dquery0_all = d_gather([dstate1, dquery0])
    dlat_part = mmt(dquery0, read_query)
    dlat = head_sum(dlat_part)
    latents_grad = dstate1 + norm_back(dlat, lat_hat, lat_root, read_gain_lat)
    dint_part = mmt(dread_kv, keyval)
    dint_normed = z_scatter(dint_part.reshape(zs, patches, wide))
    interface_grad = dint + norm_back(dint_normed, int_hat, int_root, gain_read)
    grad_read_keyval = lax.psum(tmm(int_normed, dread_kv), "dp")

    def own_rows(values):
        rows = values.shape[0] // zs
        return lax.dynamic_slice_in_dim(values, me * rows, rows, 0)

    def gain_part(grad, hat):
        return jnp.sum(own_rows(grad) * own_rows(hat), axis=0)

    small = jnp.concatenate(
        [
            jnp.sum(dlat_part * lat_hat, axis=0),
            gain_part(dnormed1, hat1),
            gain_part(dnormed2, hat2),
            gain_part(dnormed3, hat3),
            gain_part(dsum4, hat4),
            jnp.sum(dint_normed * int_hat, axis=0),
            jnp.sum(dwrite_normed * int_hat, axis=0),
            jnp.sum(dafter_normed * after_hat, axis=0),
        ]
    )
    small = lax.psum(small, ("dp", "head"))
    lat_gains = small[: 5 * deep].reshape(5, deep)
    int_gains = small[5 * deep :].reshape(3, zs, wide // zs)
    int_gains = lax.dynamic_index_in_dim(int_gains, me, 1, keepdims=False)

    return (
        interface_new[None],
        state4[None],
        interface_grad[None],
        latents_grad[None],
        lat_gains[0],
        int_gains[0],
        tmm(lat_all, dquery0_all),
        grad_read_keyval.reshape(read_keyval.shape),
        tmm(read_att_all, dstate1_all),
        lat_gains[1],
        tmm(normed1_all, dpre1_all),
        tmm(act1_all, dstate2_all),
        lat_gains[2][None],
        tmm(normed2_all, dpacked_all).reshape(layer_qkv.shape),
        tmm(self_att_all, dstate3_all)[None],
        lat_gains[3][None],
        tmm(normed3_all, dpre3_all)[None],
        tmm(act3_all, dstate4_all)[None],
        int_gains[1],
        grad_write_query,
        lat_gains[4],
        tmm(normed4_all, dkv_all).reshape(write_keyval.shape),
        grad_write_out,
        int_gains[2],
        grad_write_up,
        down_mine,
    )


def solution(mesh):
    rows, both = P("dp", "head", None), P("dp", None, None)
    weights = (
        P(),
        P("head"),
        P(None, "head"),
        P(None, None, "head"),
        P("head", None),
        P(),
        P(None, "head"),
        P("head", None),
        P(),
        P(None, None, None, "head"),
        P(None, "head", None),
        P(),
        P(None, None, "head"),
        P(None, "head", None),
        P("head"),
        P("head", None),
        P(),
        P(None, None, "head"),
        P("head", None),
        P("head"),
        P("head", None),
        P("head", None),
    )
    in_specs = (rows, both, P("dp", None)) + weights + (rows, both)
    out_specs = (rows, both, rows, both) + weights
    return jax.shard_map(local, mesh=mesh, in_specs=in_specs, out_specs=out_specs, check_vma=False)
```

```python
import functools

import jax
import jax.numpy as jnp
from jax import lax
from jax.experimental import pallas as pl
from jax.experimental.pallas import tpu as pltpu
from jax.sharding import PartitionSpec as P

HEADS = 16
CROPS = 4
EPSILON = 1e-05
PRECISE = lax.Precision.HIGH
ROOT_HALF = 0.7071067811865476
DENSITY = 0.3989422804014327
VMEM_LIMIT = 56 * 1024 * 1024


def mm(left, right):
    return lax.dot_general(left, right, (((1,), (0,)), ((), ())), precision=PRECISE)


def mmt(left, right):
    return lax.dot_general(left, right, (((1,), (1,)), ((), ())), precision=PRECISE)


def tmm(left, right):
    return lax.dot_general(left, right, (((0,), (0,)), ((), ())), precision=PRECISE)


def normalise(values):
    centred = values - jnp.mean(values, axis=-1, keepdims=True)
    root = lax.rsqrt(jnp.mean(centred * centred, axis=-1, keepdims=True) + EPSILON)
    return centred * root, root


def norm_back(grad, xhat, root, gain):
    scaled = grad * gain
    return root * (
        scaled
        - jnp.mean(scaled, axis=-1, keepdims=True)
        - xhat * jnp.mean(scaled * xhat, axis=-1, keepdims=True)
    )


def cdf(values):
    return 0.5 * (1.0 + lax.erf(values * ROOT_HALF))


def gelu_slope(values):
    return cdf(values) + values * DENSITY * jnp.exp(-0.5 * values * values)


def shape_of(*dims):
    return jax.ShapeDtypeStruct(dims, jnp.float32)


def run_whole(kernel, outs, args, flops=1e9, scratch=(), anywhere=0):
    moved = sum(a.size * 4 for a in args) + sum(int(functools.reduce(lambda x, y: x * y, o.shape)) * 4 for o in outs)
    fast = len(args) - anywhere
    return pl.pallas_call(
        kernel,
        out_shape=outs,
        in_specs=[pl.BlockSpec(memory_space=pltpu.VMEM)] * fast + [pl.BlockSpec(memory_space=pl.ANY)] * anywhere,
        out_specs=[pl.BlockSpec(memory_space=pltpu.VMEM)] * len(outs),
        scratch_shapes=list(scratch),
        compiler_params=pltpu.CompilerParams(vmem_limit_bytes=VMEM_LIMIT),
        cost_estimate=pl.CostEstimate(flops=int(flops * 3), bytes_accessed=int(moved), transcendentals=0),
    )(*args)


def lane_mask(lanes, width, head):
    return lax.broadcasted_iota(jnp.int32, (1, lanes), 1) // width == head


def spread(values, width):
    lanes = values.shape[1]
    return jnp.concatenate(
        [jnp.where(lane_mask(lanes, width, h), values, 0.0) for h in range(lanes // width)], axis=0
    )


def fold(values, width):
    lanes = values.shape[1]
    rows = values.shape[0] // (lanes // width)
    total = jnp.zeros((rows, lanes), jnp.float32)
    for h in range(lanes // width):
        total = total + jnp.where(lane_mask(lanes, width, h), values[h * rows : (h + 1) * rows], 0.0)
    return total


def attend_group(q, k, v, mask, width):
    count = q.shape[1] // width
    scores = mmt(spread(q, width), k) * (width ** -0.5)
    scores = scores.reshape(count, q.shape[0], k.shape[0])
    scores = jnp.where(mask[None], scores, -1e30)
    weights = jnp.exp(scores - jnp.max(scores, axis=-1, keepdims=True))
    weights = weights / jnp.sum(weights, axis=-1, keepdims=True)
    weights = weights.reshape(count * q.shape[0], k.shape[0])
    return fold(mm(weights, v), width), weights


def attend_group_back(grad, q, k, v, weights, width):
    grads = spread(grad, width)
    dp = mmt(grads, v)
    ds = weights * (dp - jnp.sum(dp * weights, axis=-1, keepdims=True)) * (width ** -0.5)
    return fold(mm(ds, k), width), tmm(ds, spread(q, width)), tmm(weights, grads)


def crop_rows(count, total):
    return lax.broadcasted_iota(jnp.int32, (count, 1), 0) // (total // CROPS)


def crop_lanes(count, total):
    return lax.broadcasted_iota(jnp.int32, (1, count), 1) // (total // CROPS)


def groups_of(ref, start, size, lanes):
    return [slice(start + at, start + at + lanes) for at in range(0, size, lanes)]


def ffn_kernel(state_ref, gain_ref, up_ref, down_ref, normed_ref, pre_ref, act_ref, out_ref):
    @pl.when(pl.program_id(0) == 0)
    def _():
        hat, _ = normalise(state_ref[...])
        normed_ref[...] = hat * gain_ref[...]
        out_ref[...] = jnp.zeros_like(out_ref)

    pre = mm(normed_ref[...], up_ref[...])
    act = pre * cdf(pre)
    pre_ref[...] = pre
    act_ref[...] = act
    out_ref[...] += mm(act, down_ref[...])


def ffn_forward(state, gain, up, down):
    rows, deep = state.shape
    inner = up.shape[1]
    tile = min(256, inner)
    whole = pl.BlockSpec((rows, deep), lambda t: (0, 0))
    part = pl.BlockSpec((rows, tile), lambda t: (0, t))
    return pl.pallas_call(
        ffn_kernel,
        grid=(inner // tile,),
        out_shape=[shape_of(rows, deep), shape_of(rows, inner), shape_of(rows, inner), shape_of(rows, deep)],
        in_specs=[
            whole,
            pl.BlockSpec((1, deep), lambda t: (0, 0)),
            pl.BlockSpec((deep, tile), lambda t: (0, t)),
            pl.BlockSpec((tile, deep), lambda t: (t, 0)),
        ],
        out_specs=[whole, part, part, whole],
        compiler_params=pltpu.CompilerParams(vmem_limit_bytes=VMEM_LIMIT),
        cost_estimate=pl.CostEstimate(flops=12 * rows * deep * inner, bytes_accessed=8 * deep * inner, transcendentals=0),
    )(state, gain[None], up, down)


def residual_back(base_ref, dsum_ref, state_ref, gain_ref, grad_ref, dgain_ref):
    hat, root = normalise(state_ref[...])
    dsum = dsum_ref[...]
    grad_ref[...] = base_ref[...] + norm_back(dsum, hat, root, gain_ref[...])
    dgain_ref[...] = jnp.sum(dsum * hat, axis=0, keepdims=True)


def ffn_back_kernel(
    base_ref, dsum_ref, state_ref, gain_ref, pre_ref, up_ref, down_ref, grad_ref, dgain_ref, dpre_ref, out_ref
):
    @pl.when(pl.program_id(0) == 0)
    def _():
        residual_back(base_ref, dsum_ref, state_ref, gain_ref, grad_ref, dgain_ref)
        out_ref[...] = jnp.zeros_like(out_ref)

    dpre = mmt(grad_ref[...], down_ref[...]) * gelu_slope(pre_ref[...])
    dpre_ref[...] = dpre
    out_ref[...] += mmt(dpre, up_ref[...])


def ffn_backward(base, dsum, state, gain, pre, up, down):
    rows, deep = state.shape
    inner = up.shape[1]
    tile = min(256, inner)
    whole = pl.BlockSpec((rows, deep), lambda t: (0, 0))
    row = pl.BlockSpec((1, deep), lambda t: (0, 0))
    part = pl.BlockSpec((rows, tile), lambda t: (0, t))
    return pl.pallas_call(
        ffn_back_kernel,
        grid=(inner // tile,),
        out_shape=[shape_of(rows, deep), shape_of(1, deep), shape_of(rows, inner), shape_of(rows, deep)],
        in_specs=[
            whole,
            whole,
            whole,
            row,
            part,
            pl.BlockSpec((deep, tile), lambda t: (0, t)),
            pl.BlockSpec((tile, deep), lambda t: (t, 0)),
        ],
        out_specs=[whole, row, part, whole],
        compiler_params=pltpu.CompilerParams(vmem_limit_bytes=VMEM_LIMIT),
        cost_estimate=pl.CostEstimate(flops=12 * rows * deep * inner, bytes_accessed=8 * deep * inner, transcendentals=0),
    )(base, dsum, state, gain[None], pre, up, down)


def self_kernel(width, state_ref, gain_ref, qkv_ref, wout_ref, normed_ref, packed_ref, att_ref, weights_ref, out_ref):
    hat, _ = normalise(state_ref[...])
    normed = hat * gain_ref[...]
    normed_ref[...] = normed
    part = att_ref.shape[1]
    for at in range(3):
        packed_ref[:, at * part : (at + 1) * part] = mm(normed, qkv_ref[:, at * part : (at + 1) * part])
    rows = normed.shape[0]
    mask = crop_rows(rows, rows) == crop_lanes(rows, rows)
    for g in range(part // 128):
        q, k, v = [packed_ref[:, at * part + g * 128 : at * part + (g + 1) * 128] for at in range(3)]
        att, weights = attend_group(q, k, v, mask, width)
        att_ref[:, g * 128 : (g + 1) * 128] = att
        n = weights.shape[0]
        weights_ref[g * n : (g + 1) * n] = weights
    out_ref[...] = mm(att_ref[...], wout_ref[...])


def self_back_kernel(
    width,
    base_ref,
    dsum_ref,
    state_ref,
    gain_ref,
    packed_ref,
    weights_ref,
    qkv_ref,
    wout_ref,
    grad_ref,
    dgain_ref,
    dpacked_ref,
    out_ref,
):
    residual_back(base_ref, dsum_ref, state_ref, gain_ref, grad_ref, dgain_ref)
    part = dpacked_ref.shape[1] // 3
    datt = mmt(grad_ref[...], wout_ref[...])
    count = 128 // width * datt.shape[0]
    for g in range(part // 128):
        q, k, v = [packed_ref[:, at * part + g * 128 : at * part + (g + 1) * 128] for at in range(3)]
        found = attend_group_back(
            datt[:, g * 128 : (g + 1) * 128], q, k, v, weights_ref[g * count : (g + 1) * count], width
        )
        for at in range(3):
            dpacked_ref[:, at * part + g * 128 : at * part + (g + 1) * 128] = found[at]
    out_ref[...] = mmt(dpacked_ref[...], qkv_ref[...])


def read_kernel(width, q_ref, hat_ref, gain_ref, seg_ref, keyval_ref, wout_ref, kv_ref, att_ref, weights_ref, out_ref):
    part = att_ref.shape[1]
    patches = kv_ref.shape[0] // hat_ref.shape[0]
    for z in range(hat_ref.shape[0]):
        kv_ref[z * patches : (z + 1) * patches] = mm(hat_ref[z, :patches] * gain_ref[...], keyval_ref[...])
    rows = q_ref.shape[0]
    mask = crop_rows(rows, rows) == seg_ref[...]
    for g in range(part // 128):
        at = slice(g * 128, (g + 1) * 128)
        att, weights = attend_group(
            q_ref[:, at], kv_ref[:, at], kv_ref[:, part + g * 128 : part + (g + 1) * 128], mask, width
        )
        att_ref[:, at] = att
        n = weights.shape[0]
        weights_ref[g * n : (g + 1) * n] = weights
    out_ref[...] = mm(att_ref[...], wout_ref[...])


def read_back_kernel(
    width,
    base_ref,
    dsum_ref,
    state_ref,
    gain_ref,
    q_ref,
    kv_ref,
    weights_ref,
    wquery_ref,
    keyval_ref,
    wout_ref,
    latents_ref,
    hat_ref,
    grad_ref,
    dgain_ref,
    dq_ref,
    dkv_ref,
    dlat_ref,
    dint_ref,
    dgain_lat_ref,
    dgain_int_ref,
):
    residual_back(base_ref, dsum_ref, state_ref, gain_ref, grad_ref, dgain_ref)
    part = dq_ref.shape[1]
    datt = mmt(grad_ref[...], wout_ref[...])
    count = 128 // width * datt.shape[0]
    for g in range(part // 128):
        at, behind = slice(g * 128, (g + 1) * 128), slice(part + g * 128, part + (g + 1) * 128)
        found = attend_group_back(
            datt[:, at], q_ref[:, at], kv_ref[:, at], kv_ref[:, behind], weights_ref[g * count : (g + 1) * count], width
        )
        dq_ref[:, at], dkv_ref[:, at], dkv_ref[:, behind] = found
    dlat = mmt(dq_ref[...], wquery_ref[...])
    dlat_ref[...] = dlat
    hat, _ = normalise(latents_ref[...])
    dgain_lat_ref[...] = jnp.sum(dlat * hat, axis=0, keepdims=True)
    dint = mmt(dkv_ref[...], keyval_ref[...])
    dint_ref[...] = dint
    patches = dint.shape[0] // hat_ref.shape[0]
    dgain_int = jnp.zeros_like(dgain_int_ref)
    for z in range(hat_ref.shape[0]):
        dgain_int += jnp.sum(dint[z * patches : (z + 1) * patches] * hat_ref[z, :patches], axis=0, keepdims=True)
    dgain_int_ref[...] = dgain_int


def write_kernel(
    width,
    state_ref,
    gain_ref,
    hat_ref,
    int_ref,
    cot_ref,
    gains_ref,
    seg_ref,
    place_ref,
    sources,
    normed_ref,
    new_ref,
    dafter_ref,
    dq_ref,
    att_ref,
    y_ref,
    act_ref,
    dpre_ref,
    dkv_ref,
    dgain_ref,
    out_ref,
    dhat_ref,
    wkv,
    wquery,
    wout,
    up,
    down,
    kv,
    q,
    weights,
    dy,
    sems,
):
    targets = [wkv, wquery, wout, up, down]
    if len(sources) == 5:
        for n in range(5):
            pltpu.make_async_copy(sources[n], targets[n], sems.at[n]).start()
    else:
        bring_pieces(sources, targets, sems, place_ref[0])

    def arrived(n):
        pltpu.make_async_copy(targets[n], targets[n], sems.at[n]).wait()

    hat4, _ = normalise(state_ref[...])
    normed = hat4 * gain_ref[...]
    normed_ref[...] = normed
    wide = hat_ref.shape[1]
    patches = hat_ref.shape[0]
    lats = normed.shape[0]
    arrived(1)
    q[...] = mm(hat_ref[...] * gains_ref[0:1], wquery[...].reshape(wide, wide))
    arrived(0)

    def project(t, carry):
        at = pl.ds(pl.multiple_of(t * 256, 256), 256)
        kv[:, at] = mm(normed_ref[...], wkv[:, at])
        return carry

    lax.fori_loop(0, kv.shape[1] // 256, project, 0)
    mask = seg_ref[...] == crop_lanes(lats, lats)
    count = 128 // width * patches

    def forward(g, carry):
        at = pl.ds(pl.multiple_of(g * 128, 128), 128)
        behind = pl.ds(pl.multiple_of(wide + g * 128, 128), 128)
        found, shares = attend_group(q[:, at], kv[:, at], kv[:, behind], mask, width)
        att_ref[:, at] = found
        weights[pl.ds(pl.multiple_of(g * count, count), count)] = shares
        return carry

    lax.fori_loop(0, wide // 128, forward, 0)
    arrived(2)
    after = int_ref[...] + mm(att_ref[...], wout[...].reshape(wide, wide))
    after_hat, after_root = normalise(after)
    y_ref[...] = after_hat * gains_ref[1:2]
    new_ref[...] = after
    dy[...] = jnp.zeros_like(dy)
    arrived(3)
    arrived(4)
    tile = down.shape[1] * down.shape[2]

    def mlp(t, carry):
        at = pl.ds(pl.multiple_of(t * tile, tile), tile)
        up_part = up[:, :, at].reshape(wide, tile)
        down_part = down[t].reshape(tile, wide)
        pre = mm(y_ref[...], up_part)
        share = cdf(pre)
        act = pre * share
        act_ref[:, at] = act
        new_ref[...] += mm(act, down_part)
        slope = share + pre * DENSITY * jnp.exp(-0.5 * pre * pre)
        dpre = mmt(cot_ref[...], down_part) * slope
        dpre_ref[:, at] = dpre
        dy[...] += mmt(dpre, up_part)
        return carry

    lax.fori_loop(0, down.shape[0], mlp, 0)
    dgain_ref[...] = jnp.sum(dy[...] * after_hat, axis=0, keepdims=True)
    dafter_ref[...] = cot_ref[...] + norm_back(dy[...], after_hat, after_root, gains_ref[1:2])
    dy[...] = mmt(dafter_ref[...], wout[...].reshape(wide, wide))

    def backward(g, carry):
        at = pl.ds(pl.multiple_of(g * 128, 128), 128)
        behind = pl.ds(pl.multiple_of(wide + g * 128, 128), 128)
        shares = weights[pl.ds(pl.multiple_of(g * count, count), count)]
        found = attend_group_back(dy[:, at], q[:, at], kv[:, at], kv[:, behind], shares, width)
        dq_ref[:, at], dkv_ref[:, at], dkv_ref[:, behind] = found
        return carry

    lax.fori_loop(0, wide // 128, backward, 0)

    def close(t, carry):
        at = pl.ds(pl.multiple_of(t * 256, 256), 256)
        out_ref[:, at] = mmt(dkv_ref[...], wkv[at, :])
        return carry

    lax.fori_loop(0, out_ref.shape[1] // 256, close, 0)
    dhat_ref[...] = mmt(dq_ref[...], wquery[...].reshape(wide, wide))


def bring_pieces(sources, targets, sems, place):
    wkv, wquery, wout, up, down = targets
    zs, rows, wide = wquery.shape
    ds, _, inner, _ = down.shape
    pack = up.shape[2] // ds
    deep_rows, q_rows = wkv.shape[0] // ds, rows // ds
    lanes = wide // zs
    first = rows + inner * (wide // pack)
    for step in range(ds):
        d = jnp.bitwise_xor(place, step)
        base = (step % 2) * 5
        near = sources[base + min(step // 2, 3)]
        far, shift = (sources[base + 4], first) if step // 2 == 3 else (near, 0)

        def bring(source, target, sem):
            pltpu.make_async_copy(source, target, sems.at[sem]).start()

        at = first - shift
        for z in range(zs):
            for b in range(2):
                bring(
                    far.at[z, at : at + deep_rows, b * lanes : (b + 1) * lanes],
                    wkv.at[pl.ds(pl.multiple_of(d * deep_rows, deep_rows), deep_rows), pl.ds(b * wide + z * lanes, lanes)],
                    0,
                )
        at += deep_rows
        for n, target in ((1, wquery), (2, wout)):
            for b in range(wide // pack):
                bring(
                    far.at[:, at : at + q_rows],
                    target.at[:, pl.ds(pl.multiple_of(d * q_rows, q_rows), q_rows), pl.ds(b * pack, pack)],
                    n,
                )
                at += q_rows
        bring(near.at[:, :rows], up.at[:, :, pl.ds(pl.multiple_of(d * pack, pack), pack)], 3)
        for b in range(wide // pack):
            start = rows + b * inner
            bring(near.at[:, start : start + inner], down.at[d, :, :, pl.ds(b * pack, pack)], 4)


def write_stage(state, gain, hat, interface, cot, gains, seg, place, sources, shapes):
    rows, deep = state.shape
    patches, wide = hat.shape
    hidden = shapes[3][2]
    n = HEADS * patches
    small = shape_of(patches, wide)
    big = shape_of(patches, hidden)
    outs = [
        shape_of(rows, deep), small, small, small, small, small, big, big,
        shape_of(rows, 2 * wide), shape_of(1, wide), shape_of(rows, deep), small,
    ]
    vmem = pl.BlockSpec(memory_space=pltpu.VMEM)
    kernel = functools.partial(write_kernel, wide // HEADS)
    count = len(sources)

    def call(*refs):
        kernel(*refs[:8], refs[8 : 8 + count], *refs[8 + count :])

    return pl.pallas_call(
        call,
        out_shape=outs,
        in_specs=[vmem] * 7 + [pl.BlockSpec(memory_space=pltpu.SMEM)] + [pl.BlockSpec(memory_space=pl.ANY)] * count,
        out_specs=[vmem] * len(outs),
        scratch_shapes=[pltpu.VMEM(shape, jnp.float32) for shape in shapes]
        + [
            pltpu.VMEM((rows, 2 * wide), jnp.float32),
            pltpu.VMEM((patches, wide), jnp.float32),
            pltpu.VMEM((n, rows), jnp.float32),
            pltpu.VMEM((patches, wide), jnp.float32),
            pltpu.SemaphoreType.DMA((5,)),
        ],
        compiler_params=pltpu.CompilerParams(vmem_limit_bytes=VMEM_LIMIT),
        cost_estimate=pl.CostEstimate(flops=20_000_000_000, bytes_accessed=40_000_000, transcendentals=0),
    )(state, gain[None], hat, interface, cot, gains, seg, place, *sources)


def grads_kernel(y_ref, dpre_ref, act_ref, cot_ref, hat_ref, gain_ref, dq_ref, att_ref, dafter_ref, place_ref, mine_ref, other_ref, square):
    core = jnp.bitwise_and(place_ref[0], 1)
    wide = y_ref.shape[1]
    pack = mine_ref.shape[3]
    chips, zs = mine_ref.shape[0], mine_ref.shape[1]
    rows = wide // zs
    inner = pack // zs
    q_rows = rows // (2 * chips)
    square[0] = tmm(hat_ref[...] * gain_ref[...], dq_ref[...])
    square[1] = tmm(att_ref[...], dafter_ref[...])

    def step(j, carry):
        for out_ref, bit in ((mine_ref, core), (other_ref, 1 - core)):
            d = 2 * j + bit
            at = pl.ds(pl.multiple_of(d * pack, pack), pack)
            out_ref[j, :, :rows] = tmm(y_ref[...], dpre_ref[:, at]).reshape(zs, rows, pack)
            start = rows
            ddown = tmm(act_ref[:, at], cot_ref[...])
            for b in range(wide // pack):
                out_ref[j, :, start : start + inner] = ddown[:, b * pack : (b + 1) * pack].reshape(zs, inner, pack)
                start += inner
            for n in range(2):
                for b in range(wide // pack):
                    for z in range(zs):
                        source = pl.ds(pl.multiple_of(z * rows + d * q_rows, q_rows), q_rows)
                        out_ref[j, z, start : start + q_rows] = square[n, source, b * pack : (b + 1) * pack]
                    start += q_rows
        return carry

    lax.fori_loop(0, chips, step, 0)


def interface_grads(y, dpre, act, cot, hat, gain, dq, att, dafter, place, zs, rows):
    patches, wide = y.shape
    pack = dpre.shape[1] // 8
    out = shape_of(4, zs, rows, pack)
    vmem = pl.BlockSpec(memory_space=pltpu.VMEM)
    return pl.pallas_call(
        grads_kernel,
        out_shape=[out, out],
        in_specs=[vmem] * 9 + [pl.BlockSpec(memory_space=pltpu.SMEM)],
        out_specs=[vmem, vmem],
        scratch_shapes=[pltpu.VMEM((2, wide, wide), jnp.float32)],
        compiler_params=pltpu.CompilerParams(vmem_limit_bytes=VMEM_LIMIT),
        cost_estimate=pl.CostEstimate(flops=10_000_000_000, bytes_accessed=20_000_000, transcendentals=0),
    )(y, dpre, act, cot, hat, gain, dq, att, dafter, place)


def outer_kernel(specs, lefts, sums, place_ref, *refs):
    pieces, refs = refs[:10], refs[10:]
    arrays, refs = refs[:lefts], refs[lefts:]
    outs, refs = refs[: len(specs)], refs[len(specs) :]
    if sums:
        sum_ref, refs = refs[0], refs[1:]
    right, held, sems = refs[0], refs[1 : 1 + len(specs)], refs[1 + len(specs)]
    ds, rows, _ = right.shape
    for step in range(ds):
        d = jnp.bitwise_xor(place_ref[0], step)
        base, far = (step % 2) * 5, step // 2
        if far < 3:
            pltpu.make_async_copy(pieces[base + far], right.at[d], sems.at[0]).start()
        else:
            for n in range(2):
                target = right.at[d, n * rows // 2 : (n + 1) * rows // 2]
                pltpu.make_async_copy(pieces[base + 3 + n], target, sems.at[0]).start()
    copies = []
    for n, (which, at, width, _, _) in enumerate(specs):
        copies.append(pltpu.make_async_copy(arrays[which].at[:, at : at + width], held[n], sems.at[n + 1]))
        copies[-1].start()
    pltpu.make_async_copy(right, right, sems.at[0]).wait()
    if sums:
        sum_ref[...] = jnp.sum(right[:, :, sums[0] : sums[0] + sums[1]], axis=0)
    for n, (_, _, width, at, columns) in enumerate(specs):
        copies[n].wait()
        tile = min(256, width)

        def step(t, carry, n=n, at=at, columns=columns, tile=tile):
            here = pl.ds(pl.multiple_of(t * tile, tile), tile)
            values = right[:, :, at : at + columns].reshape(ds * rows, columns)
            outs[n][here, :] = tmm(held[n][:, here], values)
            return carry

        lax.fori_loop(0, width // tile, step, 0)


def outer_products(pieces, place, arrays, specs, sums=()):
    rows, columns = pieces[0].shape
    outs = [shape_of(spec[2], spec[4]) for spec in specs]
    if sums:
        outs.append(shape_of(rows, sums[1]))
    anywhere = pl.BlockSpec(memory_space=pl.ANY)
    total = arrays[0].shape[0]
    return pl.pallas_call(
        functools.partial(outer_kernel, specs, len(arrays), sums),
        out_shape=outs,
        in_specs=[pl.BlockSpec(memory_space=pltpu.SMEM)] + [anywhere] * (len(pieces) + len(arrays)),
        out_specs=[pl.BlockSpec(memory_space=pltpu.VMEM)] * len(outs),
        scratch_shapes=[pltpu.VMEM((total // rows, rows, columns), jnp.float32)]
        + [pltpu.VMEM((total, spec[2]), jnp.float32) for spec in specs]
        + [pltpu.SemaphoreType.DMA((len(specs) + 1,))],
        compiler_params=pltpu.CompilerParams(vmem_limit_bytes=VMEM_LIMIT),
        cost_estimate=pl.CostEstimate(
            flops=sum(6 * total * spec[2] * spec[4] for spec in specs), bytes_accessed=20_000_000, transcendentals=0
        ),
    )(place, *pieces, *arrays)


def local(
    interface,
    latents,
    segment_ids,
    read_gain_lat,
    read_gain_int,
    read_query,
    read_keyval,
    read_out,
    read_gain_mlp,
    read_up,
    read_down,
    layer_gain_att,
    layer_qkv,
    layer_out,
    layer_gain_mlp,
    layer_up,
    layer_down,
    write_gain_int,
    write_query,
    write_gain_lat,
    write_keyval,
    write_out,
    write_gain_mlp,
    write_up,
    write_down,
    interface_cot,
    latents_cot,
):
    zs, ds = lax.axis_size("head"), lax.axis_size("dp")
    me, dd = lax.axis_index("head"), lax.axis_index("dp")
    here = HEADS // zs

    def shift(values, step):
        return lax.ppermute(values, "head", [(i, (i + step) % zs) for i in range(zs)])

    def z_scatter(parts):
        total = lax.dynamic_index_in_dim(parts, me, 0, keepdims=False)
        for step in range(1, zs):
            sent = lax.dynamic_index_in_dim(parts, (me + step) % zs, 0, keepdims=False)
            total = total + shift(sent, step)
        return total

    def z_gather(own):
        out = jnp.zeros((zs,) + own.shape, own.dtype)
        out = lax.dynamic_update_index_in_dim(out, own, me, 0)
        for step in range(1, zs):
            out = lax.dynamic_update_index_in_dim(out, shift(own, step), (me - step) % zs, 0)
        return out

    def tie(*values):
        return lax.optimization_barrier(values)

    def sum_over_head(partial, base=None, release=()):
        rows = partial.shape[0] // zs
        own = z_scatter(partial.reshape(zs, rows, -1))
        if base is not None:
            own = own + lax.dynamic_slice_in_dim(base, me * rows, rows, 0)
        own, *release = tie(own, *release)
        full = z_gather(own).reshape(partial.shape)
        return (full, *release) if release else full

    def cut_up(full, parts):
        out, at = [], 0
        for part in parts:
            out.append(full[:, at : at + part.shape[1]])
            at += part.shape[1]
        return out

    def join(parts):
        return jnp.concatenate(parts, axis=1) if len(parts) > 1 else parts[0]

    def d_gather(parts):
        return lax.all_gather(join(parts), "dp", axis=0, tiled=True)

    direct = ds == 8
    chip, core = dd // 2, dd % 2

    def swap(values, bits):
        return lax.ppermute(values, "dp", [(i, i ^ bits) for i in range(ds)])

    def to_sides(joined):
        return [joined, swap(joined, 2), swap(joined, 4)]

    def to_across(joined, by_x, by_y):
        half = joined.shape[0] // 2
        return [joined, by_x, by_y, swap(by_x[:half], 4), swap(by_y[half:], 2)]

    def to_core(*blocks):
        return [*blocks, *(swap(block, 1) for block in blocks)]

    def pick(values, index, axis):
        return lax.dynamic_index_in_dim(values, index, axis, keepdims=False)

    def scatter_one(mine, got):
        x, rows = chip % 2, mine.shape[1]
        mine = mine.reshape((2, 2) + mine.shape[1:])
        got = got.reshape(mine.shape)
        y = chip // 2
        mh, gh, ml, gl = mine[:, :, : rows // 2], got[:, :, : rows // 2], mine[:, :, rows // 2 :], got[:, :, rows // 2 :]
        high, low = pick(mh, x, 1) + pick(gh, x, 1), pick(ml, y, 0) + pick(gl, y, 0)
        sent_high, sent_low = pick(mh, 1 - x, 1) + pick(gh, 1 - x, 1), pick(ml, 1 - y, 0) + pick(gl, 1 - y, 0)
        return high, low, swap(sent_high, 2), swap(sent_low, 4)

    def scatter_two(high, low, got_high, got_low):
        y, x = chip // 2, chip % 2
        sent_high, sent_low = pick(high, 1 - y, 0) + pick(got_high, 1 - y, 0), pick(low, 1 - x, 0) + pick(got_low, 1 - x, 0)
        high, low = pick(high, y, 0) + pick(got_high, y, 0), pick(low, x, 0) + pick(got_low, x, 0)
        return jnp.concatenate([high + swap(sent_high, 4), low + swap(sent_low, 2)], axis=0)

    def d_scatter(parts):
        parts = parts.reshape((4, 2) + parts.shape[1:])
        return scatter_two(*scatter_one(pick(parts, core, 1), swap(pick(parts, 1 - core, 1), 1)))

    interface, latents, segments = interface[0], latents[0], segment_ids[0]
    interface_cot, latents_cot = interface_cot[0], latents_cot[0]
    layer_gain_att, layer_gain_mlp = layer_gain_att[0], layer_gain_mlp[0]
    layer_out, layer_up, layer_down = layer_out[0], layer_up[0], layer_down[0]
    patches, wide = interface.shape
    count, deep = latents.shape
    qkv = layer_qkv[0].reshape(deep, -1)
    keyval = read_keyval.reshape(wide, -1)
    part = deep // zs
    hidden = write_down.shape[0] * zs

    own_segments = lax.dynamic_slice_in_dim(segments, me * patches, patches, 0)

    lat_hat, lat_root = normalise(latents)
    lat_normed = lat_hat * read_gain_lat
    early_all = d_gather([lat_normed])
    int_hat, int_root = normalise(interface)
    gains = jnp.stack([read_gain_int, write_gain_int, write_gain_mlp])
    gains = jnp.pad(gains, ((0, 5), (0, wide - gains.shape[1])))
    int_pack = z_gather(jnp.concatenate([int_hat, gains], axis=0))
    query = mm(lat_normed, read_query)

    wq_rows, up_cols, kv_rows = wide // zs // ds, hidden // ds, deep // ds
    pack = up_cols
    up_share = write_up.reshape(wide // zs, zs, ds, up_cols // zs)
    up_share = lax.dynamic_index_in_dim(up_share, dd, 2, keepdims=False).reshape(wide // zs, up_cols)
    down_share = lax.dynamic_index_in_dim(write_down.reshape(ds, -1, wide), dd, 0, keepdims=False)
    kv_share = lax.dynamic_slice_in_dim(write_keyval, dd * kv_rows, kv_rows, 0).reshape(kv_rows, -1)
    q_share = lax.dynamic_slice_in_dim(write_query, dd * wq_rows, wq_rows, 0)
    o_share = lax.dynamic_slice_in_dim(write_out, dd * wq_rows, wq_rows, 0)

    def narrow(share):
        return [share[:, at : at + pack] for at in range(0, share.shape[1], pack)]

    def widen(full, at, rows, columns):
        n = columns // pack
        return jnp.concatenate([full[:, :, at + i * rows : at + (i + 1) * rows] for i in range(n)], axis=-1)

    flat = jnp.concatenate(
        [up_share] + narrow(down_share) + narrow(kv_share) + narrow(q_share) + narrow(o_share), axis=0
    )
    query, int_pack, flat, early_all = lax.optimization_barrier((query, int_pack, flat, early_all))
    gains = jnp.transpose(int_pack[:, patches : patches + 3, : wide // zs], (1, 0, 2)).reshape(3, wide)
    gain_read, gain_write, gain_mlp = gains[0], gains[1], gains[2]
    shares = lax.all_gather(flat, "head", axis=0, tiled=False)

    kv0, read_attended, read_weights, part0 = run_whole(
        functools.partial(read_kernel, deep // HEADS),
        [
            shape_of(zs * patches, 2 * part),
            shape_of(count, part),
            shape_of(here * count, zs * patches),
            shape_of(count, deep),
        ],
        (query, int_pack, gain_read[None], segment_ids, keyval, read_out),
        flops=8 * zs * patches * wide * part,
    )

    state1 = sum_over_head(part0, latents)
    normed1, pre1, act1, part1 = ffn_forward(state1, read_gain_mlp, read_up, read_down)
    down_rows = hidden // zs // ds
    middle = wide // zs + down_rows * (wide // pack)
    part1, shares = tie(part1, shares)
    if direct:
        by_x, by_y = swap(shares, 2), swap(shares, 4)
    state2, read_attended, normed1, act1 = sum_over_head(part1, state1, (read_attended, normed1, act1))
    read_joined = join([read_attended, normed1, act1])

    normed2, packed, self_attended, self_weights, part2 = run_whole(
        functools.partial(self_kernel, deep // HEADS),
        [
            shape_of(count, deep),
            shape_of(count, 3 * part),
            shape_of(count, part),
            shape_of(here * count, count),
            shape_of(count, deep),
        ],
        (state2, layer_gain_att[None], qkv, layer_out),
        flops=8 * count * deep * part,
    )
    if direct:
        part2, by_x, by_y = tie(part2, by_x, by_y)
        pieces = [shares, by_x, by_y, swap(by_x[:, :middle], 4), swap(by_y[:, middle:], 2)]
    state3 = sum_over_head(part2, state2)
    normed3, pre3, act3, part3 = ffn_forward(state3, layer_gain_mlp, layer_up, layer_down)

    if direct:
        part3, read_joined, *pieces = tie(part3, read_joined, *pieces)
        pieces = pieces + [swap(piece, 1) for piece in pieces]
    else:
        everything = lax.all_gather(shares, "dp", axis=0, tiled=False)
        full_up = jnp.transpose(everything[:, :, : wide // zs], (1, 2, 0, 3)).reshape(zs, wide // zs, hidden)
        at = wide // zs
        full_down = widen(everything, at, down_rows, wide)
        at += down_rows * (wide // pack)
        full_kv = widen(everything, at, kv_rows, 2 * wide // zs)
        full_kv = jnp.transpose(full_kv.reshape(ds, zs, kv_rows, 2, -1), (0, 2, 3, 1, 4)).reshape(deep, 2 * wide)
        at += kv_rows * (2 * wide // zs // pack)
        full_query = jnp.transpose(widen(everything, at, wq_rows, wide), (1, 0, 2, 3)).reshape(zs, -1, wide)
        at += wq_rows * (wide // pack)
        full_out = jnp.transpose(widen(everything, at, wq_rows, wide), (1, 0, 2, 3)).reshape(zs, -1, wide)
        pieces = [full_kv, full_query, full_out, full_up, full_down]
    read_all = d_gather([read_joined])
    state4, normed2, self_attended, normed3, act3 = sum_over_head(
        part3, state3, (normed2, self_attended, normed3, act3)
    )
    layer_all = d_gather([normed2, self_attended, normed3, act3])

    (
        normed4, interface_new, dafter, dwrite_q, write_attended, after_normed, act5, dpre5, dkv4, dgain_mlp, part4,
        dwrite_normed,
    ) = write_stage(
        state4,
        write_gain_lat,
        int_hat,
        interface,
        interface_cot,
        jnp.stack([gain_write, gain_mlp]),
        own_segments[:, None],
        dd.astype(jnp.int32)[None],
        pieces,
        [
            (deep, 2 * wide),
            (zs, wide // zs, wide),
            (zs, wide // zs, wide),
            (zs, wide // zs, hidden),
            (ds, zs, down_rows, wide),
        ],
    )
    dsum4, after_normed, dpre5, act5, dwrite_q, write_attended, dafter, dkv4 = sum_over_head(
        part4, None, (after_normed, dpre5, act5, dwrite_q, write_attended, dafter, dkv4)
    )

    place = dd.astype(jnp.int32)[None]
    piece_rows = middle + 2 * wq_rows * (wide // pack)
    if direct:
        grads_mine, grads_other = interface_grads(
            after_normed, dpre5, act5, interface_cot, int_hat, gain_write[None], dwrite_q, write_attended, dafter,
            place, zs, piece_rows,
        )
        dsum4, grads_mine, grads_other = tie(dsum4, grads_mine, grads_other)
        grads_mine = grads_mine.reshape(4, -1, pack)
        grads_got = swap(grads_other.reshape(4, -1, pack), 1)
    else:
        write_normed = int_hat * gain_write
        dup = jnp.transpose(tmm(after_normed, dpre5).reshape(zs, wide // zs, ds, -1), (2, 0, 1, 3))

        def pack_grad(grad, rows):
            grad = grad.reshape(ds, zs, rows, wide)
            return [grad[..., at : at + pack] for at in range(0, wide, pack)]

        ddown = tmm(act5, interface_cot)
        dquery = jnp.transpose(tmm(write_normed, dwrite_q).reshape(zs, ds, wq_rows, wide), (1, 0, 2, 3))
        dout = jnp.transpose(tmm(write_attended, dafter).reshape(zs, ds, wq_rows, wide), (1, 0, 2, 3))
        packed_grads = jnp.concatenate(
            [dup] + pack_grad(ddown, down_rows) + pack_grad(dquery, wq_rows) + pack_grad(dout, wq_rows), axis=2
        )
        grads_mine = lax.psum_scatter(packed_grads, "dp", scatter_dimension=0, tiled=False)

    dint = dafter + norm_back(dwrite_normed, int_hat, int_root, gain_write)

    dkv_parts = jnp.transpose(dkv4.reshape(count, 2, zs, -1), (2, 0, 1, 3)).reshape(zs, count, -1)
    dsum4, dkv_parts = tie(dsum4, dkv_parts)
    dkv_mine = z_scatter(dkv_parts)
    dstate4, dgain4, dpre3, part5 = ffn_backward(
        latents_cot, dsum4, state4, write_gain_lat, pre3, layer_up, layer_down
    )
    if direct:
        part5, grads_mine, grads_got, dkv_mine = tie(part5, grads_mine, grads_got, dkv_mine)
        grads_mine = lax.psum_scatter(
            grads_mine + grads_got,
            "dp",
            scatter_dimension=0,
            axis_index_groups=[[2 * k + c for k in range(ds // 2)] for c in range(2)],
        )
    dsum3, normed4, dkv_mine, released4, dpre3 = sum_over_head(part5, None, (normed4, dkv_mine, dstate4, dpre3))
    write_all = d_gather([normed4, dkv_mine, released4, dpre3])
    dsum3, read_all = tie(dsum3, read_all)
    dstate3, dgain3, dpacked, part6 = run_whole(
        functools.partial(self_back_kernel, deep // HEADS),
        [shape_of(count, deep), shape_of(1, deep), shape_of(count, 3 * part), shape_of(count, deep)],
        (dstate4, dsum3, state3, layer_gain_mlp[None], packed, self_weights, qkv, layer_out),
        flops=8 * count * deep * part,
    )
    dsum2, released3, dpacked = sum_over_head(part6, None, (dstate3, dpacked))
    dsum2, layer_all = tie(dsum2, layer_all)

    dstate2, dgain2, dpre1, part7 = ffn_backward(
        dstate3, dsum2, state2, layer_gain_att, pre1, read_up, read_down
    )
    dsum1, released2, dpre1 = sum_over_head(part7, None, (dstate2, dpre1))
    both_all = d_gather([released3, dpacked, released2, dpre1])
    dsum1, grads_mine = tie(dsum1, grads_mine)
    grads_mine = z_scatter(grads_mine.reshape(zs, -1, pack))
    dstate1, dgain1, dquery0, dread_kv, dlat_part, dint_part, dgain_lat, dgain_int = run_whole(
        functools.partial(read_back_kernel, deep // HEADS),
        [
            shape_of(count, deep),
            shape_of(1, deep),
            shape_of(count, part),
            shape_of(zs * patches, 2 * part),
            shape_of(count, deep),
            shape_of(zs * patches, wide),
            shape_of(1, deep),
            shape_of(1, wide),
        ],
        (dstate2, dsum1, state1, read_gain_mlp[None], query, kv0, read_weights, read_query, keyval, read_out, latents, int_pack),
        flops=16 * zs * patches * wide * part,
    )
    dlat_part, dstate1, grads_mine = tie(dlat_part, dstate1, grads_mine)

    first = (me == 0).astype(jnp.float32)
    small = jnp.concatenate(
        [dgain_lat[0]]
        + [g[0] * first for g in (dgain1, dgain2, dgain3, dgain4)]
        + [dgain_int[0], jnp.sum(dwrite_normed * int_hat, axis=0), dgain_mlp[0]]
    )
    lanes = small.size // count
    fill = jnp.pad(small.reshape(count, lanes), ((0, 0), (0, -lanes % 128)))
    late = [join([dstate1, dquery0, fill])]

    dkeyval = tmm(int_pack[:, :patches].reshape(zs * patches, wide) * gain_read, dread_kv)
    half = z_scatter(dlat_part.reshape(zs, count // zs, deep))
    wide_lat = read_attended.shape[1]
    write_all = tie(write_all, dgain_int)[0]
    normed4_all, dkv_all, dstate4_all, dpre3_all = cut_up(write_all, [normed4, dkv_mine, dstate4, dpre3])
    normed2_all, self_att_all, normed3_all, act3_all = cut_up(layer_all, [normed2, self_attended, normed3, act3])
    grad_layer_up, grad_layer_down = tmm(normed3_all, dpre3_all), tmm(act3_all, dstate4_all)
    grad_write_keyval = tmm(normed4_all, dkv_all)
    if direct:
        late = to_sides(*late)
        dkeyval = dkeyval.reshape(4, 2, -1, 2 * part)
        pair = [pick(dkeyval, core, 1), swap(pick(dkeyval, 1 - core, 1), 1)]
        half, dint_part, grad_layer_up, grad_layer_down, grad_write_keyval, *held = tie(
            half, dint_part, grad_layer_up, grad_layer_down, grad_write_keyval, *late, *pair
        )
        late, pair = to_across(*held[:3]), scatter_one(*held[3:])
    dint_normed = z_scatter(dint_part.reshape(zs, patches, wide))
    dlat = z_gather(half).reshape(count, deep)
    if direct:
        dlat, dint_normed, both_all, *held = tie(dlat, dint_normed, both_all, *late, *pair)
        late, pair = held[:5], held[5:]
        late, dkeyval = to_core(*late), scatter_two(*pair)
        flat = jnp.concatenate([grads_mine] + [dkeyval[:, at : at + pack] for at in range(0, 2 * part, pack)], axis=0)
        grads_all = lax.all_gather(flat, "dp", axis=0, tiled=False)
        grad_read_keyval = widen(grads_all[:, None], piece_rows, dkeyval.shape[0], 2 * part)
    else:
        grads_all = lax.all_gather(grads_mine, "dp", axis=0, tiled=False)
        grad_read_keyval = lax.psum(dkeyval, "dp")
    dstate3_all, dpacked_all, dstate2_all, dpre1_all = cut_up(both_all, [dstate3, dpacked, dstate2, dpre1])
    grad_layer_qkv, grad_layer_out = tmm(normed2_all, dpacked_all), tmm(self_att_all, dstate3_all)
    read_att_all, normed1_all, act1_all = cut_up(read_all, [read_attended, normed1, act1])
    if direct:
        grad_read_query, grad_read_out, small = outer_products(
            late,
            place,
            [early_all, read_all],
            [(0, 0, deep, deep, part), (1, 0, part, 0, deep)],
            (deep + part, fill.shape[1]),
        )
        small = small[:, :lanes]
    else:
        late_all = d_gather(late)
        dstate1_all, dquery0_all, small = cut_up(late_all, [dstate1, dquery0, fill])
        grad_read_query, grad_read_out = tmm(early_all, dquery0_all), tmm(read_att_all, dstate1_all)
        small = jnp.sum(small.reshape(ds, count, -1)[:, :, :lanes], axis=0)
    grad_read_up, grad_read_down = tmm(normed1_all, dpre1_all), tmm(act1_all, dstate2_all)
    latents_grad = dstate1 + norm_back(dlat, lat_hat, lat_root, read_gain_lat)
    interface_grad = dint + norm_back(dint_normed, int_hat, int_root, gain_read)
    small = jnp.sum(z_gather(small), axis=0).reshape(-1)
    lat_gains = small[: 5 * deep].reshape(5, deep)
    int_gains = small[5 * deep :].reshape(3, zs, wide // zs)
    int_gains = lax.dynamic_index_in_dim(int_gains, me, 1, keepdims=False)

    full = grads_all[:, None]
    grad_write_up = grads_all[:, : wide // zs].reshape(ds, wide // zs, zs, up_cols // zs)
    grad_write_up = jnp.transpose(grad_write_up, (1, 2, 0, 3)).reshape(write_up.shape)
    at = wide // zs
    grad_write_down = widen(full, at, down_rows, wide).reshape(write_down.shape)
    at += down_rows * (wide // pack)
    grad_write_query = widen(full, at, wq_rows, wide).reshape(write_query.shape)
    at += wq_rows * (wide // pack)
    grad_write_out = widen(full, at, wq_rows, wide).reshape(write_out.shape)

    return (
        interface_new[None],
        state4[None],
        interface_grad[None],
        latents_grad[None],
        lat_gains[0],
        int_gains[0],
        grad_read_query,
        grad_read_keyval.reshape(read_keyval.shape),
        grad_read_out,
        lat_gains[1],
        grad_read_up,
        grad_read_down,
        lat_gains[2][None],
        grad_layer_qkv.reshape(layer_qkv.shape),
        grad_layer_out[None],
        lat_gains[3][None],
        grad_layer_up[None],
        grad_layer_down[None],
        int_gains[1],
        grad_write_query,
        lat_gains[4],
        grad_write_keyval.reshape(write_keyval.shape),
        grad_write_out,
        int_gains[2],
        grad_write_up,
        grad_write_down,
    )


def solution(mesh):
    rows, both = P("dp", "head", None), P("dp", None, None)
    weights = (
        P(),
        P("head"),
        P(None, "head"),
        P(None, None, "head"),
        P("head", None),
        P(),
        P(None, "head"),
        P("head", None),
        P(),
        P(None, None, None, "head"),
        P(None, "head", None),
        P(),
        P(None, None, "head"),
        P(None, "head", None),
        P("head"),
        P("head", None),
        P(),
        P(None, None, "head"),
        P("head", None),
        P("head"),
        P("head", None),
        P("head", None),
    )
    in_specs = (rows, both, P("dp", None)) + weights + (rows, both)
    out_specs = (rows, both, rows, both) + weights
    return jax.shard_map(local, mesh=mesh, in_specs=in_specs, out_specs=out_specs, check_vma=False)
```

```python
import functools

import jax
import jax.numpy as jnp
from jax import lax
from jax.experimental import pallas as pl
from jax.experimental.pallas import tpu as pltpu
from jax.sharding import PartitionSpec as P

HEADS = 16
CROPS = 4
EPSILON = 1e-05
PRECISE = lax.Precision.HIGH
ROOT_HALF = 0.7071067811865476
DENSITY = 0.3989422804014327
VMEM_LIMIT = 56 * 1024 * 1024


def mm(left, right):
    return lax.dot_general(left, right, (((1,), (0,)), ((), ())), precision=PRECISE)


def mmt(left, right):
    return lax.dot_general(left, right, (((1,), (1,)), ((), ())), precision=PRECISE)


def tmm(left, right):
    return lax.dot_general(left, right, (((0,), (0,)), ((), ())), precision=PRECISE)


def normalise(values):
    centred = values - jnp.mean(values, axis=-1, keepdims=True)
    root = lax.rsqrt(jnp.mean(centred * centred, axis=-1, keepdims=True) + EPSILON)
    return centred * root, root


def norm_back(grad, xhat, root, gain):
    scaled = grad * gain
    return root * (
        scaled
        - jnp.mean(scaled, axis=-1, keepdims=True)
        - xhat * jnp.mean(scaled * xhat, axis=-1, keepdims=True)
    )


def cdf(values):
    return 0.5 * (1.0 + lax.erf(values * ROOT_HALF))


def gelu_slope(values):
    return cdf(values) + values * DENSITY * jnp.exp(-0.5 * values * values)


def shape_of(*dims):
    return jax.ShapeDtypeStruct(dims, jnp.float32)


def run_whole(kernel, outs, args, flops=1e9, moved=None, scratch=(), anywhere=0):
    moved = moved or sum(a.size * 4 for a in args) + sum(int(functools.reduce(lambda x, y: x * y, o.shape)) * 4 for o in outs)
    fast = len(args) - anywhere
    return pl.pallas_call(
        kernel,
        out_shape=outs,
        in_specs=[pl.BlockSpec(memory_space=pltpu.VMEM)] * fast + [pl.BlockSpec(memory_space=pl.ANY)] * anywhere,
        out_specs=[pl.BlockSpec(memory_space=pltpu.VMEM)] * len(outs),
        scratch_shapes=list(scratch),
        compiler_params=pltpu.CompilerParams(vmem_limit_bytes=VMEM_LIMIT),
        cost_estimate=pl.CostEstimate(flops=int(flops * 3), bytes_accessed=int(moved), transcendentals=0),
    )(*args)


def lane_mask(lanes, width, head):
    return lax.broadcasted_iota(jnp.int32, (1, lanes), 1) // width == head


def spread(values, width):
    lanes = values.shape[1]
    return jnp.concatenate(
        [jnp.where(lane_mask(lanes, width, h), values, 0.0) for h in range(lanes // width)], axis=0
    )


def fold(values, width):
    lanes = values.shape[1]
    rows = values.shape[0] // (lanes // width)
    total = jnp.zeros((rows, lanes), jnp.float32)
    for h in range(lanes // width):
        total = total + jnp.where(lane_mask(lanes, width, h), values[h * rows : (h + 1) * rows], 0.0)
    return total


def attend_group(q, k, v, mask, width):
    count = q.shape[1] // width
    scores = mmt(spread(q, width), k) * (width ** -0.5)
    scores = scores.reshape(count, q.shape[0], k.shape[0])
    scores = jnp.where(mask[None], scores, -1e30)
    weights = jnp.exp(scores - jnp.max(scores, axis=-1, keepdims=True))
    weights = weights / jnp.sum(weights, axis=-1, keepdims=True)
    weights = weights.reshape(count * q.shape[0], k.shape[0])
    return fold(mm(weights, v), width), weights


def attend_group_back(grad, q, k, v, weights, width):
    grads = spread(grad, width)
    dp = mmt(grads, v)
    ds = weights * (dp - jnp.sum(dp * weights, axis=-1, keepdims=True)) * (width ** -0.5)
    return fold(mm(ds, k), width), tmm(ds, spread(q, width)), tmm(weights, grads)


def crop_rows(count, total):
    return lax.broadcasted_iota(jnp.int32, (count, 1), 0) // (total // CROPS)


def crop_lanes(count, total):
    return lax.broadcasted_iota(jnp.int32, (1, count), 1) // (total // CROPS)


def groups_of(ref, start, size, lanes):
    return [slice(start + at, start + at + lanes) for at in range(0, size, lanes)]


def ffn_kernel(state_ref, gain_ref, up_ref, down_ref, normed_ref, pre_ref, act_ref, out_ref):
    @pl.when(pl.program_id(0) == 0)
    def _():
        hat, _ = normalise(state_ref[...])
        normed_ref[...] = hat * gain_ref[...]
        out_ref[...] = jnp.zeros_like(out_ref)

    pre = mm(normed_ref[...], up_ref[...])
    act = pre * cdf(pre)
    pre_ref[...] = pre
    act_ref[...] = act
    out_ref[...] += mm(act, down_ref[...])


def ffn_forward(state, gain, up, down):
    rows, deep = state.shape
    inner = up.shape[1]
    tile = min(256, inner)
    whole = pl.BlockSpec((rows, deep), lambda t: (0, 0))
    part = pl.BlockSpec((rows, tile), lambda t: (0, t))
    return pl.pallas_call(
        ffn_kernel,
        grid=(inner // tile,),
        out_shape=[shape_of(rows, deep), shape_of(rows, inner), shape_of(rows, inner), shape_of(rows, deep)],
        in_specs=[
            whole,
            pl.BlockSpec((1, deep), lambda t: (0, 0)),
            pl.BlockSpec((deep, tile), lambda t: (0, t)),
            pl.BlockSpec((tile, deep), lambda t: (t, 0)),
        ],
        out_specs=[whole, part, part, whole],
        compiler_params=pltpu.CompilerParams(vmem_limit_bytes=VMEM_LIMIT),
        cost_estimate=pl.CostEstimate(flops=12 * rows * deep * inner, bytes_accessed=8 * deep * inner, transcendentals=0),
    )(state, gain[None], up, down)


def residual_back(base_ref, dsum_ref, state_ref, gain_ref, grad_ref, dgain_ref):
    hat, root = normalise(state_ref[...])
    dsum = dsum_ref[...]
    grad_ref[...] = base_ref[...] + norm_back(dsum, hat, root, gain_ref[...])
    dgain_ref[...] = jnp.sum(dsum * hat, axis=0, keepdims=True)


def ffn_back_kernel(
    base_ref, dsum_ref, state_ref, gain_ref, pre_ref, up_ref, down_ref, grad_ref, dgain_ref, dpre_ref, out_ref
):
    @pl.when(pl.program_id(0) == 0)
    def _():
        residual_back(base_ref, dsum_ref, state_ref, gain_ref, grad_ref, dgain_ref)
        out_ref[...] = jnp.zeros_like(out_ref)

    dpre = mmt(grad_ref[...], down_ref[...]) * gelu_slope(pre_ref[...])
    dpre_ref[...] = dpre
    out_ref[...] += mmt(dpre, up_ref[...])


def ffn_backward(base, dsum, state, gain, pre, up, down):
    rows, deep = state.shape
    inner = up.shape[1]
    tile = min(256, inner)
    whole = pl.BlockSpec((rows, deep), lambda t: (0, 0))
    row = pl.BlockSpec((1, deep), lambda t: (0, 0))
    part = pl.BlockSpec((rows, tile), lambda t: (0, t))
    return pl.pallas_call(
        ffn_back_kernel,
        grid=(inner // tile,),
        out_shape=[shape_of(rows, deep), shape_of(1, deep), shape_of(rows, inner), shape_of(rows, deep)],
        in_specs=[
            whole,
            whole,
            whole,
            row,
            part,
            pl.BlockSpec((deep, tile), lambda t: (0, t)),
            pl.BlockSpec((tile, deep), lambda t: (t, 0)),
        ],
        out_specs=[whole, row, part, whole],
        compiler_params=pltpu.CompilerParams(vmem_limit_bytes=VMEM_LIMIT),
        cost_estimate=pl.CostEstimate(flops=12 * rows * deep * inner, bytes_accessed=8 * deep * inner, transcendentals=0),
    )(base, dsum, state, gain[None], pre, up, down)


def self_kernel(width, state_ref, gain_ref, qkv_ref, wout_ref, normed_ref, packed_ref, att_ref, weights_ref, out_ref):
    hat, _ = normalise(state_ref[...])
    normed = hat * gain_ref[...]
    normed_ref[...] = normed
    part = att_ref.shape[1]
    for at in range(3):
        packed_ref[:, at * part : (at + 1) * part] = mm(normed, qkv_ref[:, at * part : (at + 1) * part])
    rows = normed.shape[0]
    mask = crop_rows(rows, rows) == crop_lanes(rows, rows)
    for g in range(part // 128):
        q, k, v = [packed_ref[:, at * part + g * 128 : at * part + (g + 1) * 128] for at in range(3)]
        att, weights = attend_group(q, k, v, mask, width)
        att_ref[:, g * 128 : (g + 1) * 128] = att
        n = weights.shape[0]
        weights_ref[g * n : (g + 1) * n] = weights
    out_ref[...] = mm(att_ref[...], wout_ref[...])


def self_back_kernel(
    width,
    base_ref,
    dsum_ref,
    state_ref,
    gain_ref,
    packed_ref,
    weights_ref,
    qkv_ref,
    wout_ref,
    grad_ref,
    dgain_ref,
    dpacked_ref,
    out_ref,
):
    residual_back(base_ref, dsum_ref, state_ref, gain_ref, grad_ref, dgain_ref)
    part = dpacked_ref.shape[1] // 3
    datt = mmt(grad_ref[...], wout_ref[...])
    count = 128 // width * datt.shape[0]
    for g in range(part // 128):
        q, k, v = [packed_ref[:, at * part + g * 128 : at * part + (g + 1) * 128] for at in range(3)]
        found = attend_group_back(
            datt[:, g * 128 : (g + 1) * 128], q, k, v, weights_ref[g * count : (g + 1) * count], width
        )
        for at in range(3):
            dpacked_ref[:, at * part + g * 128 : at * part + (g + 1) * 128] = found[at]
    out_ref[...] = mmt(dpacked_ref[...], qkv_ref[...])


def read_kernel(width, q_ref, hat_ref, gain_ref, seg_ref, keyval_ref, wout_ref, kv_ref, att_ref, weights_ref, out_ref):
    part = att_ref.shape[1]
    patches = kv_ref.shape[0] // hat_ref.shape[0]
    for z in range(hat_ref.shape[0]):
        kv_ref[z * patches : (z + 1) * patches] = mm(hat_ref[z, :patches] * gain_ref[...], keyval_ref[...])
    rows = q_ref.shape[0]
    mask = crop_rows(rows, rows) == seg_ref[...]
    for g in range(part // 128):
        at = slice(g * 128, (g + 1) * 128)
        att, weights = attend_group(
            q_ref[:, at], kv_ref[:, at], kv_ref[:, part + g * 128 : part + (g + 1) * 128], mask, width
        )
        att_ref[:, at] = att
        n = weights.shape[0]
        weights_ref[g * n : (g + 1) * n] = weights
    out_ref[...] = mm(att_ref[...], wout_ref[...])


def read_back_kernel(
    width,
    base_ref,
    dsum_ref,
    state_ref,
    gain_ref,
    q_ref,
    kv_ref,
    weights_ref,
    wquery_ref,
    keyval_ref,
    wout_ref,
    latents_ref,
    hat_ref,
    int_gain_ref,
    att_ref,
    grad_ref,
    dgain_ref,
    dq_ref,
    dkv_ref,
    dlat_ref,
    dint_ref,
    dgain_lat_ref,
    dgain_int_ref,
    dkeyval_ref,
    dout_ref,
):
    residual_back(base_ref, dsum_ref, state_ref, gain_ref, grad_ref, dgain_ref)
    part = dq_ref.shape[1]
    datt = mmt(grad_ref[...], wout_ref[...])
    count = 128 // width * datt.shape[0]
    for g in range(part // 128):
        at, behind = slice(g * 128, (g + 1) * 128), slice(part + g * 128, part + (g + 1) * 128)
        found = attend_group_back(
            datt[:, at], q_ref[:, at], kv_ref[:, at], kv_ref[:, behind], weights_ref[g * count : (g + 1) * count], width
        )
        dq_ref[:, at], dkv_ref[:, at], dkv_ref[:, behind] = found
    dlat = mmt(dq_ref[...], wquery_ref[...])
    dlat_ref[...] = dlat
    hat, _ = normalise(latents_ref[...])
    dgain_lat_ref[...] = jnp.sum(dlat * hat, axis=0, keepdims=True)
    dint = mmt(dkv_ref[...], keyval_ref[...])
    dint_ref[...] = dint
    patches = dint.shape[0] // hat_ref.shape[0]
    dgain_int = jnp.zeros_like(dgain_int_ref)
    for z in range(hat_ref.shape[0]):
        dgain_int += jnp.sum(dint[z * patches : (z + 1) * patches] * hat_ref[z, :patches], axis=0, keepdims=True)
    dgain_int_ref[...] = dgain_int
    dout_ref[...] = tmm(att_ref[...], grad_ref[...])
    total = jnp.zeros_like(dkeyval_ref)
    for z in range(hat_ref.shape[0]):
        total += tmm(hat_ref[z, :patches] * int_gain_ref[...], dkv_ref[z * patches : (z + 1) * patches])
    dkeyval_ref[...] = total


def write_kernel(
    width,
    state_ref,
    gain_ref,
    hat_ref,
    int_ref,
    cot_ref,
    gains_ref,
    seg_ref,
    place_ref,
    sources,
    normed_ref,
    new_ref,
    dafter_ref,
    dq_ref,
    att_ref,
    y_ref,
    act_ref,
    dpre_ref,
    dkv_ref,
    dgain_ref,
    out_ref,
    dhat_ref,
    wkv,
    wquery,
    wout,
    up,
    down,
    kv,
    q,
    weights,
    dy,
    sems,
):
    targets = [wkv, wquery, wout, up, down]
    if len(sources) == 5:
        for n in range(5):
            pltpu.make_async_copy(sources[n], targets[n], sems.at[n]).start()
    else:
        bring_pieces(sources, targets, sems, place_ref[0])

    def arrived(n):
        pltpu.make_async_copy(targets[n], targets[n], sems.at[n]).wait()

    hat4, _ = normalise(state_ref[...])
    normed = hat4 * gain_ref[...]
    normed_ref[...] = normed
    wide = hat_ref.shape[1]
    patches = hat_ref.shape[0]
    lats = normed.shape[0]
    arrived(1)
    q[...] = mm(hat_ref[...] * gains_ref[0:1], wquery[...].reshape(wide, wide))
    arrived(0)

    def project(t, carry):
        at = pl.ds(pl.multiple_of(t * 256, 256), 256)
        kv[:, at] = mm(normed_ref[...], wkv[:, at])
        return carry

    lax.fori_loop(0, kv.shape[1] // 256, project, 0)
    mask = seg_ref[...] == crop_lanes(lats, lats)
    count = 128 // width * patches

    def forward(g, carry):
        at = pl.ds(pl.multiple_of(g * 128, 128), 128)
        behind = pl.ds(pl.multiple_of(wide + g * 128, 128), 128)
        found, shares = attend_group(q[:, at], kv[:, at], kv[:, behind], mask, width)
        att_ref[:, at] = found
        weights[pl.ds(pl.multiple_of(g * count, count), count)] = shares
        return carry

    lax.fori_loop(0, wide // 128, forward, 0)
    arrived(2)
    after = int_ref[...] + mm(att_ref[...], wout[...].reshape(wide, wide))
    after_hat, after_root = normalise(after)
    y_ref[...] = after_hat * gains_ref[1:2]
    new_ref[...] = after
    dy[...] = jnp.zeros_like(dy)
    arrived(3)
    arrived(4)
    tile = down.shape[1] * down.shape[2]

    def mlp(t, carry):
        at = pl.ds(pl.multiple_of(t * tile, tile), tile)
        up_part = up[:, :, at].reshape(wide, tile)
        down_part = down[t].reshape(tile, wide)
        pre = mm(y_ref[...], up_part)
        share = cdf(pre)
        act = pre * share
        act_ref[:, at] = act
        new_ref[...] += mm(act, down_part)
        slope = share + pre * DENSITY * jnp.exp(-0.5 * pre * pre)
        dpre = mmt(cot_ref[...], down_part) * slope
        dpre_ref[:, at] = dpre
        dy[...] += mmt(dpre, up_part)
        return carry

    lax.fori_loop(0, down.shape[0], mlp, 0)
    dgain_ref[...] = jnp.sum(dy[...] * after_hat, axis=0, keepdims=True)
    dafter_ref[...] = cot_ref[...] + norm_back(dy[...], after_hat, after_root, gains_ref[1:2])
    dy[...] = mmt(dafter_ref[...], wout[...].reshape(wide, wide))

    def backward(g, carry):
        at = pl.ds(pl.multiple_of(g * 128, 128), 128)
        behind = pl.ds(pl.multiple_of(wide + g * 128, 128), 128)
        shares = weights[pl.ds(pl.multiple_of(g * count, count), count)]
        found = attend_group_back(dy[:, at], q[:, at], kv[:, at], kv[:, behind], shares, width)
        dq_ref[:, at], dkv_ref[:, at], dkv_ref[:, behind] = found
        return carry

    lax.fori_loop(0, wide // 128, backward, 0)

    def close(t, carry):
        at = pl.ds(pl.multiple_of(t * 256, 256), 256)
        out_ref[:, at] = mmt(dkv_ref[...], wkv[at, :])
        return carry

    lax.fori_loop(0, out_ref.shape[1] // 256, close, 0)
    dhat_ref[...] = mmt(dq_ref[...], wquery[...].reshape(wide, wide))


def bring_pieces(sources, targets, sems, place):
    wkv, wquery, wout, up, down = targets
    zs, rows, wide = wquery.shape
    ds, _, inner, _ = down.shape
    pack = up.shape[2] // ds
    deep_rows, q_rows = wkv.shape[0] // ds, rows // ds
    lanes = wide // zs
    first = rows + inner * (wide // pack)
    for step in range(ds):
        d = jnp.bitwise_xor(place, step)
        base = (step % 2) * 5
        near = sources[base + min(step // 2, 3)]
        far, shift = (sources[base + 4], first) if step // 2 == 3 else (near, 0)

        def bring(source, target, sem):
            pltpu.make_async_copy(source, target, sems.at[sem]).start()

        at = first - shift
        for z in range(zs):
            for b in range(2):
                bring(
                    far.at[z, at : at + deep_rows, b * lanes : (b + 1) * lanes],
                    wkv.at[pl.ds(pl.multiple_of(d * deep_rows, deep_rows), deep_rows), pl.ds(b * wide + z * lanes, lanes)],
                    0,
                )
        at += deep_rows
        for n, target in ((1, wquery), (2, wout)):
            for b in range(wide // pack):
                bring(
                    far.at[:, at : at + q_rows],
                    target.at[:, pl.ds(pl.multiple_of(d * q_rows, q_rows), q_rows), pl.ds(b * pack, pack)],
                    n,
                )
                at += q_rows
        bring(near.at[:, :rows], up.at[:, :, pl.ds(pl.multiple_of(d * pack, pack), pack)], 3)
        for b in range(wide // pack):
            start = rows + b * inner
            bring(near.at[:, start : start + inner], down.at[d, :, :, pl.ds(b * pack, pack)], 4)


def write_stage(state, gain, hat, interface, cot, gains, seg, place, sources, shapes):
    rows, deep = state.shape
    patches, wide = hat.shape
    hidden = shapes[3][2]
    n = HEADS * patches
    small = shape_of(patches, wide)
    big = shape_of(patches, hidden)
    outs = [
        shape_of(rows, deep), small, small, small, small, small, big, big,
        shape_of(rows, 2 * wide), shape_of(1, wide), shape_of(rows, deep), small,
    ]
    vmem = pl.BlockSpec(memory_space=pltpu.VMEM)
    kernel = functools.partial(write_kernel, wide // HEADS)
    count = len(sources)

    def call(*refs):
        kernel(*refs[:8], refs[8 : 8 + count], *refs[8 + count :])

    return pl.pallas_call(
        call,
        out_shape=outs,
        in_specs=[vmem] * 7 + [pl.BlockSpec(memory_space=pltpu.SMEM)] + [pl.BlockSpec(memory_space=pl.ANY)] * count,
        out_specs=[vmem] * len(outs),
        scratch_shapes=[pltpu.VMEM(shape, jnp.float32) for shape in shapes]
        + [
            pltpu.VMEM((rows, 2 * wide), jnp.float32),
            pltpu.VMEM((patches, wide), jnp.float32),
            pltpu.VMEM((n, rows), jnp.float32),
            pltpu.VMEM((patches, wide), jnp.float32),
            pltpu.SemaphoreType.DMA((5,)),
        ],
        compiler_params=pltpu.CompilerParams(vmem_limit_bytes=VMEM_LIMIT),
        cost_estimate=pl.CostEstimate(flops=20_000_000_000, bytes_accessed=40_000_000, transcendentals=0),
    )(state, gain[None], hat, interface, cot, gains, seg, place, *sources)


def grads_kernel(y_ref, dpre_ref, act_ref, cot_ref, hat_ref, gain_ref, dq_ref, att_ref, dafter_ref, place_ref, mine_ref, other_ref, square):
    core = jnp.bitwise_and(place_ref[0], 1)
    wide = y_ref.shape[1]
    pack = mine_ref.shape[3]
    chips, zs = mine_ref.shape[0], mine_ref.shape[1]
    rows = wide // zs
    inner = pack // zs
    q_rows = rows // (2 * chips)
    square[0] = tmm(hat_ref[...] * gain_ref[...], dq_ref[...])
    square[1] = tmm(att_ref[...], dafter_ref[...])

    def step(j, carry):
        for out_ref, bit in ((mine_ref, core), (other_ref, 1 - core)):
            d = 2 * j + bit
            at = pl.ds(pl.multiple_of(d * pack, pack), pack)
            out_ref[j, :, :rows] = tmm(y_ref[...], dpre_ref[:, at]).reshape(zs, rows, pack)
            start = rows
            ddown = tmm(act_ref[:, at], cot_ref[...])
            for b in range(wide // pack):
                out_ref[j, :, start : start + inner] = ddown[:, b * pack : (b + 1) * pack].reshape(zs, inner, pack)
                start += inner
            for n in range(2):
                for b in range(wide // pack):
                    for z in range(zs):
                        source = pl.ds(pl.multiple_of(z * rows + d * q_rows, q_rows), q_rows)
                        out_ref[j, z, start : start + q_rows] = square[n, source, b * pack : (b + 1) * pack]
                    start += q_rows
        return carry

    lax.fori_loop(0, chips, step, 0)


def interface_grads(y, dpre, act, cot, hat, gain, dq, att, dafter, place, zs, rows):
    patches, wide = y.shape
    pack = dpre.shape[1] // 8
    out = shape_of(4, zs, rows, pack)
    vmem = pl.BlockSpec(memory_space=pltpu.VMEM)
    return pl.pallas_call(
        grads_kernel,
        out_shape=[out, out],
        in_specs=[vmem] * 9 + [pl.BlockSpec(memory_space=pltpu.SMEM)],
        out_specs=[vmem, vmem],
        scratch_shapes=[pltpu.VMEM((2, wide, wide), jnp.float32)],
        compiler_params=pltpu.CompilerParams(vmem_limit_bytes=VMEM_LIMIT),
        cost_estimate=pl.CostEstimate(flops=10_000_000_000, bytes_accessed=20_000_000, transcendentals=0),
    )(y, dpre, act, cot, hat, gain, dq, att, dafter, place)


def outer_kernel(specs, lefts, sums, place_ref, *refs):
    pieces, refs = refs[:10], refs[10:]
    arrays, refs = refs[:lefts], refs[lefts:]
    outs, refs = refs[: len(specs)], refs[len(specs) :]
    if sums:
        sum_ref, refs = refs[0], refs[1:]
    right, held, sems = refs[0], refs[1 : 1 + len(specs)], refs[1 + len(specs)]
    ds, rows, _ = right.shape
    for step in range(ds):
        d = jnp.bitwise_xor(place_ref[0], step)
        base, far = (step % 2) * 5, step // 2
        if far < 3:
            pltpu.make_async_copy(pieces[base + far], right.at[d], sems.at[0]).start()
        else:
            for n in range(2):
                target = right.at[d, n * rows // 2 : (n + 1) * rows // 2]
                pltpu.make_async_copy(pieces[base + 3 + n], target, sems.at[0]).start()
    copies = []
    for n, (which, at, width, _, _) in enumerate(specs):
        copies.append(pltpu.make_async_copy(arrays[which].at[:, at : at + width], held[n], sems.at[n + 1]))
        copies[-1].start()
    pltpu.make_async_copy(right, right, sems.at[0]).wait()
    if sums:
        sum_ref[...] = jnp.sum(right[:, :, sums[0] : sums[0] + sums[1]], axis=0)
    for n, (_, _, width, at, columns) in enumerate(specs):
        copies[n].wait()
        tile = min(256, width)

        def step(t, carry, n=n, at=at, columns=columns, tile=tile):
            here = pl.ds(pl.multiple_of(t * tile, tile), tile)
            values = right[:, :, at : at + columns].reshape(ds * rows, columns)
            outs[n][here, :] = tmm(held[n][:, here], values)
            return carry

        lax.fori_loop(0, width // tile, step, 0)


def outer_products(pieces, place, arrays, specs, sums=()):
    rows, columns = pieces[0].shape
    outs = [shape_of(spec[2], spec[4]) for spec in specs]
    if sums:
        outs.append(shape_of(rows, sums[1]))
    anywhere = pl.BlockSpec(memory_space=pl.ANY)
    total = arrays[0].shape[0]
    return pl.pallas_call(
        functools.partial(outer_kernel, specs, len(arrays), sums),
        out_shape=outs,
        in_specs=[pl.BlockSpec(memory_space=pltpu.SMEM)] + [anywhere] * (len(pieces) + len(arrays)),
        out_specs=[pl.BlockSpec(memory_space=pltpu.VMEM)] * len(outs),
        scratch_shapes=[pltpu.VMEM((total // rows, rows, columns), jnp.float32)]
        + [pltpu.VMEM((total, spec[2]), jnp.float32) for spec in specs]
        + [pltpu.SemaphoreType.DMA((len(specs) + 1,))],
        compiler_params=pltpu.CompilerParams(vmem_limit_bytes=VMEM_LIMIT),
        cost_estimate=pl.CostEstimate(
            flops=sum(6 * total * spec[2] * spec[4] for spec in specs), bytes_accessed=20_000_000, transcendentals=0
        ),
    )(place, *pieces, *arrays)


def local(
    interface,
    latents,
    segment_ids,
    read_gain_lat,
    read_gain_int,
    read_query,
    read_keyval,
    read_out,
    read_gain_mlp,
    read_up,
    read_down,
    layer_gain_att,
    layer_qkv,
    layer_out,
    layer_gain_mlp,
    layer_up,
    layer_down,
    write_gain_int,
    write_query,
    write_gain_lat,
    write_keyval,
    write_out,
    write_gain_mlp,
    write_up,
    write_down,
    interface_cot,
    latents_cot,
):
    zs, ds = lax.axis_size("head"), lax.axis_size("dp")
    me, dd = lax.axis_index("head"), lax.axis_index("dp")
    here = HEADS // zs

    def shift(values, step):
        return lax.ppermute(values, "head", [(i, (i + step) % zs) for i in range(zs)])

    def z_scatter(parts):
        total = lax.dynamic_index_in_dim(parts, me, 0, keepdims=False)
        for step in range(1, zs):
            sent = lax.dynamic_index_in_dim(parts, (me + step) % zs, 0, keepdims=False)
            total = total + shift(sent, step)
        return total

    def z_pieces(parts):
        pieces = [lax.dynamic_index_in_dim(parts, me, 0, keepdims=False)]
        for step in range(1, zs):
            sent = lax.dynamic_index_in_dim(parts, (me + step) % zs, 0, keepdims=False)
            pieces.append(shift(sent, step))
        return pieces

    def z_gather(own):
        out = jnp.zeros((zs,) + own.shape, own.dtype)
        out = lax.dynamic_update_index_in_dim(out, own, me, 0)
        for step in range(1, zs):
            out = lax.dynamic_update_index_in_dim(out, shift(own, step), (me - step) % zs, 0)
        return out

    def tie(*values):
        return lax.optimization_barrier(values)

    def sum_over_head(partial, base=None, release=()):
        rows = partial.shape[0] // zs
        own = z_scatter(partial.reshape(zs, rows, -1))
        if base is not None:
            own = own + lax.dynamic_slice_in_dim(base, me * rows, rows, 0)
        own, *release = tie(own, *release)
        full = z_gather(own).reshape(partial.shape)
        return (full, *release) if release else full

    def cut_up(full, parts):
        out, at = [], 0
        for part in parts:
            out.append(full[:, at : at + part.shape[1]])
            at += part.shape[1]
        return out

    def join(parts):
        return jnp.concatenate(parts, axis=1) if len(parts) > 1 else parts[0]

    def d_gather(parts):
        return lax.all_gather(join(parts), "dp", axis=0, tiled=True)

    direct = ds == 8
    chip, core = dd // 2, dd % 2

    def swap(values, bits):
        return lax.ppermute(values, "dp", [(i, i ^ bits) for i in range(ds)])

    def to_sides(joined):
        return [joined, swap(joined, 2), swap(joined, 4)]

    def to_across(joined, by_x, by_y):
        half = joined.shape[0] // 2
        return [joined, by_x, by_y, swap(by_x[:half], 4), swap(by_y[half:], 2)]

    def to_core(*blocks):
        return [*blocks, *(swap(block, 1) for block in blocks)]

    def pick(values, index, axis):
        return lax.dynamic_index_in_dim(values, index, axis, keepdims=False)

    def scatter_one(mine, got):
        x, rows = chip % 2, mine.shape[1]
        mine = mine.reshape((2, 2) + mine.shape[1:])
        got = got.reshape(mine.shape)
        y = chip // 2
        mh, gh, ml, gl = mine[:, :, : rows // 2], got[:, :, : rows // 2], mine[:, :, rows // 2 :], got[:, :, rows // 2 :]
        high, low = pick(mh, x, 1) + pick(gh, x, 1), pick(ml, y, 0) + pick(gl, y, 0)
        sent_high, sent_low = pick(mh, 1 - x, 1) + pick(gh, 1 - x, 1), pick(ml, 1 - y, 0) + pick(gl, 1 - y, 0)
        return high, low, swap(sent_high, 2), swap(sent_low, 4)

    def scatter_two(high, low, got_high, got_low):
        y, x = chip // 2, chip % 2
        sent_high, sent_low = pick(high, 1 - y, 0) + pick(got_high, 1 - y, 0), pick(low, 1 - x, 0) + pick(got_low, 1 - x, 0)
        high, low = pick(high, y, 0) + pick(got_high, y, 0), pick(low, x, 0) + pick(got_low, x, 0)
        return jnp.concatenate([high + swap(sent_high, 4), low + swap(sent_low, 2)], axis=0)

    def d_scatter(parts):
        parts = parts.reshape((4, 2) + parts.shape[1:])
        return scatter_two(*scatter_one(pick(parts, core, 1), swap(pick(parts, 1 - core, 1), 1)))

    interface, latents, segments = interface[0], latents[0], segment_ids[0]
    interface_cot, latents_cot = interface_cot[0], latents_cot[0]
    layer_gain_att, layer_gain_mlp = layer_gain_att[0], layer_gain_mlp[0]
    layer_out, layer_up, layer_down = layer_out[0], layer_up[0], layer_down[0]
    patches, wide = interface.shape
    count, deep = latents.shape
    qkv = layer_qkv[0].reshape(deep, -1)
    keyval = read_keyval.reshape(wide, -1)
    part = deep // zs
    hidden = write_down.shape[0] * zs

    own_segments = lax.dynamic_slice_in_dim(segments, me * patches, patches, 0)

    lat_hat, lat_root = normalise(latents)
    lat_normed = lat_hat * read_gain_lat
    early_all = d_gather([lat_normed])
    int_hat, int_root = normalise(interface)
    gains = jnp.stack([read_gain_int, write_gain_int, write_gain_mlp])
    gains = jnp.pad(gains, ((0, 5), (0, wide - gains.shape[1])))
    int_pack = z_gather(jnp.concatenate([int_hat, gains], axis=0))
    query = mm(lat_normed, read_query)

    wq_rows, up_cols, kv_rows = wide // zs // ds, hidden // ds, deep // ds
    pack = up_cols
    up_share = write_up.reshape(wide // zs, zs, ds, up_cols // zs)
    up_share = lax.dynamic_index_in_dim(up_share, dd, 2, keepdims=False).reshape(wide // zs, up_cols)
    down_share = lax.dynamic_index_in_dim(write_down.reshape(ds, -1, wide), dd, 0, keepdims=False)
    kv_share = lax.dynamic_slice_in_dim(write_keyval, dd * kv_rows, kv_rows, 0).reshape(kv_rows, -1)
    q_share = lax.dynamic_slice_in_dim(write_query, dd * wq_rows, wq_rows, 0)
    o_share = lax.dynamic_slice_in_dim(write_out, dd * wq_rows, wq_rows, 0)

    def narrow(share):
        return [share[:, at : at + pack] for at in range(0, share.shape[1], pack)]

    def widen(full, at, rows, columns):
        n = columns // pack
        return jnp.concatenate([full[:, :, at + i * rows : at + (i + 1) * rows] for i in range(n)], axis=-1)

    flat = jnp.concatenate(
        [up_share] + narrow(down_share) + narrow(kv_share) + narrow(q_share) + narrow(o_share), axis=0
    )
    query, int_pack, flat, early_all = lax.optimization_barrier((query, int_pack, flat, early_all))
    gains = jnp.transpose(int_pack[:, patches : patches + 3, : wide // zs], (1, 0, 2)).reshape(3, wide)
    gain_read, gain_write, gain_mlp = gains[0], gains[1], gains[2]
    shares = lax.all_gather(flat, "head", axis=0, tiled=False)

    kv0, read_attended, read_weights, part0 = run_whole(
        functools.partial(read_kernel, deep // HEADS),
        [
            shape_of(zs * patches, 2 * part),
            shape_of(count, part),
            shape_of(here * count, zs * patches),
            shape_of(count, deep),
        ],
        (query, int_pack, gain_read[None], segment_ids, keyval, read_out),
        flops=8 * zs * patches * wide * part,
    )

    state1 = sum_over_head(part0, latents)
    normed1, pre1, act1, part1 = ffn_forward(state1, read_gain_mlp, read_up, read_down)
    down_rows = hidden // zs // ds
    middle = wide // zs + down_rows * (wide // pack)
    part1, shares = tie(part1, shares)
    if direct:
        by_x, by_y = swap(shares, 2), swap(shares, 4)
    state2, normed1, act1 = sum_over_head(part1, state1, (normed1, act1))
    read_joined = join([normed1, act1])

    normed2, packed, self_attended, self_weights, part2 = run_whole(
        functools.partial(self_kernel, deep // HEADS),
        [
            shape_of(count, deep),
            shape_of(count, 3 * part),
            shape_of(count, part),
            shape_of(here * count, count),
            shape_of(count, deep),
        ],
        (state2, layer_gain_att[None], qkv, layer_out),
        flops=8 * count * deep * part,
    )
    if direct:
        part2, by_x, by_y = tie(part2, by_x, by_y)
        pieces = [shares, by_x, by_y, swap(by_x[:, :middle], 4), swap(by_y[:, middle:], 2)]
    state3 = sum_over_head(part2, state2)
    normed3, pre3, act3, part3 = ffn_forward(state3, layer_gain_mlp, layer_up, layer_down)

    if direct:
        part3, read_joined, *pieces = tie(part3, read_joined, *pieces)
        pieces = pieces + [swap(piece, 1) for piece in pieces]
    else:
        everything = lax.all_gather(shares, "dp", axis=0, tiled=False)
        full_up = jnp.transpose(everything[:, :, : wide // zs], (1, 2, 0, 3)).reshape(zs, wide // zs, hidden)
        at = wide // zs
        full_down = widen(everything, at, down_rows, wide)
        at += down_rows * (wide // pack)
        full_kv = widen(everything, at, kv_rows, 2 * wide // zs)
        full_kv = jnp.transpose(full_kv.reshape(ds, zs, kv_rows, 2, -1), (0, 2, 3, 1, 4)).reshape(deep, 2 * wide)
        at += kv_rows * (2 * wide // zs // pack)
        full_query = jnp.transpose(widen(everything, at, wq_rows, wide), (1, 0, 2, 3)).reshape(zs, -1, wide)
        at += wq_rows * (wide // pack)
        full_out = jnp.transpose(widen(everything, at, wq_rows, wide), (1, 0, 2, 3)).reshape(zs, -1, wide)
        pieces = [full_kv, full_query, full_out, full_up, full_down]
    read_all = d_gather([read_joined])
    state4, normed2, normed3, act3 = sum_over_head(part3, state3, (normed2, normed3, act3))
    layer_all = d_gather([normed2, normed3, act3])

    (
        normed4, interface_new, dafter, dwrite_q, write_attended, after_normed, act5, dpre5, dkv4, dgain_mlp, part4,
        dwrite_normed,
    ) = write_stage(
        state4,
        write_gain_lat,
        int_hat,
        interface,
        interface_cot,
        jnp.stack([gain_write, gain_mlp]),
        own_segments[:, None],
        dd.astype(jnp.int32)[None],
        pieces,
        [
            (deep, 2 * wide),
            (zs, wide // zs, wide),
            (zs, wide // zs, wide),
            (zs, wide // zs, hidden),
            (ds, zs, down_rows, wide),
        ],
    )
    dsum4, after_normed, dpre5, act5, dwrite_q, write_attended, dafter, dkv4 = sum_over_head(
        part4, None, (after_normed, dpre5, act5, dwrite_q, write_attended, dafter, dkv4)
    )

    place = dd.astype(jnp.int32)[None]
    piece_rows = middle + 2 * wq_rows * (wide // pack)
    if direct:
        grads_mine, grads_other = interface_grads(
            after_normed, dpre5, act5, interface_cot, int_hat, gain_write[None], dwrite_q, write_attended, dafter,
            place, zs, piece_rows,
        )
        dsum4, grads_mine, grads_other = tie(dsum4, grads_mine, grads_other)
        grads_mine = grads_mine.reshape(4, -1, pack)
        grads_got = swap(grads_other.reshape(4, -1, pack), 1)
    else:
        write_normed = int_hat * gain_write
        dup = jnp.transpose(tmm(after_normed, dpre5).reshape(zs, wide // zs, ds, -1), (2, 0, 1, 3))

        def pack_grad(grad, rows):
            grad = grad.reshape(ds, zs, rows, wide)
            return [grad[..., at : at + pack] for at in range(0, wide, pack)]

        ddown = tmm(act5, interface_cot)
        dquery = jnp.transpose(tmm(write_normed, dwrite_q).reshape(zs, ds, wq_rows, wide), (1, 0, 2, 3))
        dout = jnp.transpose(tmm(write_attended, dafter).reshape(zs, ds, wq_rows, wide), (1, 0, 2, 3))
        packed_grads = jnp.concatenate(
            [dup] + pack_grad(ddown, down_rows) + pack_grad(dquery, wq_rows) + pack_grad(dout, wq_rows), axis=2
        )
        grads_mine = lax.psum_scatter(packed_grads, "dp", scatter_dimension=0, tiled=False)

    dint = dafter + norm_back(dwrite_normed, int_hat, int_root, gain_write)

    dkv_parts = jnp.transpose(dkv4.reshape(count, 2, zs, -1), (2, 0, 1, 3)).reshape(zs, count, -1)
    dsum4, dkv_parts = tie(dsum4, dkv_parts)
    dkv_mine = z_scatter(dkv_parts)
    dstate4, dgain4, dpre3, part5 = ffn_backward(
        latents_cot, dsum4, state4, write_gain_lat, pre3, layer_up, layer_down
    )
    if direct:
        part5, grads_mine, grads_got, dkv_mine = tie(part5, grads_mine, grads_got, dkv_mine)
        grads_mine = lax.psum_scatter(
            grads_mine + grads_got,
            "dp",
            scatter_dimension=0,
            axis_index_groups=[[2 * k + c for k in range(ds // 2)] for c in range(2)],
        )
    dsum3, normed4, dkv_mine, released4, dpre3 = sum_over_head(part5, None, (normed4, dkv_mine, dstate4, dpre3))
    write_all = d_gather([normed4, dkv_mine, released4, dpre3])
    dsum3, read_all = tie(dsum3, read_all)
    dstate3, dgain3, dpacked, part6 = run_whole(
        functools.partial(self_back_kernel, deep // HEADS),
        [shape_of(count, deep), shape_of(1, deep), shape_of(count, 3 * part), shape_of(count, deep)],
        (dstate4, dsum3, state3, layer_gain_mlp[None], packed, self_weights, qkv, layer_out),
        flops=8 * count * deep * part,
    )
    dsum2, dpacked = sum_over_head(part6, None, (dpacked,))
    dlayer_out = tmm(self_attended, dstate3)
    dsum2, layer_all = tie(dsum2, layer_all)

    dstate2, dgain2, dpre1, part7 = ffn_backward(
        dstate3, dsum2, state2, layer_gain_att, pre1, read_up, read_down
    )
    dsum1, released2, dpre1 = sum_over_head(part7, None, (dstate2, dpre1))
    both_all = d_gather([dpacked, released2, dpre1])
    dsum1, grads_mine = tie(dsum1, grads_mine)
    grads_mine = z_scatter(grads_mine.reshape(zs, -1, pack))
    dstate1, dgain1, dquery0, dread_kv, dlat_part, dint_part, dgain_lat, dgain_int, dkeyval, dread_out = run_whole(
        functools.partial(read_back_kernel, deep // HEADS),
        [
            shape_of(count, deep),
            shape_of(1, deep),
            shape_of(count, part),
            shape_of(zs * patches, 2 * part),
            shape_of(count, deep),
            shape_of(zs * patches, wide),
            shape_of(1, deep),
            shape_of(1, wide),
            shape_of(wide, 2 * part),
            shape_of(part, deep),
        ],
        (dstate2, dsum1, state1, read_gain_mlp[None], query, kv0, read_weights, read_query, keyval, read_out, latents, int_pack,
         gain_read[None], read_attended),
        flops=1e6,
        moved=1e6,
    )

    first = (me == 0).astype(jnp.float32)
    small = jnp.concatenate(
        [dgain_lat[0]]
        + [g[0] * first for g in (dgain1, dgain2, dgain3, dgain4)]
        + [dgain_int[0], jnp.sum(dwrite_normed * int_hat, axis=0), dgain_mlp[0]]
    )
    dlat_part, dstate1, grads_mine, small = tie(dlat_part, dstate1, grads_mine, small)
    lanes = small.size // count
    small = jnp.sum(z_gather(small.reshape(count, lanes)), axis=0)
    fill = jnp.pad(small, ((0, 0), (0, -lanes % 128)))
    late = [join([dquery0, fill])]

    half = z_scatter(dlat_part.reshape(zs, count // zs, deep))
    write_all = tie(write_all, dgain_int)[0]
    normed4_all, dkv_all, dstate4_all, dpre3_all = cut_up(write_all, [normed4, dkv_mine, dstate4, dpre3])
    normed2_all, normed3_all, act3_all = cut_up(layer_all, [normed2, normed3, act3])
    grad_layer_up = tmm(normed3_all, dpre3_all)
    if direct:
        late = to_sides(*late)
        dkeyval = [dkeyval] + [
            grad.reshape(ds, -1, deep)[:, :, at : at + 2 * part].reshape(-1, 2 * part)
            for grad in (dlayer_out, dread_out)
            for at in range(0, deep, 2 * part)
        ]
        dkeyval = jnp.concatenate([grad.reshape(ds, -1, 2 * part) for grad in dkeyval], axis=1)
        dkeyval = dkeyval.reshape(4, 2, -1, 2 * part)
        pair = [pick(dkeyval, core, 1), swap(pick(dkeyval, 1 - core, 1), 1)]
        half, dint_part, grad_layer_up, act3_all, normed4_all, *held = tie(
            half, dint_part, grad_layer_up, act3_all, normed4_all, *late, *pair
        )
        late, pair = to_across(*held[:3]), scatter_one(*held[3:])
    dint_own, *dint_got = z_pieces(dint_part.reshape(zs, patches, wide))
    near, middle_got, far = dint_got[0], dint_got[1:-1], dint_got[-1]
    dlat = z_gather(half).reshape(count, deep)
    grad_layer_down, grad_write_keyval = tmm(act3_all, dstate4_all), tmm(normed4_all, dkv_all)
    if direct:
        grad_layer_down, both_all, near, *held = tie(grad_layer_down, both_all, near, *late, *pair)
        late, dkeyval = to_core(*held[:5]), scatter_two(*held[5:])
    dpacked_all, dstate2_all, dpre1_all = cut_up(both_all, [dpacked, dstate2, dpre1])
    normed1_all, act1_all = cut_up(read_all, [normed1, act1])
    grad_layer_qkv, grad_read_up = tmm(normed2_all, dpacked_all), tmm(normed1_all, dpre1_all)
    if direct:
        dkeyval, grad_layer_qkv, dstate2_all, far, *late = tie(dkeyval, grad_layer_qkv, dstate2_all, far, *late)
    grad_read_down = tmm(act1_all, dstate2_all)
    if direct:
        dlat, grad_write_keyval, grad_read_up, grad_read_down, *middle_got = tie(
            dlat, grad_write_keyval, grad_read_up, grad_read_down, *middle_got
        )
        flat = jnp.concatenate([grads_mine] + [dkeyval[:, at : at + pack] for at in range(0, 2 * part, pack)], axis=0)
        grads_all = lax.all_gather(flat, "dp", axis=0, tiled=False)
        grad_read_query, small = outer_products(
            late, place, [early_all], [(0, 0, deep, 0, part)], (part, fill.shape[1])
        )
        small = small[:, :lanes]
        sums = widen(grads_all[:, None], piece_rows, dkeyval.shape[0], 2 * part)[:, 0]
        at, few = read_keyval.shape[0] // ds, part // ds
        grad_read_keyval = sums[:, :at]
        found = []
        for _ in range(2):
            blocks = [sums[:, at + n * few : at + (n + 1) * few] for n in range(deep // (2 * part))]
            found.append(jnp.concatenate(blocks, axis=-1).reshape(part, deep))
            at += few * len(blocks)
        grad_layer_out, grad_read_out = found
    else:
        grads_all = lax.all_gather(grads_mine, "dp", axis=0, tiled=False)
        grad_read_keyval, grad_layer_out, grad_read_out = lax.psum((dkeyval, dlayer_out, dread_out), "dp")
        dquery0_all, small = cut_up(d_gather(late), [dquery0, fill])
        grad_read_query = tmm(early_all, dquery0_all)
        small = jnp.sum(small.reshape(ds, count, -1)[:, :, :lanes], axis=0)
    latents_grad = dstate1 + norm_back(dlat, lat_hat, lat_root, read_gain_lat)
    dint_normed = dint_own + near + far
    for piece in middle_got:
        dint_normed = dint_normed + piece
    interface_grad = dint + norm_back(dint_normed, int_hat, int_root, gain_read)
    small = small.reshape(-1)
    lat_gains = small[: 5 * deep].reshape(5, deep)
    int_gains = small[5 * deep :].reshape(3, zs, wide // zs)
    int_gains = lax.dynamic_index_in_dim(int_gains, me, 1, keepdims=False)

    full = grads_all[:, None]
    grad_write_up = grads_all[:, : wide // zs].reshape(ds, wide // zs, zs, up_cols // zs)
    grad_write_up = jnp.transpose(grad_write_up, (1, 2, 0, 3)).reshape(write_up.shape)
    at = wide // zs
    grad_write_down = widen(full, at, down_rows, wide).reshape(write_down.shape)
    at += down_rows * (wide // pack)
    grad_write_query = widen(full, at, wq_rows, wide).reshape(write_query.shape)
    at += wq_rows * (wide // pack)
    grad_write_out = widen(full, at, wq_rows, wide).reshape(write_out.shape)

    return (
        interface_new[None],
        state4[None],
        interface_grad[None],
        latents_grad[None],
        lat_gains[0],
        int_gains[0],
        grad_read_query,
        grad_read_keyval.reshape(read_keyval.shape),
        grad_read_out,
        lat_gains[1],
        grad_read_up,
        grad_read_down,
        lat_gains[2][None],
        grad_layer_qkv.reshape(layer_qkv.shape),
        grad_layer_out[None],
        lat_gains[3][None],
        grad_layer_up[None],
        grad_layer_down[None],
        int_gains[1],
        grad_write_query,
        lat_gains[4],
        grad_write_keyval.reshape(write_keyval.shape),
        grad_write_out,
        int_gains[2],
        grad_write_up,
        grad_write_down,
    )


def solution(mesh):
    rows, both = P("dp", "head", None), P("dp", None, None)
    weights = (
        P(),
        P("head"),
        P(None, "head"),
        P(None, None, "head"),
        P("head", None),
        P(),
        P(None, "head"),
        P("head", None),
        P(),
        P(None, None, None, "head"),
        P(None, "head", None),
        P(),
        P(None, None, "head"),
        P(None, "head", None),
        P("head"),
        P("head", None),
        P(),
        P(None, None, "head"),
        P("head", None),
        P("head"),
        P("head", None),
        P("head", None),
    )
    in_specs = (rows, both, P("dp", None)) + weights + (rows, both)
    out_specs = (rows, both, rows, both) + weights
    return jax.shard_map(local, mesh=mesh, in_specs=in_specs, out_specs=out_specs, check_vma=False)
```

```python
import functools

import jax
import jax.numpy as jnp
from jax import lax
from jax.experimental import pallas as pl
from jax.experimental.pallas import tpu as pltpu
from jax.sharding import PartitionSpec as P

HEADS = 16
CROPS = 4
EPSILON = 1e-05
PRECISE = lax.Precision.HIGH
ROOT_HALF = 0.7071067811865476
DENSITY = 0.3989422804014327
VMEM_LIMIT = 56 * 1024 * 1024


def mm(left, right):
    return lax.dot_general(left, right, (((1,), (0,)), ((), ())), precision=PRECISE)


def mmt(left, right):
    return lax.dot_general(left, right, (((1,), (1,)), ((), ())), precision=PRECISE)


def tmm(left, right):
    return lax.dot_general(left, right, (((0,), (0,)), ((), ())), precision=PRECISE)


def normalise(values):
    centred = values - jnp.mean(values, axis=-1, keepdims=True)
    root = lax.rsqrt(jnp.mean(centred * centred, axis=-1, keepdims=True) + EPSILON)
    return centred * root, root


def norm_back(grad, xhat, root, gain):
    scaled = grad * gain
    return root * (
        scaled
        - jnp.mean(scaled, axis=-1, keepdims=True)
        - xhat * jnp.mean(scaled * xhat, axis=-1, keepdims=True)
    )


def cdf(values):
    return 0.5 * (1.0 + lax.erf(values * ROOT_HALF))


def gelu_slope(values):
    return cdf(values) + values * DENSITY * jnp.exp(-0.5 * values * values)


def shape_of(*dims):
    return jax.ShapeDtypeStruct(dims, jnp.float32)


def run_whole(kernel, outs, args, flops=1e9, moved=None, scratch=(), anywhere=0):
    moved = moved or sum(a.size * 4 for a in args) + sum(int(functools.reduce(lambda x, y: x * y, o.shape)) * 4 for o in outs)
    fast = len(args) - anywhere
    return pl.pallas_call(
        kernel,
        out_shape=outs,
        in_specs=[pl.BlockSpec(memory_space=pltpu.VMEM)] * fast + [pl.BlockSpec(memory_space=pl.ANY)] * anywhere,
        out_specs=[pl.BlockSpec(memory_space=pltpu.VMEM)] * len(outs),
        scratch_shapes=list(scratch),
        compiler_params=pltpu.CompilerParams(vmem_limit_bytes=VMEM_LIMIT),
        cost_estimate=pl.CostEstimate(flops=int(flops * 3), bytes_accessed=int(moved), transcendentals=0),
    )(*args)


def lane_mask(lanes, width, head):
    return lax.broadcasted_iota(jnp.int32, (1, lanes), 1) // width == head


def spread(values, width):
    lanes = values.shape[1]
    return jnp.concatenate(
        [jnp.where(lane_mask(lanes, width, h), values, 0.0) for h in range(lanes // width)], axis=0
    )


def fold(values, width):
    lanes = values.shape[1]
    rows = values.shape[0] // (lanes // width)
    total = jnp.zeros((rows, lanes), jnp.float32)
    for h in range(lanes // width):
        total = total + jnp.where(lane_mask(lanes, width, h), values[h * rows : (h + 1) * rows], 0.0)
    return total


def attend_group(q, k, v, mask, width):
    count = q.shape[1] // width
    scores = mmt(spread(q, width), k) * (width ** -0.5)
    scores = scores.reshape(count, q.shape[0], k.shape[0])
    scores = jnp.where(mask[None], scores, -1e30)
    weights = jnp.exp(scores - jnp.max(scores, axis=-1, keepdims=True))
    weights = weights / jnp.sum(weights, axis=-1, keepdims=True)
    weights = weights.reshape(count * q.shape[0], k.shape[0])
    return fold(mm(weights, v), width), weights


def attend_group_back(grad, q, k, v, weights, width):
    grads = spread(grad, width)
    dp = mmt(grads, v)
    ds = weights * (dp - jnp.sum(dp * weights, axis=-1, keepdims=True)) * (width ** -0.5)
    return fold(mm(ds, k), width), tmm(ds, spread(q, width)), tmm(weights, grads)


def crop_rows(count, total):
    return lax.broadcasted_iota(jnp.int32, (count, 1), 0) // (total // CROPS)


def crop_lanes(count, total):
    return lax.broadcasted_iota(jnp.int32, (1, count), 1) // (total // CROPS)


def groups_of(ref, start, size, lanes):
    return [slice(start + at, start + at + lanes) for at in range(0, size, lanes)]


def ffn_kernel(state_ref, gain_ref, up_ref, down_ref, normed_ref, pre_ref, act_ref, out_ref):
    @pl.when(pl.program_id(0) == 0)
    def _():
        hat, _ = normalise(state_ref[...])
        normed_ref[...] = hat * gain_ref[...]
        out_ref[...] = jnp.zeros_like(out_ref)

    pre = mm(normed_ref[...], up_ref[...])
    act = pre * cdf(pre)
    pre_ref[...] = pre
    act_ref[...] = act
    out_ref[...] += mm(act, down_ref[...])


def ffn_forward(state, gain, up, down):
    rows, deep = state.shape
    inner = up.shape[1]
    tile = min(256, inner)
    whole = pl.BlockSpec((rows, deep), lambda t: (0, 0))
    part = pl.BlockSpec((rows, tile), lambda t: (0, t))
    return pl.pallas_call(
        ffn_kernel,
        grid=(inner // tile,),
        out_shape=[shape_of(rows, deep), shape_of(rows, inner), shape_of(rows, inner), shape_of(rows, deep)],
        in_specs=[
            whole,
            pl.BlockSpec((1, deep), lambda t: (0, 0)),
            pl.BlockSpec((deep, tile), lambda t: (0, t)),
            pl.BlockSpec((tile, deep), lambda t: (t, 0)),
        ],
        out_specs=[whole, part, part, whole],
        compiler_params=pltpu.CompilerParams(vmem_limit_bytes=VMEM_LIMIT),
        cost_estimate=pl.CostEstimate(flops=12 * rows * deep * inner, bytes_accessed=8 * deep * inner, transcendentals=0),
    )(state, gain[None], up, down)


def residual_back(base_ref, dsum_ref, state_ref, gain_ref, grad_ref, dgain_ref):
    hat, root = normalise(state_ref[...])
    dsum = dsum_ref[...]
    grad_ref[...] = base_ref[...] + norm_back(dsum, hat, root, gain_ref[...])
    dgain_ref[...] = jnp.sum(dsum * hat, axis=0, keepdims=True)


def ffn_back_kernel(
    base_ref, dsum_ref, state_ref, gain_ref, pre_ref, up_ref, down_ref, grad_ref, dgain_ref, dpre_ref, out_ref
):
    @pl.when(pl.program_id(0) == 0)
    def _():
        residual_back(base_ref, dsum_ref, state_ref, gain_ref, grad_ref, dgain_ref)
        out_ref[...] = jnp.zeros_like(out_ref)

    dpre = mmt(grad_ref[...], down_ref[...]) * gelu_slope(pre_ref[...])
    dpre_ref[...] = dpre
    out_ref[...] += mmt(dpre, up_ref[...])


def ffn_backward(base, dsum, state, gain, pre, up, down):
    rows, deep = state.shape
    inner = up.shape[1]
    tile = min(256, inner)
    whole = pl.BlockSpec((rows, deep), lambda t: (0, 0))
    row = pl.BlockSpec((1, deep), lambda t: (0, 0))
    part = pl.BlockSpec((rows, tile), lambda t: (0, t))
    return pl.pallas_call(
        ffn_back_kernel,
        grid=(inner // tile,),
        out_shape=[shape_of(rows, deep), shape_of(1, deep), shape_of(rows, inner), shape_of(rows, deep)],
        in_specs=[
            whole,
            whole,
            whole,
            row,
            part,
            pl.BlockSpec((deep, tile), lambda t: (0, t)),
            pl.BlockSpec((tile, deep), lambda t: (t, 0)),
        ],
        out_specs=[whole, row, part, whole],
        compiler_params=pltpu.CompilerParams(vmem_limit_bytes=VMEM_LIMIT),
        cost_estimate=pl.CostEstimate(flops=12 * rows * deep * inner, bytes_accessed=8 * deep * inner, transcendentals=0),
    )(base, dsum, state, gain[None], pre, up, down)


def self_kernel(width, state_ref, gain_ref, qkv_ref, wout_ref, normed_ref, packed_ref, att_ref, weights_ref, out_ref):
    hat, _ = normalise(state_ref[...])
    normed = hat * gain_ref[...]
    normed_ref[...] = normed
    part = att_ref.shape[1]
    for at in range(3):
        packed_ref[:, at * part : (at + 1) * part] = mm(normed, qkv_ref[:, at * part : (at + 1) * part])
    rows = normed.shape[0]
    mask = crop_rows(rows, rows) == crop_lanes(rows, rows)
    for g in range(part // 128):
        q, k, v = [packed_ref[:, at * part + g * 128 : at * part + (g + 1) * 128] for at in range(3)]
        att, weights = attend_group(q, k, v, mask, width)
        att_ref[:, g * 128 : (g + 1) * 128] = att
        n = weights.shape[0]
        weights_ref[g * n : (g + 1) * n] = weights
    out_ref[...] = mm(att_ref[...], wout_ref[...])


def self_back_kernel(
    width,
    base_ref,
    dsum_ref,
    state_ref,
    gain_ref,
    packed_ref,
    weights_ref,
    qkv_ref,
    wout_ref,
    grad_ref,
    dgain_ref,
    dpacked_ref,
    out_ref,
):
    residual_back(base_ref, dsum_ref, state_ref, gain_ref, grad_ref, dgain_ref)
    part = dpacked_ref.shape[1] // 3
    datt = mmt(grad_ref[...], wout_ref[...])
    count = 128 // width * datt.shape[0]
    for g in range(part // 128):
        q, k, v = [packed_ref[:, at * part + g * 128 : at * part + (g + 1) * 128] for at in range(3)]
        found = attend_group_back(
            datt[:, g * 128 : (g + 1) * 128], q, k, v, weights_ref[g * count : (g + 1) * count], width
        )
        for at in range(3):
            dpacked_ref[:, at * part + g * 128 : at * part + (g + 1) * 128] = found[at]
    out_ref[...] = mmt(dpacked_ref[...], qkv_ref[...])


def read_kernel(width, q_ref, hat_ref, gain_ref, seg_ref, keyval_ref, wout_ref, kv_ref, att_ref, weights_ref, out_ref):
    part = att_ref.shape[1]
    patches = kv_ref.shape[0] // hat_ref.shape[0]
    for z in range(hat_ref.shape[0]):
        kv_ref[z * patches : (z + 1) * patches] = mm(hat_ref[z, :patches] * gain_ref[...], keyval_ref[...])
    rows = q_ref.shape[0]
    mask = crop_rows(rows, rows) == seg_ref[...]
    for g in range(part // 128):
        at = slice(g * 128, (g + 1) * 128)
        att, weights = attend_group(
            q_ref[:, at], kv_ref[:, at], kv_ref[:, part + g * 128 : part + (g + 1) * 128], mask, width
        )
        att_ref[:, at] = att
        n = weights.shape[0]
        weights_ref[g * n : (g + 1) * n] = weights
    out_ref[...] = mm(att_ref[...], wout_ref[...])


def read_back_kernel(
    width,
    base_ref,
    dsum_ref,
    state_ref,
    gain_ref,
    q_ref,
    kv_ref,
    weights_ref,
    wquery_ref,
    keyval_ref,
    wout_ref,
    latents_ref,
    hat_ref,
    int_gain_ref,
    att_ref,
    grad_ref,
    dgain_ref,
    dq_ref,
    dkv_ref,
    dlat_ref,
    dint_ref,
    dgain_lat_ref,
    dgain_int_ref,
    dkeyval_ref,
    dout_ref,
):
    residual_back(base_ref, dsum_ref, state_ref, gain_ref, grad_ref, dgain_ref)
    part = dq_ref.shape[1]
    datt = mmt(grad_ref[...], wout_ref[...])
    count = 128 // width * datt.shape[0]
    for g in range(part // 128):
        at, behind = slice(g * 128, (g + 1) * 128), slice(part + g * 128, part + (g + 1) * 128)
        found = attend_group_back(
            datt[:, at], q_ref[:, at], kv_ref[:, at], kv_ref[:, behind], weights_ref[g * count : (g + 1) * count], width
        )
        dq_ref[:, at], dkv_ref[:, at], dkv_ref[:, behind] = found
    dlat = mmt(dq_ref[...], wquery_ref[...])
    dlat_ref[...] = dlat
    hat, _ = normalise(latents_ref[...])
    dgain_lat_ref[...] = jnp.sum(dlat * hat, axis=0, keepdims=True)
    dint = mmt(dkv_ref[...], keyval_ref[...])
    dint_ref[...] = dint
    patches = dint.shape[0] // hat_ref.shape[0]
    dgain_int = jnp.zeros_like(dgain_int_ref)
    for z in range(hat_ref.shape[0]):
        dgain_int += jnp.sum(dint[z * patches : (z + 1) * patches] * hat_ref[z, :patches], axis=0, keepdims=True)
    dgain_int_ref[...] = dgain_int
    dout_ref[...] = tmm(att_ref[...], grad_ref[...])
    total = jnp.zeros_like(dkeyval_ref)
    for z in range(hat_ref.shape[0]):
        total += tmm(hat_ref[z, :patches] * int_gain_ref[...], dkv_ref[z * patches : (z + 1) * patches])
    dkeyval_ref[...] = total


def write_kernel(
    width,
    state_ref,
    gain_ref,
    hat_ref,
    int_ref,
    cot_ref,
    gains_ref,
    seg_ref,
    place_ref,
    sources,
    normed_ref,
    new_ref,
    dafter_ref,
    dq_ref,
    att_ref,
    y_ref,
    act_ref,
    dpre_ref,
    dkv_ref,
    dgain_ref,
    out_ref,
    dhat_ref,
    wkv,
    wquery,
    wout,
    up,
    down,
    kv,
    q,
    weights,
    dy,
    sems,
):
    targets = [wkv, wquery, wout, up, down]
    if len(sources) == 5:
        for n in range(5):
            pltpu.make_async_copy(sources[n], targets[n], sems.at[n]).start()
    else:
        bring_pieces(sources, targets, sems, place_ref[0])

    def arrived(n):
        pltpu.make_async_copy(targets[n], targets[n], sems.at[n]).wait()

    hat4, _ = normalise(state_ref[...])
    normed = hat4 * gain_ref[...]
    normed_ref[...] = normed
    wide = hat_ref.shape[1]
    patches = hat_ref.shape[0]
    lats = normed.shape[0]
    arrived(1)
    q[...] = mm(hat_ref[...] * gains_ref[0:1], wquery[...].reshape(wide, wide))
    arrived(0)

    def project(t, carry):
        at = pl.ds(pl.multiple_of(t * 256, 256), 256)
        kv[:, at] = mm(normed_ref[...], wkv[:, at])
        return carry

    lax.fori_loop(0, kv.shape[1] // 256, project, 0)
    mask = seg_ref[...] == crop_lanes(lats, lats)
    count = 128 // width * patches

    def forward(g, carry):
        at = pl.ds(pl.multiple_of(g * 128, 128), 128)
        behind = pl.ds(pl.multiple_of(wide + g * 128, 128), 128)
        found, shares = attend_group(q[:, at], kv[:, at], kv[:, behind], mask, width)
        att_ref[:, at] = found
        weights[pl.ds(pl.multiple_of(g * count, count), count)] = shares
        return carry

    lax.fori_loop(0, wide // 128, forward, 0)
    arrived(2)
    after = int_ref[...] + mm(att_ref[...], wout[...].reshape(wide, wide))
    after_hat, after_root = normalise(after)
    y_ref[...] = after_hat * gains_ref[1:2]
    new_ref[...] = after
    dy[...] = jnp.zeros_like(dy)
    arrived(3)
    arrived(4)
    tile = down.shape[1] * down.shape[2]

    def mlp(t, carry):
        at = pl.ds(pl.multiple_of(t * tile, tile), tile)
        up_part = up[:, :, at].reshape(wide, tile)
        down_part = down[t].reshape(tile, wide)
        pre = mm(y_ref[...], up_part)
        share = cdf(pre)
        act = pre * share
        act_ref[:, at] = act
        new_ref[...] += mm(act, down_part)
        slope = share + pre * DENSITY * jnp.exp(-0.5 * pre * pre)
        dpre = mmt(cot_ref[...], down_part) * slope
        dpre_ref[:, at] = dpre
        dy[...] += mmt(dpre, up_part)
        return carry

    lax.fori_loop(0, down.shape[0], mlp, 0)
    dgain_ref[...] = jnp.sum(dy[...] * after_hat, axis=0, keepdims=True)
    dafter_ref[...] = cot_ref[...] + norm_back(dy[...], after_hat, after_root, gains_ref[1:2])
    dy[...] = mmt(dafter_ref[...], wout[...].reshape(wide, wide))

    def backward(g, carry):
        at = pl.ds(pl.multiple_of(g * 128, 128), 128)
        behind = pl.ds(pl.multiple_of(wide + g * 128, 128), 128)
        shares = weights[pl.ds(pl.multiple_of(g * count, count), count)]
        found = attend_group_back(dy[:, at], q[:, at], kv[:, at], kv[:, behind], shares, width)
        dq_ref[:, at], dkv_ref[:, at], dkv_ref[:, behind] = found
        return carry

    lax.fori_loop(0, wide // 128, backward, 0)

    def close(t, carry):
        at = pl.ds(pl.multiple_of(t * 256, 256), 256)
        out_ref[:, at] = mmt(dkv_ref[...], wkv[at, :])
        return carry

    lax.fori_loop(0, out_ref.shape[1] // 256, close, 0)
    dhat_ref[...] = mmt(dq_ref[...], wquery[...].reshape(wide, wide))


def bring_pieces(sources, targets, sems, place):
    wkv, wquery, wout, up, down = targets
    zs, rows, wide = wquery.shape
    ds, _, inner, _ = down.shape
    pack = up.shape[2] // ds
    deep_rows, q_rows = wkv.shape[0] // ds, rows // ds
    lanes = wide // zs
    first = rows + inner * (wide // pack)
    for step in range(ds):
        d = jnp.bitwise_xor(place, step)
        base = (step % 2) * 5
        near = sources[base + min(step // 2, 3)]
        far, shift = (sources[base + 4], first) if step // 2 == 3 else (near, 0)

        def bring(source, target, sem):
            pltpu.make_async_copy(source, target, sems.at[sem]).start()

        at = first - shift
        for z in range(zs):
            for b in range(2):
                bring(
                    far.at[z, at : at + deep_rows, b * lanes : (b + 1) * lanes],
                    wkv.at[pl.ds(pl.multiple_of(d * deep_rows, deep_rows), deep_rows), pl.ds(b * wide + z * lanes, lanes)],
                    0,
                )
        at += deep_rows
        for n, target in ((1, wquery), (2, wout)):
            for b in range(wide // pack):
                bring(
                    far.at[:, at : at + q_rows],
                    target.at[:, pl.ds(pl.multiple_of(d * q_rows, q_rows), q_rows), pl.ds(b * pack, pack)],
                    n,
                )
                at += q_rows
        bring(near.at[:, :rows], up.at[:, :, pl.ds(pl.multiple_of(d * pack, pack), pack)], 3)
        for b in range(wide // pack):
            start = rows + b * inner
            bring(near.at[:, start : start + inner], down.at[d, :, :, pl.ds(b * pack, pack)], 4)


def write_stage(state, gain, hat, interface, cot, gains, seg, place, sources, shapes):
    rows, deep = state.shape
    patches, wide = hat.shape
    hidden = shapes[3][2]
    n = HEADS * patches
    small = shape_of(patches, wide)
    big = shape_of(patches, hidden)
    outs = [
        shape_of(rows, deep), small, small, small, small, small, big, big,
        shape_of(rows, 2 * wide), shape_of(1, wide), shape_of(rows, deep), small,
    ]
    vmem = pl.BlockSpec(memory_space=pltpu.VMEM)
    kernel = functools.partial(write_kernel, wide // HEADS)
    count = len(sources)

    def call(*refs):
        kernel(*refs[:8], refs[8 : 8 + count], *refs[8 + count :])

    return pl.pallas_call(
        call,
        out_shape=outs,
        in_specs=[vmem] * 7 + [pl.BlockSpec(memory_space=pltpu.SMEM)] + [pl.BlockSpec(memory_space=pl.ANY)] * count,
        out_specs=[vmem] * len(outs),
        scratch_shapes=[pltpu.VMEM(shape, jnp.float32) for shape in shapes]
        + [
            pltpu.VMEM((rows, 2 * wide), jnp.float32),
            pltpu.VMEM((patches, wide), jnp.float32),
            pltpu.VMEM((n, rows), jnp.float32),
            pltpu.VMEM((patches, wide), jnp.float32),
            pltpu.SemaphoreType.DMA((5,)),
        ],
        compiler_params=pltpu.CompilerParams(vmem_limit_bytes=VMEM_LIMIT),
        cost_estimate=pl.CostEstimate(flops=20_000_000_000, bytes_accessed=40_000_000, transcendentals=0),
    )(state, gain[None], hat, interface, cot, gains, seg, place, *sources)


def grads_kernel(y_ref, dpre_ref, act_ref, cot_ref, hat_ref, gain_ref, dq_ref, att_ref, dafter_ref, place_ref, mine_ref, other_ref, square):
    core = jnp.bitwise_and(place_ref[0], 1)
    wide = y_ref.shape[1]
    pack = mine_ref.shape[3]
    chips, zs = mine_ref.shape[0], mine_ref.shape[1]
    rows = wide // zs
    inner = pack // zs
    q_rows = rows // (2 * chips)
    square[0] = tmm(hat_ref[...] * gain_ref[...], dq_ref[...])
    square[1] = tmm(att_ref[...], dafter_ref[...])

    def step(j, carry):
        for out_ref, bit in ((mine_ref, core), (other_ref, 1 - core)):
            d = 2 * j + bit
            at = pl.ds(pl.multiple_of(d * pack, pack), pack)
            out_ref[j, :, :rows] = tmm(y_ref[...], dpre_ref[:, at]).reshape(zs, rows, pack)
            start = rows
            ddown = tmm(act_ref[:, at], cot_ref[...])
            for b in range(wide // pack):
                out_ref[j, :, start : start + inner] = ddown[:, b * pack : (b + 1) * pack].reshape(zs, inner, pack)
                start += inner
            for n in range(2):
                for b in range(wide // pack):
                    for z in range(zs):
                        source = pl.ds(pl.multiple_of(z * rows + d * q_rows, q_rows), q_rows)
                        out_ref[j, z, start : start + q_rows] = square[n, source, b * pack : (b + 1) * pack]
                    start += q_rows
        return carry

    lax.fori_loop(0, chips, step, 0)


def interface_grads(y, dpre, act, cot, hat, gain, dq, att, dafter, place, zs, rows):
    patches, wide = y.shape
    pack = dpre.shape[1] // 8
    out = shape_of(4, zs, rows, pack)
    vmem = pl.BlockSpec(memory_space=pltpu.VMEM)
    return pl.pallas_call(
        grads_kernel,
        out_shape=[out, out],
        in_specs=[vmem] * 9 + [pl.BlockSpec(memory_space=pltpu.SMEM)],
        out_specs=[vmem, vmem],
        scratch_shapes=[pltpu.VMEM((2, wide, wide), jnp.float32)],
        compiler_params=pltpu.CompilerParams(vmem_limit_bytes=VMEM_LIMIT),
        cost_estimate=pl.CostEstimate(flops=10_000_000_000, bytes_accessed=20_000_000, transcendentals=0),
    )(y, dpre, act, cot, hat, gain, dq, att, dafter, place)


def outer_kernel(specs, lefts, sums, place_ref, *refs):
    pieces, refs = refs[:10], refs[10:]
    arrays, refs = refs[:lefts], refs[lefts:]
    outs, refs = refs[: len(specs)], refs[len(specs) :]
    if sums:
        sum_ref, refs = refs[0], refs[1:]
    right, held, sems = refs[0], refs[1 : 1 + len(specs)], refs[1 + len(specs)]
    ds, rows, _ = right.shape
    for step in range(ds):
        d = jnp.bitwise_xor(place_ref[0], step)
        base, far = (step % 2) * 5, step // 2
        if far < 3:
            pltpu.make_async_copy(pieces[base + far], right.at[d], sems.at[0]).start()
        else:
            for n in range(2):
                target = right.at[d, n * rows // 2 : (n + 1) * rows // 2]
                pltpu.make_async_copy(pieces[base + 3 + n], target, sems.at[0]).start()
    copies = []
    for n, (which, at, width, _, _) in enumerate(specs):
        copies.append(pltpu.make_async_copy(arrays[which].at[:, at : at + width], held[n], sems.at[n + 1]))
        copies[-1].start()
    pltpu.make_async_copy(right, right, sems.at[0]).wait()
    if sums:
        sum_ref[...] = jnp.sum(right[:, :, sums[0] : sums[0] + sums[1]], axis=0)
    for n, (_, _, width, at, columns) in enumerate(specs):
        copies[n].wait()
        tile = min(256, width)

        def step(t, carry, n=n, at=at, columns=columns, tile=tile):
            here = pl.ds(pl.multiple_of(t * tile, tile), tile)
            values = right[:, :, at : at + columns].reshape(ds * rows, columns)
            outs[n][here, :] = tmm(held[n][:, here], values)
            return carry

        lax.fori_loop(0, width // tile, step, 0)


def outer_products(pieces, place, arrays, specs, sums=()):
    rows, columns = pieces[0].shape
    outs = [shape_of(spec[2], spec[4]) for spec in specs]
    if sums:
        outs.append(shape_of(rows, sums[1]))
    anywhere = pl.BlockSpec(memory_space=pl.ANY)
    total = arrays[0].shape[0]
    return pl.pallas_call(
        functools.partial(outer_kernel, specs, len(arrays), sums),
        out_shape=outs,
        in_specs=[pl.BlockSpec(memory_space=pltpu.SMEM)] + [anywhere] * (len(pieces) + len(arrays)),
        out_specs=[pl.BlockSpec(memory_space=pltpu.VMEM)] * len(outs),
        scratch_shapes=[pltpu.VMEM((total // rows, rows, columns), jnp.float32)]
        + [pltpu.VMEM((total, spec[2]), jnp.float32) for spec in specs]
        + [pltpu.SemaphoreType.DMA((len(specs) + 1,))],
        compiler_params=pltpu.CompilerParams(vmem_limit_bytes=VMEM_LIMIT),
        cost_estimate=pl.CostEstimate(
            flops=sum(6 * total * spec[2] * spec[4] for spec in specs), bytes_accessed=20_000_000, transcendentals=0
        ),
    )(place, *pieces, *arrays)


def local(
    interface,
    latents,
    segment_ids,
    read_gain_lat,
    read_gain_int,
    read_query,
    read_keyval,
    read_out,
    read_gain_mlp,
    read_up,
    read_down,
    layer_gain_att,
    layer_qkv,
    layer_out,
    layer_gain_mlp,
    layer_up,
    layer_down,
    write_gain_int,
    write_query,
    write_gain_lat,
    write_keyval,
    write_out,
    write_gain_mlp,
    write_up,
    write_down,
    interface_cot,
    latents_cot,
):
    zs, ds = lax.axis_size("head"), lax.axis_size("dp")
    me, dd = lax.axis_index("head"), lax.axis_index("dp")
    here = HEADS // zs

    def shift(values, step):
        return lax.ppermute(values, "head", [(i, (i + step) % zs) for i in range(zs)])

    def z_scatter(parts):
        total = lax.dynamic_index_in_dim(parts, me, 0, keepdims=False)
        for step in range(1, zs):
            sent = lax.dynamic_index_in_dim(parts, (me + step) % zs, 0, keepdims=False)
            total = total + shift(sent, step)
        return total

    def z_pieces(parts):
        pieces = [lax.dynamic_index_in_dim(parts, me, 0, keepdims=False)]
        for step in range(1, zs):
            sent = lax.dynamic_index_in_dim(parts, (me + step) % zs, 0, keepdims=False)
            pieces.append(shift(sent, step))
        return pieces

    def z_gather(own):
        out = jnp.zeros((zs,) + own.shape, own.dtype)
        out = lax.dynamic_update_index_in_dim(out, own, me, 0)
        for step in range(1, zs):
            out = lax.dynamic_update_index_in_dim(out, shift(own, step), (me - step) % zs, 0)
        return out

    def tie(*values):
        return lax.optimization_barrier(values)

    def sum_over_head(partial, base=None, release=()):
        rows = partial.shape[0] // zs
        own = z_scatter(partial.reshape(zs, rows, -1))
        if base is not None:
            own = own + lax.dynamic_slice_in_dim(base, me * rows, rows, 0)
        own, *release = tie(own, *release)
        full = z_gather(own).reshape(partial.shape)
        return (full, *release) if release else full

    def cut_up(full, parts):
        out, at = [], 0
        for part in parts:
            out.append(full[:, at : at + part.shape[1]])
            at += part.shape[1]
        return out

    def join(parts):
        return jnp.concatenate(parts, axis=1) if len(parts) > 1 else parts[0]

    def d_gather(parts):
        return lax.all_gather(join(parts), "dp", axis=0, tiled=True)

    direct = ds == 8
    chip, core = dd // 2, dd % 2

    def swap(values, bits):
        return lax.ppermute(values, "dp", [(i, i ^ bits) for i in range(ds)])

    def to_sides(joined):
        return [joined, swap(joined, 2), swap(joined, 4)]

    def to_across(joined, by_x, by_y):
        half = joined.shape[0] // 2
        return [joined, by_x, by_y, swap(by_x[:half], 4), swap(by_y[half:], 2)]

    def to_core(*blocks):
        return [*blocks, *(swap(block, 1) for block in blocks)]

    def pick(values, index, axis):
        return lax.dynamic_index_in_dim(values, index, axis, keepdims=False)

    def scatter_one(mine, got):
        x, rows = chip % 2, mine.shape[1]
        mine = mine.reshape((2, 2) + mine.shape[1:])
        got = got.reshape(mine.shape)
        y = chip // 2
        mh, gh, ml, gl = mine[:, :, : rows // 2], got[:, :, : rows // 2], mine[:, :, rows // 2 :], got[:, :, rows // 2 :]
        high, low = pick(mh, x, 1) + pick(gh, x, 1), pick(ml, y, 0) + pick(gl, y, 0)
        sent_high, sent_low = pick(mh, 1 - x, 1) + pick(gh, 1 - x, 1), pick(ml, 1 - y, 0) + pick(gl, 1 - y, 0)
        return high, low, swap(sent_high, 2), swap(sent_low, 4)

    def scatter_two(high, low, got_high, got_low):
        y, x = chip // 2, chip % 2
        sent_high, sent_low = pick(high, 1 - y, 0) + pick(got_high, 1 - y, 0), pick(low, 1 - x, 0) + pick(got_low, 1 - x, 0)
        high, low = pick(high, y, 0) + pick(got_high, y, 0), pick(low, x, 0) + pick(got_low, x, 0)
        return jnp.concatenate([high + swap(sent_high, 4), low + swap(sent_low, 2)], axis=0)

    def d_scatter(parts):
        parts = parts.reshape((4, 2) + parts.shape[1:])
        return scatter_two(*scatter_one(pick(parts, core, 1), swap(pick(parts, 1 - core, 1), 1)))

    interface, latents, segments = interface[0], latents[0], segment_ids[0]
    interface_cot, latents_cot = interface_cot[0], latents_cot[0]
    layer_gain_att, layer_gain_mlp = layer_gain_att[0], layer_gain_mlp[0]
    layer_out, layer_up, layer_down = layer_out[0], layer_up[0], layer_down[0]
    patches, wide = interface.shape
    count, deep = latents.shape
    qkv = layer_qkv[0].reshape(deep, -1)
    keyval = read_keyval.reshape(wide, -1)
    part = deep // zs
    hidden = write_down.shape[0] * zs

    own_segments = lax.dynamic_slice_in_dim(segments, me * patches, patches, 0)

    lat_hat, lat_root = normalise(latents)
    lat_normed = lat_hat * read_gain_lat
    early_all = d_gather([lat_normed])
    int_hat, int_root = normalise(interface)
    gains = jnp.stack([read_gain_int, write_gain_int, write_gain_mlp])
    gains = jnp.pad(gains, ((0, 5), (0, wide - gains.shape[1])))
    int_pack = z_gather(jnp.concatenate([int_hat, gains], axis=0))
    query = mm(lat_normed, read_query)

    wq_rows, up_cols, kv_rows = wide // zs // ds, hidden // ds, deep // ds
    pack = up_cols
    up_share = write_up.reshape(wide // zs, zs, ds, up_cols // zs)
    up_share = lax.dynamic_index_in_dim(up_share, dd, 2, keepdims=False).reshape(wide // zs, up_cols)
    down_share = lax.dynamic_index_in_dim(write_down.reshape(ds, -1, wide), dd, 0, keepdims=False)
    kv_share = lax.dynamic_slice_in_dim(write_keyval, dd * kv_rows, kv_rows, 0).reshape(kv_rows, -1)
    q_share = lax.dynamic_slice_in_dim(write_query, dd * wq_rows, wq_rows, 0)
    o_share = lax.dynamic_slice_in_dim(write_out, dd * wq_rows, wq_rows, 0)

    def narrow(share):
        return [share[:, at : at + pack] for at in range(0, share.shape[1], pack)]

    def widen(full, at, rows, columns):
        n = columns // pack
        return jnp.concatenate([full[:, :, at + i * rows : at + (i + 1) * rows] for i in range(n)], axis=-1)

    flat = jnp.concatenate(
        [up_share] + narrow(down_share) + narrow(kv_share) + narrow(q_share) + narrow(o_share), axis=0
    )
    query, int_pack, flat, early_all = lax.optimization_barrier((query, int_pack, flat, early_all))
    gains = jnp.transpose(int_pack[:, patches : patches + 3, : wide // zs], (1, 0, 2)).reshape(3, wide)
    gain_read, gain_write, gain_mlp = gains[0], gains[1], gains[2]
    shares = lax.all_gather(flat, "head", axis=0, tiled=False)

    kv0, read_attended, read_weights, part0 = run_whole(
        functools.partial(read_kernel, deep // HEADS),
        [
            shape_of(zs * patches, 2 * part),
            shape_of(count, part),
            shape_of(here * count, zs * patches),
            shape_of(count, deep),
        ],
        (query, int_pack, gain_read[None], segment_ids, keyval, read_out),
        flops=8 * zs * patches * wide * part,
    )

    state1 = sum_over_head(part0, latents)
    normed1, pre1, act1, part1 = ffn_forward(state1, read_gain_mlp, read_up, read_down)
    down_rows = hidden // zs // ds
    middle = wide // zs + down_rows * (wide // pack)
    part1, shares = tie(part1, shares)
    if direct:
        by_x, by_y = swap(shares, 2), swap(shares, 4)
    state2, normed1, act1 = sum_over_head(part1, state1, (normed1, act1))
    read_joined = join([normed1, act1])

    normed2, packed, self_attended, self_weights, part2 = run_whole(
        functools.partial(self_kernel, deep // HEADS),
        [
            shape_of(count, deep),
            shape_of(count, 3 * part),
            shape_of(count, part),
            shape_of(here * count, count),
            shape_of(count, deep),
        ],
        (state2, layer_gain_att[None], qkv, layer_out),
        flops=8 * count * deep * part,
    )
    if direct:
        part2, by_x, by_y = tie(part2, by_x, by_y)
        pieces = [shares, by_x, by_y, swap(by_x[:, :middle], 4), swap(by_y[:, middle:], 2)]
    state3 = sum_over_head(part2, state2)
    normed3, pre3, act3, part3 = ffn_forward(state3, layer_gain_mlp, layer_up, layer_down)

    if direct:
        part3, read_joined, *pieces = tie(part3, read_joined, *pieces)
        pieces = pieces + [swap(piece, 1) for piece in pieces]
    else:
        everything = lax.all_gather(shares, "dp", axis=0, tiled=False)
        full_up = jnp.transpose(everything[:, :, : wide // zs], (1, 2, 0, 3)).reshape(zs, wide // zs, hidden)
        at = wide // zs
        full_down = widen(everything, at, down_rows, wide)
        at += down_rows * (wide // pack)
        full_kv = widen(everything, at, kv_rows, 2 * wide // zs)
        full_kv = jnp.transpose(full_kv.reshape(ds, zs, kv_rows, 2, -1), (0, 2, 3, 1, 4)).reshape(deep, 2 * wide)
        at += kv_rows * (2 * wide // zs // pack)
        full_query = jnp.transpose(widen(everything, at, wq_rows, wide), (1, 0, 2, 3)).reshape(zs, -1, wide)
        at += wq_rows * (wide // pack)
        full_out = jnp.transpose(widen(everything, at, wq_rows, wide), (1, 0, 2, 3)).reshape(zs, -1, wide)
        pieces = [full_kv, full_query, full_out, full_up, full_down]
    read_all = d_gather([read_joined])
    state4, normed2, normed3, act3 = sum_over_head(part3, state3, (normed2, normed3, act3))
    layer_all = d_gather([normed2, normed3, act3])

    (
        normed4, interface_new, dafter, dwrite_q, write_attended, after_normed, act5, dpre5, dkv4, dgain_mlp, part4,
        dwrite_normed,
    ) = write_stage(
        state4,
        write_gain_lat,
        int_hat,
        interface,
        interface_cot,
        jnp.stack([gain_write, gain_mlp]),
        own_segments[:, None],
        dd.astype(jnp.int32)[None],
        pieces,
        [
            (deep, 2 * wide),
            (zs, wide // zs, wide),
            (zs, wide // zs, wide),
            (zs, wide // zs, hidden),
            (ds, zs, down_rows, wide),
        ],
    )
    dsum4, after_normed, dpre5, act5, dwrite_q, write_attended, dafter, dkv4 = sum_over_head(
        part4, None, (after_normed, dpre5, act5, dwrite_q, write_attended, dafter, dkv4)
    )

    place = dd.astype(jnp.int32)[None]
    piece_rows = middle + 2 * wq_rows * (wide // pack)
    if direct:
        grads_mine, grads_other = interface_grads(
            after_normed, dpre5, act5, interface_cot, int_hat, gain_write[None], dwrite_q, write_attended, dafter,
            place, zs, piece_rows,
        )
        dsum4, grads_mine, grads_other = tie(dsum4, grads_mine, grads_other)
        grads_mine = grads_mine.reshape(4, -1, pack)
        grads_got = swap(grads_other.reshape(4, -1, pack), 1)
    else:
        write_normed = int_hat * gain_write
        dup = jnp.transpose(tmm(after_normed, dpre5).reshape(zs, wide // zs, ds, -1), (2, 0, 1, 3))

        def pack_grad(grad, rows):
            grad = grad.reshape(ds, zs, rows, wide)
            return [grad[..., at : at + pack] for at in range(0, wide, pack)]

        ddown = tmm(act5, interface_cot)
        dquery = jnp.transpose(tmm(write_normed, dwrite_q).reshape(zs, ds, wq_rows, wide), (1, 0, 2, 3))
        dout = jnp.transpose(tmm(write_attended, dafter).reshape(zs, ds, wq_rows, wide), (1, 0, 2, 3))
        packed_grads = jnp.concatenate(
            [dup] + pack_grad(ddown, down_rows) + pack_grad(dquery, wq_rows) + pack_grad(dout, wq_rows), axis=2
        )
        grads_mine = lax.psum_scatter(packed_grads, "dp", scatter_dimension=0, tiled=False)

    dint = dafter + norm_back(dwrite_normed, int_hat, int_root, gain_write)

    dkv_parts = jnp.transpose(dkv4.reshape(count, 2, zs, -1), (2, 0, 1, 3)).reshape(zs, count, -1)
    dsum4, dkv_parts = tie(dsum4, dkv_parts)
    dkv_mine = z_scatter(dkv_parts)
    dstate4, dgain4, dpre3, part5 = ffn_backward(
        latents_cot, dsum4, state4, write_gain_lat, pre3, layer_up, layer_down
    )
    if direct:
        part5, grads_mine, grads_got, dkv_mine = tie(part5, grads_mine, grads_got, dkv_mine)
        grads_mine = lax.psum_scatter(
            grads_mine + grads_got,
            "dp",
            scatter_dimension=0,
            axis_index_groups=[[2 * k + c for k in range(ds // 2)] for c in range(2)],
        )
    dsum3, normed4, dkv_mine, released4, dpre3 = sum_over_head(part5, None, (normed4, dkv_mine, dstate4, dpre3))
    write_all = d_gather([normed4, dkv_mine, released4, dpre3])
    dsum3, read_all = tie(dsum3, read_all)
    dstate3, dgain3, dpacked, part6 = run_whole(
        functools.partial(self_back_kernel, deep // HEADS),
        [shape_of(count, deep), shape_of(1, deep), shape_of(count, 3 * part), shape_of(count, deep)],
        (dstate4, dsum3, state3, layer_gain_mlp[None], packed, self_weights, qkv, layer_out),
        flops=8 * count * deep * part,
    )
    dsum2, dpacked = sum_over_head(part6, None, (dpacked,))
    dlayer_out = tmm(self_attended, dstate3)
    dsum2, layer_all = tie(dsum2, layer_all)

    dstate2, dgain2, dpre1, part7 = ffn_backward(
        dstate3, dsum2, state2, layer_gain_att, pre1, read_up, read_down
    )
    dsum1, released2, dpre1 = sum_over_head(part7, None, (dstate2, dpre1))
    both_all = d_gather([dpacked, released2, dpre1])
    dsum1, grads_mine = tie(dsum1, grads_mine)
    grads_mine = z_scatter(grads_mine.reshape(zs, -1, pack))
    dstate1, dgain1, dquery0, dread_kv, dlat_part, dint_part, dgain_lat, dgain_int, dkeyval, dread_out = run_whole(
        functools.partial(read_back_kernel, deep // HEADS),
        [
            shape_of(count, deep),
            shape_of(1, deep),
            shape_of(count, part),
            shape_of(zs * patches, 2 * part),
            shape_of(count, deep),
            shape_of(zs * patches, wide),
            shape_of(1, deep),
            shape_of(1, wide),
            shape_of(wide, 2 * part),
            shape_of(part, deep),
        ],
        (dstate2, dsum1, state1, read_gain_mlp[None], query, kv0, read_weights, read_query, keyval, read_out, latents, int_pack,
         gain_read[None], read_attended),
        flops=1e6,
        moved=1e6,
    )

    first = (me == 0).astype(jnp.float32)
    small = jnp.concatenate(
        [dgain_lat[0]]
        + [g[0] * first for g in (dgain1, dgain2, dgain3, dgain4)]
        + [dgain_int[0], jnp.sum(dwrite_normed * int_hat, axis=0), dgain_mlp[0]]
    )
    dlat_part, dstate1, grads_mine, small = tie(dlat_part, dstate1, grads_mine, small)
    lanes = small.size // count
    small = jnp.sum(z_gather(small.reshape(count, lanes)), axis=0)
    fill = jnp.pad(small, ((0, 0), (0, -lanes % 128)))
    late = [join([dquery0, fill])]

    half = z_scatter(dlat_part.reshape(zs, count // zs, deep))
    write_all = tie(write_all, dgain_int)[0]
    normed4_all, dkv_all, dstate4_all, dpre3_all = cut_up(write_all, [normed4, dkv_mine, dstate4, dpre3])
    normed2_all, normed3_all, act3_all = cut_up(layer_all, [normed2, normed3, act3])
    grad_layer_up = tmm(normed3_all, dpre3_all)
    if direct:
        late = to_sides(*late)
        dkeyval = [dkeyval] + [
            grad.reshape(ds, -1, deep)[:, :, at : at + 2 * part].reshape(-1, 2 * part)
            for grad in (dlayer_out, dread_out)
            for at in range(0, deep, 2 * part)
        ]
        dkeyval = jnp.concatenate([grad.reshape(ds, -1, 2 * part) for grad in dkeyval], axis=1)
        dkeyval = dkeyval.reshape(4, 2, -1, 2 * part)
        pair = [pick(dkeyval, core, 1), swap(pick(dkeyval, 1 - core, 1), 1)]
        half, dint_part, grad_layer_up, layer_all, write_all, *held = tie(
            half, dint_part, grad_layer_up, layer_all, write_all, *late, *pair
        )
        _, _, act3_all = cut_up(layer_all, [normed2, normed3, act3])
        normed4_all, dkv_all, dstate4_all, _ = cut_up(write_all, [normed4, dkv_mine, dstate4, dpre3])
        late, pair = to_across(*held[:3]), scatter_one(*held[3:])
    dint_own, *dint_got = z_pieces(dint_part.reshape(zs, patches, wide))
    near, middle_got, far = dint_got[0], dint_got[1:-1], dint_got[-1]
    dlat = z_gather(half).reshape(count, deep)
    grad_layer_down, grad_write_keyval = tmm(act3_all, dstate4_all), tmm(normed4_all, dkv_all)
    if direct:
        grad_layer_down, both_all, near, *held = tie(grad_layer_down, both_all, near, *late, *pair)
        late, dkeyval = to_core(*held[:5]), scatter_two(*held[5:])
    dpacked_all, dstate2_all, dpre1_all = cut_up(both_all, [dpacked, dstate2, dpre1])
    normed1_all, act1_all = cut_up(read_all, [normed1, act1])
    grad_layer_qkv, grad_read_up = tmm(normed2_all, dpacked_all), tmm(normed1_all, dpre1_all)
    if direct:
        dkeyval, grad_layer_qkv, both_all, far, *late = tie(dkeyval, grad_layer_qkv, both_all, far, *late)
        _, dstate2_all, _ = cut_up(both_all, [dpacked, dstate2, dpre1])
    grad_read_down = tmm(act1_all, dstate2_all)
    if direct:
        dlat, grad_write_keyval, grad_read_up, grad_read_down, *middle_got = tie(
            dlat, grad_write_keyval, grad_read_up, grad_read_down, *middle_got
        )
        flat = jnp.concatenate([grads_mine] + [dkeyval[:, at : at + pack] for at in range(0, 2 * part, pack)], axis=0)
        grads_all = lax.all_gather(flat, "dp", axis=0, tiled=False)
        grad_read_query, small = outer_products(
            late, place, [early_all], [(0, 0, deep, 0, part)], (part, fill.shape[1])
        )
        small = small[:, :lanes]
        sums = widen(grads_all[:, None], piece_rows, dkeyval.shape[0], 2 * part)[:, 0]
        at, few = read_keyval.shape[0] // ds, part // ds
        grad_read_keyval = sums[:, :at]
        found = []
        for _ in range(2):
            blocks = [sums[:, at + n * few : at + (n + 1) * few] for n in range(deep // (2 * part))]
            found.append(jnp.concatenate(blocks, axis=-1).reshape(part, deep))
            at += few * len(blocks)
        grad_layer_out, grad_read_out = found
    else:
        grads_all = lax.all_gather(grads_mine, "dp", axis=0, tiled=False)
        grad_read_keyval, grad_layer_out, grad_read_out = lax.psum((dkeyval, dlayer_out, dread_out), "dp")
        dquery0_all, small = cut_up(d_gather(late), [dquery0, fill])
        grad_read_query = tmm(early_all, dquery0_all)
        small = jnp.sum(small.reshape(ds, count, -1)[:, :, :lanes], axis=0)
    latents_grad = dstate1 + norm_back(dlat, lat_hat, lat_root, read_gain_lat)
    dint_normed = dint_own + near + far
    for piece in middle_got:
        dint_normed = dint_normed + piece
    interface_grad = dint + norm_back(dint_normed, int_hat, int_root, gain_read)
    small = small.reshape(-1)
    lat_gains = small[: 5 * deep].reshape(5, deep)
    int_gains = small[5 * deep :].reshape(3, zs, wide // zs)
    int_gains = lax.dynamic_index_in_dim(int_gains, me, 1, keepdims=False)

    full = grads_all[:, None]
    grad_write_up = grads_all[:, : wide // zs].reshape(ds, wide // zs, zs, up_cols // zs)
    grad_write_up = jnp.transpose(grad_write_up, (1, 2, 0, 3)).reshape(write_up.shape)
    at = wide // zs
    grad_write_down = widen(full, at, down_rows, wide).reshape(write_down.shape)
    at += down_rows * (wide // pack)
    grad_write_query = widen(full, at, wq_rows, wide).reshape(write_query.shape)
    at += wq_rows * (wide // pack)
    grad_write_out = widen(full, at, wq_rows, wide).reshape(write_out.shape)

    return (
        interface_new[None],
        state4[None],
        interface_grad[None],
        latents_grad[None],
        lat_gains[0],
        int_gains[0],
        grad_read_query,
        grad_read_keyval.reshape(read_keyval.shape),
        grad_read_out,
        lat_gains[1],
        grad_read_up,
        grad_read_down,
        lat_gains[2][None],
        grad_layer_qkv.reshape(layer_qkv.shape),
        grad_layer_out[None],
        lat_gains[3][None],
        grad_layer_up[None],
        grad_layer_down[None],
        int_gains[1],
        grad_write_query,
        lat_gains[4],
        grad_write_keyval.reshape(write_keyval.shape),
        grad_write_out,
        int_gains[2],
        grad_write_up,
        grad_write_down,
    )


def solution(mesh):
    rows, both = P("dp", "head", None), P("dp", None, None)
    weights = (
        P(),
        P("head"),
        P(None, "head"),
        P(None, None, "head"),
        P("head", None),
        P(),
        P(None, "head"),
        P("head", None),
        P(),
        P(None, None, None, "head"),
        P(None, "head", None),
        P(),
        P(None, None, "head"),
        P(None, "head", None),
        P("head"),
        P("head", None),
        P(),
        P(None, None, "head"),
        P("head", None),
        P("head"),
        P("head", None),
        P("head", None),
    )
    in_specs = (rows, both, P("dp", None)) + weights + (rows, both)
    out_specs = (rows, both, rows, both) + weights
    return jax.shard_map(local, mesh=mesh, in_specs=in_specs, out_specs=out_specs, check_vma=False)
```

```python
import functools

import jax
import jax.numpy as jnp
from jax import lax
from jax.experimental import pallas as pl
from jax.experimental.pallas import tpu as pltpu
from jax.sharding import PartitionSpec as P

HEADS = 16
CROPS = 4
EPSILON = 1e-05
PRECISE = lax.Precision.HIGH
ROOT_HALF = 0.7071067811865476
DENSITY = 0.3989422804014327
VMEM_LIMIT = 56 * 1024 * 1024


def mm(left, right):
    return lax.dot_general(left, right, (((1,), (0,)), ((), ())), precision=PRECISE)


def mmt(left, right):
    return lax.dot_general(left, right, (((1,), (1,)), ((), ())), precision=PRECISE)


def tmm(left, right):
    return lax.dot_general(left, right, (((0,), (0,)), ((), ())), precision=PRECISE)


def normalise(values):
    centred = values - jnp.mean(values, axis=-1, keepdims=True)
    root = lax.rsqrt(jnp.mean(centred * centred, axis=-1, keepdims=True) + EPSILON)
    return centred * root, root


def norm_back(grad, xhat, root, gain):
    scaled = grad * gain
    return root * (
        scaled
        - jnp.mean(scaled, axis=-1, keepdims=True)
        - xhat * jnp.mean(scaled * xhat, axis=-1, keepdims=True)
    )


def cdf(values):
    return 0.5 * (1.0 + lax.erf(values * ROOT_HALF))


def gelu_slope(values):
    return cdf(values) + values * DENSITY * jnp.exp(-0.5 * values * values)


def shape_of(*dims):
    return jax.ShapeDtypeStruct(dims, jnp.float32)


def run_whole(kernel, outs, args, flops=1e9, moved=None, scratch=(), anywhere=0):
    moved = moved or sum(a.size * 4 for a in args) + sum(int(functools.reduce(lambda x, y: x * y, o.shape)) * 4 for o in outs)
    fast = len(args) - anywhere
    return pl.pallas_call(
        kernel,
        out_shape=outs,
        in_specs=[pl.BlockSpec(memory_space=pltpu.VMEM)] * fast + [pl.BlockSpec(memory_space=pl.ANY)] * anywhere,
        out_specs=[pl.BlockSpec(memory_space=pltpu.VMEM)] * len(outs),
        scratch_shapes=list(scratch),
        compiler_params=pltpu.CompilerParams(vmem_limit_bytes=VMEM_LIMIT),
        cost_estimate=pl.CostEstimate(flops=int(flops * 3), bytes_accessed=int(moved), transcendentals=0),
    )(*args)


def lane_mask(lanes, width, head):
    return lax.broadcasted_iota(jnp.int32, (1, lanes), 1) // width == head


def spread(values, width):
    lanes = values.shape[1]
    return jnp.concatenate(
        [jnp.where(lane_mask(lanes, width, h), values, 0.0) for h in range(lanes // width)], axis=0
    )


def fold(values, width):
    lanes = values.shape[1]
    rows = values.shape[0] // (lanes // width)
    total = jnp.zeros((rows, lanes), jnp.float32)
    for h in range(lanes // width):
        total = total + jnp.where(lane_mask(lanes, width, h), values[h * rows : (h + 1) * rows], 0.0)
    return total


def attend_group(q, k, v, mask, width):
    count = q.shape[1] // width
    scores = mmt(spread(q, width), k) * (width ** -0.5)
    scores = scores.reshape(count, q.shape[0], k.shape[0])
    scores = jnp.where(mask[None], scores, -1e30)
    weights = jnp.exp(scores - jnp.max(scores, axis=-1, keepdims=True))
    weights = weights / jnp.sum(weights, axis=-1, keepdims=True)
    weights = weights.reshape(count * q.shape[0], k.shape[0])
    return fold(mm(weights, v), width), weights


def attend_group_back(grad, q, k, v, weights, width):
    grads = spread(grad, width)
    dp = mmt(grads, v)
    ds = weights * (dp - jnp.sum(dp * weights, axis=-1, keepdims=True)) * (width ** -0.5)
    return fold(mm(ds, k), width), tmm(ds, spread(q, width)), tmm(weights, grads)


def crop_rows(count, total):
    return lax.broadcasted_iota(jnp.int32, (count, 1), 0) // (total // CROPS)


def crop_lanes(count, total):
    return lax.broadcasted_iota(jnp.int32, (1, count), 1) // (total // CROPS)


def groups_of(ref, start, size, lanes):
    return [slice(start + at, start + at + lanes) for at in range(0, size, lanes)]


def ffn_kernel(state_ref, gain_ref, up_ref, down_ref, normed_ref, pre_ref, act_ref, out_ref):
    @pl.when(pl.program_id(0) == 0)
    def _():
        hat, _ = normalise(state_ref[...])
        normed_ref[...] = hat * gain_ref[...]
        out_ref[...] = jnp.zeros_like(out_ref)

    pre = mm(normed_ref[...], up_ref[...])
    act = pre * cdf(pre)
    pre_ref[...] = pre
    act_ref[...] = act
    out_ref[...] += mm(act, down_ref[...])


def ffn_forward(state, gain, up, down):
    rows, deep = state.shape
    inner = up.shape[1]
    tile = min(256, inner)
    whole = pl.BlockSpec((rows, deep), lambda t: (0, 0))
    part = pl.BlockSpec((rows, tile), lambda t: (0, t))
    return pl.pallas_call(
        ffn_kernel,
        grid=(inner // tile,),
        out_shape=[shape_of(rows, deep), shape_of(rows, inner), shape_of(rows, inner), shape_of(rows, deep)],
        in_specs=[
            whole,
            pl.BlockSpec((1, deep), lambda t: (0, 0)),
            pl.BlockSpec((deep, tile), lambda t: (0, t)),
            pl.BlockSpec((tile, deep), lambda t: (t, 0)),
        ],
        out_specs=[whole, part, part, whole],
        compiler_params=pltpu.CompilerParams(vmem_limit_bytes=VMEM_LIMIT),
        cost_estimate=pl.CostEstimate(flops=12 * rows * deep * inner, bytes_accessed=8 * deep * inner, transcendentals=0),
    )(state, gain[None], up, down)


def residual_back(base_ref, dsum_ref, state_ref, gain_ref, grad_ref, dgain_ref):
    hat, root = normalise(state_ref[...])
    dsum = dsum_ref[...]
    grad_ref[...] = base_ref[...] + norm_back(dsum, hat, root, gain_ref[...])
    dgain_ref[...] = jnp.sum(dsum * hat, axis=0, keepdims=True)


def ffn_back_kernel(
    base_ref, dsum_ref, state_ref, gain_ref, pre_ref, up_ref, down_ref, grad_ref, dgain_ref, dpre_ref, out_ref
):
    @pl.when(pl.program_id(0) == 0)
    def _():
        residual_back(base_ref, dsum_ref, state_ref, gain_ref, grad_ref, dgain_ref)
        out_ref[...] = jnp.zeros_like(out_ref)

    dpre = mmt(grad_ref[...], down_ref[...]) * gelu_slope(pre_ref[...])
    dpre_ref[...] = dpre
    out_ref[...] += mmt(dpre, up_ref[...])


def ffn_backward(base, dsum, state, gain, pre, up, down):
    rows, deep = state.shape
    inner = up.shape[1]
    tile = min(256, inner)
    whole = pl.BlockSpec((rows, deep), lambda t: (0, 0))
    row = pl.BlockSpec((1, deep), lambda t: (0, 0))
    part = pl.BlockSpec((rows, tile), lambda t: (0, t))
    return pl.pallas_call(
        ffn_back_kernel,
        grid=(inner // tile,),
        out_shape=[shape_of(rows, deep), shape_of(1, deep), shape_of(rows, inner), shape_of(rows, deep)],
        in_specs=[
            whole,
            whole,
            whole,
            row,
            part,
            pl.BlockSpec((deep, tile), lambda t: (0, t)),
            pl.BlockSpec((tile, deep), lambda t: (t, 0)),
        ],
        out_specs=[whole, row, part, whole],
        compiler_params=pltpu.CompilerParams(vmem_limit_bytes=VMEM_LIMIT),
        cost_estimate=pl.CostEstimate(flops=12 * rows * deep * inner, bytes_accessed=8 * deep * inner, transcendentals=0),
    )(base, dsum, state, gain[None], pre, up, down)


def self_kernel(width, state_ref, gain_ref, qkv_ref, wout_ref, normed_ref, packed_ref, att_ref, weights_ref, out_ref):
    hat, _ = normalise(state_ref[...])
    normed = hat * gain_ref[...]
    normed_ref[...] = normed
    part = att_ref.shape[1]
    for at in range(3):
        packed_ref[:, at * part : (at + 1) * part] = mm(normed, qkv_ref[:, at * part : (at + 1) * part])
    rows = normed.shape[0]
    mask = crop_rows(rows, rows) == crop_lanes(rows, rows)
    for g in range(part // 128):
        q, k, v = [packed_ref[:, at * part + g * 128 : at * part + (g + 1) * 128] for at in range(3)]
        att, weights = attend_group(q, k, v, mask, width)
        att_ref[:, g * 128 : (g + 1) * 128] = att
        n = weights.shape[0]
        weights_ref[g * n : (g + 1) * n] = weights
    out_ref[...] = mm(att_ref[...], wout_ref[...])


def self_back_kernel(
    width,
    base_ref,
    dsum_ref,
    state_ref,
    gain_ref,
    packed_ref,
    weights_ref,
    qkv_ref,
    wout_ref,
    grad_ref,
    dgain_ref,
    dpacked_ref,
    out_ref,
):
    residual_back(base_ref, dsum_ref, state_ref, gain_ref, grad_ref, dgain_ref)
    part = dpacked_ref.shape[1] // 3
    datt = mmt(grad_ref[...], wout_ref[...])
    count = 128 // width * datt.shape[0]
    for g in range(part // 128):
        q, k, v = [packed_ref[:, at * part + g * 128 : at * part + (g + 1) * 128] for at in range(3)]
        found = attend_group_back(
            datt[:, g * 128 : (g + 1) * 128], q, k, v, weights_ref[g * count : (g + 1) * count], width
        )
        for at in range(3):
            dpacked_ref[:, at * part + g * 128 : at * part + (g + 1) * 128] = found[at]
    out_ref[...] = mmt(dpacked_ref[...], qkv_ref[...])


def read_kernel(width, q_ref, hat_ref, gain_ref, seg_ref, keyval_ref, wout_ref, kv_ref, att_ref, weights_ref, out_ref):
    part = att_ref.shape[1]
    patches = kv_ref.shape[0] // hat_ref.shape[0]
    for z in range(hat_ref.shape[0]):
        kv_ref[z * patches : (z + 1) * patches] = mm(hat_ref[z, :patches] * gain_ref[...], keyval_ref[...])
    rows = q_ref.shape[0]
    mask = crop_rows(rows, rows) == seg_ref[...]
    for g in range(part // 128):
        at = slice(g * 128, (g + 1) * 128)
        att, weights = attend_group(
            q_ref[:, at], kv_ref[:, at], kv_ref[:, part + g * 128 : part + (g + 1) * 128], mask, width
        )
        att_ref[:, at] = att
        n = weights.shape[0]
        weights_ref[g * n : (g + 1) * n] = weights
    out_ref[...] = mm(att_ref[...], wout_ref[...])


def read_back_kernel(
    width,
    base_ref,
    dsum_ref,
    state_ref,
    gain_ref,
    q_ref,
    kv_ref,
    weights_ref,
    wquery_ref,
    keyval_ref,
    wout_ref,
    latents_ref,
    hat_ref,
    int_gain_ref,
    att_ref,
    grad_ref,
    dgain_ref,
    dq_ref,
    dkv_ref,
    dlat_ref,
    dint_ref,
    dgain_lat_ref,
    dgain_int_ref,
    dkeyval_ref,
    dout_ref,
):
    residual_back(base_ref, dsum_ref, state_ref, gain_ref, grad_ref, dgain_ref)
    part = dq_ref.shape[1]
    datt = mmt(grad_ref[...], wout_ref[...])
    count = 128 // width * datt.shape[0]
    for g in range(part // 128):
        at, behind = slice(g * 128, (g + 1) * 128), slice(part + g * 128, part + (g + 1) * 128)
        found = attend_group_back(
            datt[:, at], q_ref[:, at], kv_ref[:, at], kv_ref[:, behind], weights_ref[g * count : (g + 1) * count], width
        )
        dq_ref[:, at], dkv_ref[:, at], dkv_ref[:, behind] = found
    dlat = mmt(dq_ref[...], wquery_ref[...])
    dlat_ref[...] = dlat
    hat, _ = normalise(latents_ref[...])
    dgain_lat_ref[...] = jnp.sum(dlat * hat, axis=0, keepdims=True)
    dint = mmt(dkv_ref[...], keyval_ref[...])
    dint_ref[...] = dint
    patches = dint.shape[0] // hat_ref.shape[0]
    dgain_int = jnp.zeros_like(dgain_int_ref)
    for z in range(hat_ref.shape[0]):
        dgain_int += jnp.sum(dint[z * patches : (z + 1) * patches] * hat_ref[z, :patches], axis=0, keepdims=True)
    dgain_int_ref[...] = dgain_int
    dout_ref[...] = tmm(att_ref[...], grad_ref[...])
    total = jnp.zeros_like(dkeyval_ref)
    for z in range(hat_ref.shape[0]):
        total += tmm(hat_ref[z, :patches] * int_gain_ref[...], dkv_ref[z * patches : (z + 1) * patches])
    dkeyval_ref[...] = total


def write_kernel(
    width,
    state_ref,
    gain_ref,
    hat_ref,
    int_ref,
    cot_ref,
    gains_ref,
    seg_ref,
    place_ref,
    sources,
    normed_ref,
    new_ref,
    dafter_ref,
    dq_ref,
    att_ref,
    y_ref,
    act_ref,
    dpre_ref,
    dkv_ref,
    dgain_ref,
    out_ref,
    dhat_ref,
    wkv,
    wquery,
    wout,
    up,
    down,
    kv,
    q,
    weights,
    dy,
    sems,
):
    targets = [wkv, wquery, wout, up, down]
    if len(sources) == 5:
        for n in range(5):
            pltpu.make_async_copy(sources[n], targets[n], sems.at[n]).start()
    else:
        bring_pieces(sources, targets, sems, place_ref[0])

    def arrived(n):
        pltpu.make_async_copy(targets[n], targets[n], sems.at[n]).wait()

    hat4, _ = normalise(state_ref[...])
    normed = hat4 * gain_ref[...]
    normed_ref[...] = normed
    wide = hat_ref.shape[1]
    patches = hat_ref.shape[0]
    lats = normed.shape[0]
    arrived(1)
    q[...] = mm(hat_ref[...] * gains_ref[0:1], wquery[...].reshape(wide, wide))
    arrived(0)

    def project(t, carry):
        at = pl.ds(pl.multiple_of(t * 256, 256), 256)
        kv[:, at] = mm(normed_ref[...], wkv[:, at])
        return carry

    lax.fori_loop(0, kv.shape[1] // 256, project, 0)
    mask = seg_ref[...] == crop_lanes(lats, lats)
    count = 128 // width * patches

    def forward(g, carry):
        at = pl.ds(pl.multiple_of(g * 128, 128), 128)
        behind = pl.ds(pl.multiple_of(wide + g * 128, 128), 128)
        found, shares = attend_group(q[:, at], kv[:, at], kv[:, behind], mask, width)
        att_ref[:, at] = found
        weights[pl.ds(pl.multiple_of(g * count, count), count)] = shares
        return carry

    lax.fori_loop(0, wide // 128, forward, 0)
    arrived(2)
    after = int_ref[...] + mm(att_ref[...], wout[...].reshape(wide, wide))
    after_hat, after_root = normalise(after)
    y_ref[...] = after_hat * gains_ref[1:2]
    new_ref[...] = after
    dy[...] = jnp.zeros_like(dy)
    arrived(3)
    arrived(4)
    tile = down.shape[1] * down.shape[2]

    def mlp(t, carry):
        at = pl.ds(pl.multiple_of(t * tile, tile), tile)
        up_part = up[:, :, at].reshape(wide, tile)
        down_part = down[t].reshape(tile, wide)
        pre = mm(y_ref[...], up_part)
        share = cdf(pre)
        act = pre * share
        act_ref[:, at] = act
        new_ref[...] += mm(act, down_part)
        slope = share + pre * DENSITY * jnp.exp(-0.5 * pre * pre)
        dpre = mmt(cot_ref[...], down_part) * slope
        dpre_ref[:, at] = dpre
        dy[...] += mmt(dpre, up_part)
        return carry

    lax.fori_loop(0, down.shape[0], mlp, 0)
    dgain_ref[...] = jnp.sum(dy[...] * after_hat, axis=0, keepdims=True)
    dafter_ref[...] = cot_ref[...] + norm_back(dy[...], after_hat, after_root, gains_ref[1:2])
    dy[...] = mmt(dafter_ref[...], wout[...].reshape(wide, wide))

    def backward(g, carry):
        at = pl.ds(pl.multiple_of(g * 128, 128), 128)
        behind = pl.ds(pl.multiple_of(wide + g * 128, 128), 128)
        shares = weights[pl.ds(pl.multiple_of(g * count, count), count)]
        found = attend_group_back(dy[:, at], q[:, at], kv[:, at], kv[:, behind], shares, width)
        dq_ref[:, at], dkv_ref[:, at], dkv_ref[:, behind] = found
        return carry

    lax.fori_loop(0, wide // 128, backward, 0)

    def close(t, carry):
        at = pl.ds(pl.multiple_of(t * 256, 256), 256)
        out_ref[:, at] = mmt(dkv_ref[...], wkv[at, :])
        return carry

    lax.fori_loop(0, out_ref.shape[1] // 256, close, 0)
    dhat_ref[...] = mmt(dq_ref[...], wquery[...].reshape(wide, wide))


def bring_pieces(sources, targets, sems, place):
    wkv, wquery, wout, up, down = targets
    zs, rows, wide = wquery.shape
    ds, _, inner, _ = down.shape
    pack = up.shape[2] // ds
    deep_rows, q_rows = wkv.shape[0] // ds, rows // ds
    lanes = wide // zs
    first = rows + inner * (wide // pack)
    for step in range(ds):
        d = jnp.bitwise_xor(place, step)
        base = (step % 2) * 5
        near = sources[base + min(step // 2, 3)]
        far, shift = (sources[base + 4], first) if step // 2 == 3 else (near, 0)

        def bring(source, target, sem):
            pltpu.make_async_copy(source, target, sems.at[sem]).start()

        at = first - shift
        for z in range(zs):
            for b in range(2):
                bring(
                    far.at[z, at : at + deep_rows, b * lanes : (b + 1) * lanes],
                    wkv.at[pl.ds(pl.multiple_of(d * deep_rows, deep_rows), deep_rows), pl.ds(b * wide + z * lanes, lanes)],
                    0,
                )
        at += deep_rows
        for n, target in ((1, wquery), (2, wout)):
            for b in range(wide // pack):
                bring(
                    far.at[:, at : at + q_rows],
                    target.at[:, pl.ds(pl.multiple_of(d * q_rows, q_rows), q_rows), pl.ds(b * pack, pack)],
                    n,
                )
                at += q_rows
        bring(near.at[:, :rows], up.at[:, :, pl.ds(pl.multiple_of(d * pack, pack), pack)], 3)
        for b in range(wide // pack):
            start = rows + b * inner
            bring(near.at[:, start : start + inner], down.at[d, :, :, pl.ds(b * pack, pack)], 4)


def write_stage(state, gain, hat, interface, cot, gains, seg, place, sources, shapes):
    rows, deep = state.shape
    patches, wide = hat.shape
    hidden = shapes[3][2]
    n = HEADS * patches
    small = shape_of(patches, wide)
    big = shape_of(patches, hidden)
    outs = [
        shape_of(rows, deep), small, small, small, small, small, big, big,
        shape_of(rows, 2 * wide), shape_of(1, wide), shape_of(rows, deep), small,
    ]
    vmem = pl.BlockSpec(memory_space=pltpu.VMEM)
    kernel = functools.partial(write_kernel, wide // HEADS)
    count = len(sources)

    def call(*refs):
        kernel(*refs[:8], refs[8 : 8 + count], *refs[8 + count :])

    return pl.pallas_call(
        call,
        out_shape=outs,
        in_specs=[vmem] * 7 + [pl.BlockSpec(memory_space=pltpu.SMEM)] + [pl.BlockSpec(memory_space=pl.ANY)] * count,
        out_specs=[vmem] * len(outs),
        scratch_shapes=[pltpu.VMEM(shape, jnp.float32) for shape in shapes]
        + [
            pltpu.VMEM((rows, 2 * wide), jnp.float32),
            pltpu.VMEM((patches, wide), jnp.float32),
            pltpu.VMEM((n, rows), jnp.float32),
            pltpu.VMEM((patches, wide), jnp.float32),
            pltpu.SemaphoreType.DMA((5,)),
        ],
        compiler_params=pltpu.CompilerParams(vmem_limit_bytes=VMEM_LIMIT),
        cost_estimate=pl.CostEstimate(flops=20_000_000_000, bytes_accessed=40_000_000, transcendentals=0),
    )(state, gain[None], hat, interface, cot, gains, seg, place, *sources)


def grads_kernel(y_ref, dpre_ref, act_ref, cot_ref, hat_ref, gain_ref, dq_ref, att_ref, dafter_ref, place_ref, mine_ref, other_ref, square):
    core = jnp.bitwise_and(place_ref[0], 1)
    wide = y_ref.shape[1]
    pack = mine_ref.shape[3]
    chips, zs = mine_ref.shape[0], mine_ref.shape[1]
    rows = wide // zs
    inner = pack // zs
    q_rows = rows // (2 * chips)
    square[0] = tmm(hat_ref[...] * gain_ref[...], dq_ref[...])
    square[1] = tmm(att_ref[...], dafter_ref[...])

    def step(j, carry):
        for out_ref, bit in ((mine_ref, core), (other_ref, 1 - core)):
            d = 2 * j + bit
            at = pl.ds(pl.multiple_of(d * pack, pack), pack)
            out_ref[j, :, :rows] = tmm(y_ref[...], dpre_ref[:, at]).reshape(zs, rows, pack)
            start = rows
            ddown = tmm(act_ref[:, at], cot_ref[...])
            for b in range(wide // pack):
                out_ref[j, :, start : start + inner] = ddown[:, b * pack : (b + 1) * pack].reshape(zs, inner, pack)
                start += inner
            for n in range(2):
                for b in range(wide // pack):
                    for z in range(zs):
                        source = pl.ds(pl.multiple_of(z * rows + d * q_rows, q_rows), q_rows)
                        out_ref[j, z, start : start + q_rows] = square[n, source, b * pack : (b + 1) * pack]
                    start += q_rows
        return carry

    lax.fori_loop(0, chips, step, 0)


def interface_grads(y, dpre, act, cot, hat, gain, dq, att, dafter, place, zs, rows):
    patches, wide = y.shape
    pack = dpre.shape[1] // 8
    out = shape_of(4, zs, rows, pack)
    vmem = pl.BlockSpec(memory_space=pltpu.VMEM)
    return pl.pallas_call(
        grads_kernel,
        out_shape=[out, out],
        in_specs=[vmem] * 9 + [pl.BlockSpec(memory_space=pltpu.SMEM)],
        out_specs=[vmem, vmem],
        scratch_shapes=[pltpu.VMEM((2, wide, wide), jnp.float32)],
        compiler_params=pltpu.CompilerParams(vmem_limit_bytes=VMEM_LIMIT),
        cost_estimate=pl.CostEstimate(flops=10_000_000_000, bytes_accessed=20_000_000, transcendentals=0),
    )(y, dpre, act, cot, hat, gain, dq, att, dafter, place)


def outer_kernel(specs, lefts, sums, place_ref, *refs):
    pieces, refs = refs[:10], refs[10:]
    arrays, refs = refs[:lefts], refs[lefts:]
    outs, refs = refs[: len(specs)], refs[len(specs) :]
    if sums:
        sum_ref, refs = refs[0], refs[1:]
    right, held, sems = refs[0], refs[1 : 1 + len(specs)], refs[1 + len(specs)]
    ds, rows, _ = right.shape
    for step in range(ds):
        d = jnp.bitwise_xor(place_ref[0], step)
        base, far = (step % 2) * 5, step // 2
        if far < 3:
            pltpu.make_async_copy(pieces[base + far], right.at[d], sems.at[0]).start()
        else:
            for n in range(2):
                target = right.at[d, n * rows // 2 : (n + 1) * rows // 2]
                pltpu.make_async_copy(pieces[base + 3 + n], target, sems.at[0]).start()
    copies = []
    for n, (which, at, width, _, _) in enumerate(specs):
        copies.append(pltpu.make_async_copy(arrays[which].at[:, at : at + width], held[n], sems.at[n + 1]))
        copies[-1].start()
    pltpu.make_async_copy(right, right, sems.at[0]).wait()
    if sums:
        sum_ref[...] = jnp.sum(right[:, :, sums[0] : sums[0] + sums[1]], axis=0)
    for n, (_, _, width, at, columns) in enumerate(specs):
        copies[n].wait()
        tile = min(256, width)

        def step(t, carry, n=n, at=at, columns=columns, tile=tile):
            here = pl.ds(pl.multiple_of(t * tile, tile), tile)
            values = right[:, :, at : at + columns].reshape(ds * rows, columns)
            outs[n][here, :] = tmm(held[n][:, here], values)
            return carry

        lax.fori_loop(0, width // tile, step, 0)


def outer_products(pieces, place, arrays, specs, sums=()):
    rows, columns = pieces[0].shape
    outs = [shape_of(spec[2], spec[4]) for spec in specs]
    if sums:
        outs.append(shape_of(rows, sums[1]))
    anywhere = pl.BlockSpec(memory_space=pl.ANY)
    total = arrays[0].shape[0]
    return pl.pallas_call(
        functools.partial(outer_kernel, specs, len(arrays), sums),
        out_shape=outs,
        in_specs=[pl.BlockSpec(memory_space=pltpu.SMEM)] + [anywhere] * (len(pieces) + len(arrays)),
        out_specs=[pl.BlockSpec(memory_space=pltpu.VMEM)] * len(outs),
        scratch_shapes=[pltpu.VMEM((total // rows, rows, columns), jnp.float32)]
        + [pltpu.VMEM((total, spec[2]), jnp.float32) for spec in specs]
        + [pltpu.SemaphoreType.DMA((len(specs) + 1,))],
        compiler_params=pltpu.CompilerParams(vmem_limit_bytes=VMEM_LIMIT),
        cost_estimate=pl.CostEstimate(
            flops=sum(6 * total * spec[2] * spec[4] for spec in specs), bytes_accessed=20_000_000, transcendentals=0
        ),
    )(place, *pieces, *arrays)


def local(
    interface,
    latents,
    segment_ids,
    read_gain_lat,
    read_gain_int,
    read_query,
    read_keyval,
    read_out,
    read_gain_mlp,
    read_up,
    read_down,
    layer_gain_att,
    layer_qkv,
    layer_out,
    layer_gain_mlp,
    layer_up,
    layer_down,
    write_gain_int,
    write_query,
    write_gain_lat,
    write_keyval,
    write_out,
    write_gain_mlp,
    write_up,
    write_down,
    interface_cot,
    latents_cot,
):
    zs, ds = lax.axis_size("head"), lax.axis_size("dp")
    me, dd = lax.axis_index("head"), lax.axis_index("dp")
    here = HEADS // zs

    def shift(values, step):
        return lax.ppermute(values, "head", [(i, (i + step) % zs) for i in range(zs)])

    def z_scatter(parts):
        total = lax.dynamic_index_in_dim(parts, me, 0, keepdims=False)
        for step in range(1, zs):
            sent = lax.dynamic_index_in_dim(parts, (me + step) % zs, 0, keepdims=False)
            total = total + shift(sent, step)
        return total

    def z_pieces(parts):
        pieces = [lax.dynamic_index_in_dim(parts, me, 0, keepdims=False)]
        for step in range(1, zs):
            sent = lax.dynamic_index_in_dim(parts, (me + step) % zs, 0, keepdims=False)
            pieces.append(shift(sent, step))
        return pieces

    def z_gather(own):
        out = jnp.zeros((zs,) + own.shape, own.dtype)
        out = lax.dynamic_update_index_in_dim(out, own, me, 0)
        for step in range(1, zs):
            out = lax.dynamic_update_index_in_dim(out, shift(own, step), (me - step) % zs, 0)
        return out

    def tie(*values):
        return lax.optimization_barrier(values)

    def sum_over_head(partial, base=None, release=()):
        rows = partial.shape[0] // zs
        own = z_scatter(partial.reshape(zs, rows, -1))
        if base is not None:
            own = own + lax.dynamic_slice_in_dim(base, me * rows, rows, 0)
        own, *release = tie(own, *release)
        full = z_gather(own).reshape(partial.shape)
        return (full, *release) if release else full

    def cut_up(full, parts):
        out, at = [], 0
        for part in parts:
            out.append(full[:, at : at + part.shape[1]])
            at += part.shape[1]
        return out

    def join(parts):
        return jnp.concatenate(parts, axis=1) if len(parts) > 1 else parts[0]

    def d_gather(parts):
        return lax.all_gather(join(parts), "dp", axis=0, tiled=True)

    direct = ds == 8
    chip, core = dd // 2, dd % 2

    def swap(values, bits):
        return lax.ppermute(values, "dp", [(i, i ^ bits) for i in range(ds)])

    def to_sides(joined):
        return [joined, swap(joined, 2), swap(joined, 4)]

    def to_across(joined, by_x, by_y):
        half = joined.shape[0] // 2
        return [joined, by_x, by_y, swap(by_x[:half], 4), swap(by_y[half:], 2)]

    def to_core(*blocks):
        return [*blocks, *(swap(block, 1) for block in blocks)]

    def pick(values, index, axis):
        return lax.dynamic_index_in_dim(values, index, axis, keepdims=False)

    def scatter_one(mine, got):
        x, rows = chip % 2, mine.shape[1]
        mine = mine.reshape((2, 2) + mine.shape[1:])
        got = got.reshape(mine.shape)
        y = chip // 2
        mh, gh, ml, gl = mine[:, :, : rows // 2], got[:, :, : rows // 2], mine[:, :, rows // 2 :], got[:, :, rows // 2 :]
        high, low = pick(mh, x, 1) + pick(gh, x, 1), pick(ml, y, 0) + pick(gl, y, 0)
        sent_high, sent_low = pick(mh, 1 - x, 1) + pick(gh, 1 - x, 1), pick(ml, 1 - y, 0) + pick(gl, 1 - y, 0)
        return high, low, swap(sent_high, 2), swap(sent_low, 4)

    def scatter_two(high, low, got_high, got_low):
        y, x = chip // 2, chip % 2
        sent_high, sent_low = pick(high, 1 - y, 0) + pick(got_high, 1 - y, 0), pick(low, 1 - x, 0) + pick(got_low, 1 - x, 0)
        high, low = pick(high, y, 0) + pick(got_high, y, 0), pick(low, x, 0) + pick(got_low, x, 0)
        return jnp.concatenate([high + swap(sent_high, 4), low + swap(sent_low, 2)], axis=0)

    def d_scatter(parts):
        parts = parts.reshape((4, 2) + parts.shape[1:])
        return scatter_two(*scatter_one(pick(parts, core, 1), swap(pick(parts, 1 - core, 1), 1)))

    interface, latents, segments = interface[0], latents[0], segment_ids[0]
    interface_cot, latents_cot = interface_cot[0], latents_cot[0]
    layer_gain_att, layer_gain_mlp = layer_gain_att[0], layer_gain_mlp[0]
    layer_out, layer_up, layer_down = layer_out[0], layer_up[0], layer_down[0]
    patches, wide = interface.shape
    count, deep = latents.shape
    qkv = layer_qkv[0].reshape(deep, -1)
    keyval = read_keyval.reshape(wide, -1)
    part = deep // zs
    hidden = write_down.shape[0] * zs

    own_segments = lax.dynamic_slice_in_dim(segments, me * patches, patches, 0)

    lat_hat, lat_root = normalise(latents)
    lat_normed = lat_hat * read_gain_lat
    early_all = d_gather([lat_normed])
    int_hat, int_root = normalise(interface)
    gains = jnp.stack([read_gain_int, write_gain_int, write_gain_mlp])
    gains = jnp.pad(gains, ((0, 5), (0, wide - gains.shape[1])))
    int_pack = z_gather(jnp.concatenate([int_hat, gains], axis=0))
    query = mm(lat_normed, read_query)

    wq_rows, up_cols, kv_rows = wide // zs // ds, hidden // ds, deep // ds
    pack = up_cols
    up_share = write_up.reshape(wide // zs, zs, ds, up_cols // zs)
    up_share = lax.dynamic_index_in_dim(up_share, dd, 2, keepdims=False).reshape(wide // zs, up_cols)
    down_share = lax.dynamic_index_in_dim(write_down.reshape(ds, -1, wide), dd, 0, keepdims=False)
    kv_share = lax.dynamic_slice_in_dim(write_keyval, dd * kv_rows, kv_rows, 0).reshape(kv_rows, -1)
    q_share = lax.dynamic_slice_in_dim(write_query, dd * wq_rows, wq_rows, 0)
    o_share = lax.dynamic_slice_in_dim(write_out, dd * wq_rows, wq_rows, 0)

    def narrow(share):
        return [share[:, at : at + pack] for at in range(0, share.shape[1], pack)]

    def widen(full, at, rows, columns):
        n = columns // pack
        return jnp.concatenate([full[:, :, at + i * rows : at + (i + 1) * rows] for i in range(n)], axis=-1)

    flat = jnp.concatenate(
        [up_share] + narrow(down_share) + narrow(kv_share) + narrow(q_share) + narrow(o_share), axis=0
    )
    query, int_pack, flat, early_all = lax.optimization_barrier((query, int_pack, flat, early_all))
    gains = jnp.transpose(int_pack[:, patches : patches + 3, : wide // zs], (1, 0, 2)).reshape(3, wide)
    gain_read, gain_write, gain_mlp = gains[0], gains[1], gains[2]
    shares = lax.all_gather(flat, "head", axis=0, tiled=False)

    kv0, read_attended, read_weights, part0 = run_whole(
        functools.partial(read_kernel, deep // HEADS),
        [
            shape_of(zs * patches, 2 * part),
            shape_of(count, part),
            shape_of(here * count, zs * patches),
            shape_of(count, deep),
        ],
        (query, int_pack, gain_read[None], segment_ids, keyval, read_out),
        flops=8 * zs * patches * wide * part,
    )

    state1 = sum_over_head(part0, latents)
    normed1, pre1, act1, part1 = ffn_forward(state1, read_gain_mlp, read_up, read_down)
    down_rows = hidden // zs // ds
    middle = wide // zs + down_rows * (wide // pack)
    part1, shares = tie(part1, shares)
    if direct:
        by_x, by_y = swap(shares, 2), swap(shares, 4)
    state2, normed1, act1 = sum_over_head(part1, state1, (normed1, act1))
    read_joined = join([normed1, act1])

    normed2, packed, self_attended, self_weights, part2 = run_whole(
        functools.partial(self_kernel, deep // HEADS),
        [
            shape_of(count, deep),
            shape_of(count, 3 * part),
            shape_of(count, part),
            shape_of(here * count, count),
            shape_of(count, deep),
        ],
        (state2, layer_gain_att[None], qkv, layer_out),
        flops=8 * count * deep * part,
    )
    if direct:
        part2, by_x, by_y = tie(part2, by_x, by_y)
        pieces = [shares, by_x, by_y, swap(by_x[:, :middle], 4), swap(by_y[:, middle:], 2)]
    state3 = sum_over_head(part2, state2)
    normed3, pre3, act3, part3 = ffn_forward(state3, layer_gain_mlp, layer_up, layer_down)

    if direct:
        part3, read_joined, *pieces = tie(part3, read_joined, *pieces)
        pieces = pieces + [swap(piece, 1) for piece in pieces]
    else:
        everything = lax.all_gather(shares, "dp", axis=0, tiled=False)
        full_up = jnp.transpose(everything[:, :, : wide // zs], (1, 2, 0, 3)).reshape(zs, wide // zs, hidden)
        at = wide // zs
        full_down = widen(everything, at, down_rows, wide)
        at += down_rows * (wide // pack)
        full_kv = widen(everything, at, kv_rows, 2 * wide // zs)
        full_kv = jnp.transpose(full_kv.reshape(ds, zs, kv_rows, 2, -1), (0, 2, 3, 1, 4)).reshape(deep, 2 * wide)
        at += kv_rows * (2 * wide // zs // pack)
        full_query = jnp.transpose(widen(everything, at, wq_rows, wide), (1, 0, 2, 3)).reshape(zs, -1, wide)
        at += wq_rows * (wide // pack)
        full_out = jnp.transpose(widen(everything, at, wq_rows, wide), (1, 0, 2, 3)).reshape(zs, -1, wide)
        pieces = [full_kv, full_query, full_out, full_up, full_down]
    read_all = d_gather([read_joined])
    state4, normed2, normed3, act3, *pieces = sum_over_head(part3, state3, (normed2, normed3, act3, *pieces))
    layer_all = d_gather([normed2, normed3, act3])

    (
        normed4, interface_new, dafter, dwrite_q, write_attended, after_normed, act5, dpre5, dkv4, dgain_mlp, part4,
        dwrite_normed,
    ) = write_stage(
        state4,
        write_gain_lat,
        int_hat,
        interface,
        interface_cot,
        jnp.stack([gain_write, gain_mlp]),
        own_segments[:, None],
        dd.astype(jnp.int32)[None],
        pieces,
        [
            (deep, 2 * wide),
            (zs, wide // zs, wide),
            (zs, wide // zs, wide),
            (zs, wide // zs, hidden),
            (ds, zs, down_rows, wide),
        ],
    )
    dsum4, after_normed, dpre5, act5, dwrite_q, write_attended, dafter, dkv4 = sum_over_head(
        part4, None, (after_normed, dpre5, act5, dwrite_q, write_attended, dafter, dkv4)
    )

    place = dd.astype(jnp.int32)[None]
    piece_rows = middle + 2 * wq_rows * (wide // pack)
    if direct:
        grads_mine, grads_other = interface_grads(
            after_normed, dpre5, act5, interface_cot, int_hat, gain_write[None], dwrite_q, write_attended, dafter,
            place, zs, piece_rows,
        )
        dsum4, grads_mine, grads_other = tie(dsum4, grads_mine, grads_other)
        grads_mine = grads_mine.reshape(4, -1, pack)
        grads_got = swap(grads_other.reshape(4, -1, pack), 1)
    else:
        write_normed = int_hat * gain_write
        dup = jnp.transpose(tmm(after_normed, dpre5).reshape(zs, wide // zs, ds, -1), (2, 0, 1, 3))

        def pack_grad(grad, rows):
            grad = grad.reshape(ds, zs, rows, wide)
            return [grad[..., at : at + pack] for at in range(0, wide, pack)]

        ddown = tmm(act5, interface_cot)
        dquery = jnp.transpose(tmm(write_normed, dwrite_q).reshape(zs, ds, wq_rows, wide), (1, 0, 2, 3))
        dout = jnp.transpose(tmm(write_attended, dafter).reshape(zs, ds, wq_rows, wide), (1, 0, 2, 3))
        packed_grads = jnp.concatenate(
            [dup] + pack_grad(ddown, down_rows) + pack_grad(dquery, wq_rows) + pack_grad(dout, wq_rows), axis=2
        )
        grads_mine = lax.psum_scatter(packed_grads, "dp", scatter_dimension=0, tiled=False)

    dint = dafter + norm_back(dwrite_normed, int_hat, int_root, gain_write)

    dkv_parts = jnp.transpose(dkv4.reshape(count, 2, zs, -1), (2, 0, 1, 3)).reshape(zs, count, -1)
    dsum4, dkv_parts = tie(dsum4, dkv_parts)
    dkv_mine = z_scatter(dkv_parts)
    dstate4, dgain4, dpre3, part5 = ffn_backward(
        latents_cot, dsum4, state4, write_gain_lat, pre3, layer_up, layer_down
    )
    if direct:
        part5, grads_mine, grads_got, dkv_mine = tie(part5, grads_mine, grads_got, dkv_mine)
        grads_mine = lax.psum_scatter(
            grads_mine + grads_got,
            "dp",
            scatter_dimension=0,
            axis_index_groups=[[2 * k + c for k in range(ds // 2)] for c in range(2)],
        )
    dsum3, normed4, dkv_mine, released4, dpre3 = sum_over_head(part5, None, (normed4, dkv_mine, dstate4, dpre3))
    write_all = d_gather([normed4, dkv_mine, released4, dpre3])
    dsum3, read_all = tie(dsum3, read_all)
    dstate3, dgain3, dpacked, part6 = run_whole(
        functools.partial(self_back_kernel, deep // HEADS),
        [shape_of(count, deep), shape_of(1, deep), shape_of(count, 3 * part), shape_of(count, deep)],
        (dstate4, dsum3, state3, layer_gain_mlp[None], packed, self_weights, qkv, layer_out),
        flops=8 * count * deep * part,
    )
    dsum2, dpacked = sum_over_head(part6, None, (dpacked,))
    dlayer_out = tmm(self_attended, dstate3)
    dsum2, layer_all = tie(dsum2, layer_all)

    dstate2, dgain2, dpre1, part7 = ffn_backward(
        dstate3, dsum2, state2, layer_gain_att, pre1, read_up, read_down
    )
    dsum1, released2, dpre1 = sum_over_head(part7, None, (dstate2, dpre1))
    both_all = d_gather([dpacked, released2, dpre1])
    dsum1, grads_mine = tie(dsum1, grads_mine)
    grads_mine = z_scatter(grads_mine.reshape(zs, -1, pack))
    dstate1, dgain1, dquery0, dread_kv, dlat_part, dint_part, dgain_lat, dgain_int, dkeyval, dread_out = run_whole(
        functools.partial(read_back_kernel, deep // HEADS),
        [
            shape_of(count, deep),
            shape_of(1, deep),
            shape_of(count, part),
            shape_of(zs * patches, 2 * part),
            shape_of(count, deep),
            shape_of(zs * patches, wide),
            shape_of(1, deep),
            shape_of(1, wide),
            shape_of(wide, 2 * part),
            shape_of(part, deep),
        ],
        (dstate2, dsum1, state1, read_gain_mlp[None], query, kv0, read_weights, read_query, keyval, read_out, latents, int_pack,
         gain_read[None], read_attended),
        flops=1e6,
        moved=1e6,
    )

    first = (me == 0).astype(jnp.float32)
    small = jnp.concatenate(
        [dgain_lat[0]]
        + [g[0] * first for g in (dgain1, dgain2, dgain3, dgain4)]
        + [dgain_int[0], jnp.sum(dwrite_normed * int_hat, axis=0), dgain_mlp[0]]
    )
    dlat_part, dstate1, grads_mine, small = tie(dlat_part, dstate1, grads_mine, small)
    lanes = small.size // count
    small = jnp.sum(z_gather(small.reshape(count, lanes)), axis=0)
    fill = jnp.pad(small, ((0, 0), (0, -lanes % 128)))
    late = [join([dquery0, fill])]

    half = z_scatter(dlat_part.reshape(zs, count // zs, deep))
    write_all = tie(write_all, dgain_int)[0]
    normed4_all, dkv_all, dstate4_all, dpre3_all = cut_up(write_all, [normed4, dkv_mine, dstate4, dpre3])
    normed2_all, normed3_all, act3_all = cut_up(layer_all, [normed2, normed3, act3])
    grad_layer_up = tmm(normed3_all, dpre3_all)
    if direct:
        late = to_sides(*late)
        dkeyval = [dkeyval] + [
            grad.reshape(ds, -1, deep)[:, :, at : at + 2 * part].reshape(-1, 2 * part)
            for grad in (dlayer_out, dread_out)
            for at in range(0, deep, 2 * part)
        ]
        dkeyval = jnp.concatenate([grad.reshape(ds, -1, 2 * part) for grad in dkeyval], axis=1)
        dkeyval = dkeyval.reshape(4, 2, -1, 2 * part)
        pair = [pick(dkeyval, core, 1), swap(pick(dkeyval, 1 - core, 1), 1)]
        half, dint_part, grad_layer_up, layer_all, write_all, *held = tie(
            half, dint_part, grad_layer_up, layer_all, write_all, *late, *pair
        )
        _, _, act3_all = cut_up(layer_all, [normed2, normed3, act3])
        normed4_all, dkv_all, dstate4_all, _ = cut_up(write_all, [normed4, dkv_mine, dstate4, dpre3])
        late, pair = to_across(*held[:3]), scatter_one(*held[3:])
    dint_own, *dint_got = z_pieces(dint_part.reshape(zs, patches, wide))
    near, middle_got, far = dint_got[0], dint_got[1:-1], dint_got[-1]
    dlat = z_gather(half).reshape(count, deep)
    grad_layer_down, grad_write_keyval = tmm(act3_all, dstate4_all), tmm(normed4_all, dkv_all)
    if direct:
        grad_layer_down, both_all, near, *held = tie(grad_layer_down, both_all, near, *late, *pair)
        late, dkeyval = to_core(*held[:5]), scatter_two(*held[5:])
    dpacked_all, dstate2_all, dpre1_all = cut_up(both_all, [dpacked, dstate2, dpre1])
    normed1_all, act1_all = cut_up(read_all, [normed1, act1])
    grad_layer_qkv, grad_read_up = tmm(normed2_all, dpacked_all), tmm(normed1_all, dpre1_all)
    if direct:
        dkeyval, grad_layer_qkv, both_all, far, *late = tie(dkeyval, grad_layer_qkv, both_all, far, *late)
        _, dstate2_all, _ = cut_up(both_all, [dpacked, dstate2, dpre1])
    grad_read_down = tmm(act1_all, dstate2_all)
    if direct:
        dlat, grad_write_keyval, grad_read_up, grad_read_down, *middle_got = tie(
            dlat, grad_write_keyval, grad_read_up, grad_read_down, *middle_got
        )
        flat = jnp.concatenate([grads_mine] + [dkeyval[:, at : at + pack] for at in range(0, 2 * part, pack)], axis=0)
        grads_all = lax.all_gather(flat, "dp", axis=0, tiled=False)
        grad_read_query, small = outer_products(
            late, place, [early_all], [(0, 0, deep, 0, part)], (part, fill.shape[1])
        )
        small = small[:, :lanes]
        sums = widen(grads_all[:, None], piece_rows, dkeyval.shape[0], 2 * part)[:, 0]
        at, few = read_keyval.shape[0] // ds, part // ds
        grad_read_keyval = sums[:, :at]
        found = []
        for _ in range(2):
            blocks = [sums[:, at + n * few : at + (n + 1) * few] for n in range(deep // (2 * part))]
            found.append(jnp.concatenate(blocks, axis=-1).reshape(part, deep))
            at += few * len(blocks)
        grad_layer_out, grad_read_out = found
    else:
        grads_all = lax.all_gather(grads_mine, "dp", axis=0, tiled=False)
        grad_read_keyval, grad_layer_out, grad_read_out = lax.psum((dkeyval, dlayer_out, dread_out), "dp")
        dquery0_all, small = cut_up(d_gather(late), [dquery0, fill])
        grad_read_query = tmm(early_all, dquery0_all)
        small = jnp.sum(small.reshape(ds, count, -1)[:, :, :lanes], axis=0)
    latents_grad = dstate1 + norm_back(dlat, lat_hat, lat_root, read_gain_lat)
    dint_normed = dint_own + near + far
    for piece in middle_got:
        dint_normed = dint_normed + piece
    interface_grad = dint + norm_back(dint_normed, int_hat, int_root, gain_read)
    small = small.reshape(-1)
    lat_gains = small[: 5 * deep].reshape(5, deep)
    int_gains = small[5 * deep :].reshape(3, zs, wide // zs)
    int_gains = lax.dynamic_index_in_dim(int_gains, me, 1, keepdims=False)

    full = grads_all[:, None]
    grad_write_up = grads_all[:, : wide // zs].reshape(ds, wide // zs, zs, up_cols // zs)
    grad_write_up = jnp.transpose(grad_write_up, (1, 2, 0, 3)).reshape(write_up.shape)
    at = wide // zs
    grad_write_down = widen(full, at, down_rows, wide).reshape(write_down.shape)
    at += down_rows * (wide // pack)
    grad_write_query = widen(full, at, wq_rows, wide).reshape(write_query.shape)
    at += wq_rows * (wide // pack)
    grad_write_out = widen(full, at, wq_rows, wide).reshape(write_out.shape)

    return (
        interface_new[None],
        state4[None],
        interface_grad[None],
        latents_grad[None],
        lat_gains[0],
        int_gains[0],
        grad_read_query,
        grad_read_keyval.reshape(read_keyval.shape),
        grad_read_out,
        lat_gains[1],
        grad_read_up,
        grad_read_down,
        lat_gains[2][None],
        grad_layer_qkv.reshape(layer_qkv.shape),
        grad_layer_out[None],
        lat_gains[3][None],
        grad_layer_up[None],
        grad_layer_down[None],
        int_gains[1],
        grad_write_query,
        lat_gains[4],
        grad_write_keyval.reshape(write_keyval.shape),
        grad_write_out,
        int_gains[2],
        grad_write_up,
        grad_write_down,
    )


def solution(mesh):
    rows, both = P("dp", "head", None), P("dp", None, None)
    weights = (
        P(),
        P("head"),
        P(None, "head"),
        P(None, None, "head"),
        P("head", None),
        P(),
        P(None, "head"),
        P("head", None),
        P(),
        P(None, None, None, "head"),
        P(None, "head", None),
        P(),
        P(None, None, "head"),
        P(None, "head", None),
        P("head"),
        P("head", None),
        P(),
        P(None, None, "head"),
        P("head", None),
        P("head"),
        P("head", None),
        P("head", None),
    )
    in_specs = (rows, both, P("dp", None)) + weights + (rows, both)
    out_specs = (rows, both, rows, both) + weights
    return jax.shard_map(local, mesh=mesh, in_specs=in_specs, out_specs=out_specs, check_vma=False)
```
